256 devices in a mesh: ens: 32 (over x, y, core), bal: 8 (over z).
Axes of the slice: x: 4, y: 4, z: 8, core: 2. Of those that a mesh axis runs over, the one named last changes fastest.
Arguments:
- members: float32 [256, 1024, 4, 128], P('ens', 'bal'), may hold values from -6 to 6
- obs_ens: bfloat16 [256, 1024, 2048], P('ens', 'bal'), may hold values from -16 to 16
- obs_count: int32 [1024], replicated, may hold values from 0 to 2048, as said below
- obs_value: float32 [1024, 2048], P(('bal', 'ens')), may hold values from -6 to 6
- obs_weight: float32 [1024, 2048], P(('bal', 'ens')), may hold values from 0.02 to 0.5
Outputs:
- analysis: float32 [256, 1024, 4, 128], P('ens', 'bal')
The draws below stay inside these ranges and needn't reach their ends.
Inputs may be any that keep to these rules, and one draw needn't show every extreme that they name: `obs_count`: some tile has all 2048 slots live and some tile has none.
All inputs are finite; a program needn't handle non-finite values.
Results may differ from the reference program's by a relative error of at most 0.0031.
Values may be sent and summed in bfloat16 or wider, within the bound.
A program may use at most 64 MiB of HBM per device.

```python
import math
import jax
import jax.numpy as jnp
from jax import lax

K = 256
NF = 4
TC = 128
OBS_MAX = 2048
NEWTON = 5
TILES = 1024


level_bins = 32


mass_scale = 0.02


def slot_levels(key):
    bin_key = jax.random.fold_in(key, 501)
    jitter_key = jax.random.fold_in(key, 502)
    bins = jax.random.randint(bin_key, (TILES, OBS_MAX), 0, level_bins)
    jitter = jax.random.uniform(jitter_key, (TILES, OBS_MAX), jnp.float32)
    level = (bins.astype(jnp.float32) + jitter) / level_bins
    weight = 0.02 * jnp.power(jnp.float32(25.0), level)
    return (bins, level, weight)


def draw_obs_count(key, part):
    key = jax.random.fold_in(key, 17)
    live_key, amount_key = jax.random.split(key)
    live_draw = jax.random.randint(live_key, (TILES,), 0, 2)
    amount = jax.random.randint(amount_key, (TILES,), 1, OBS_MAX + 1)
    position = jnp.arange(TILES)
    counts = jnp.where(position == 0, OBS_MAX, live_draw * amount)
    counts = jnp.where(position == TILES - 1, 0, counts)
    return counts.astype(jnp.int32)


def draw_obs_weight(key, part):
    bins, level, weight = slot_levels(key)
    return weight.astype(jnp.float32)


def draw_obs_ens(key, part):
    bins, level, weight = slot_levels(key)
    key = jax.random.fold_in(key, 29)
    noise_key, factor_key, spread_key = jax.random.split(key, 3)
    spread = jnp.exp(jax.random.uniform(spread_key, (TILES, OBS_MAX), jnp.float32, -math.log(3.0), math.log(3.0)))
    loading = spread * jnp.sqrt(mass_scale * jnp.power(jnp.float32(10.0), 1.0 - level) / weight)
    tile_index = jnp.arange(TILES)[:, None]
    noise = jax.random.truncated_normal(noise_key, -4.0, 4.0, (K, TILES, OBS_MAX), jnp.float32)
    factors = jax.random.truncated_normal(factor_key, -4.0, 4.0, (K, TILES, level_bins), jnp.float32)
    values = noise + loading[None] * factors[:, tile_index, bins]
    return jnp.clip(values, -16.0, 16.0).astype(jnp.bfloat16)


def level_of(rng, shape, shards, low, top_value):
    gain = 1.0
    for axis_at, shards_of in shards:
        draws = jax.random.uniform(jax.random.fold_in(jax.random.fold_in(rng, 6), axis_at), (shards_of,), jnp.float32, low / len(shards), top_value / len(shards))
        gain = gain * jnp.repeat(jnp.exp(draws), shape[axis_at] // shards_of).reshape((-1,) + (1,) * (len(shape) - 1 - axis_at))
    return gain


def bell_draw(stream_key, dims, deviation, reach, shards=(), kind=jnp.bfloat16):
    loudness = level_of(stream_key, dims, shards, -0.22, 0.18) if shards else 1.0
    entries = jax.random.normal(stream_key, dims, jnp.float32) * deviation * loudness
    return jnp.minimum(jnp.maximum(entries, -reach), reach).astype(kind)


def setup_inputs(seed: int = 0) -> dict:
    splits = jax.random.split(jax.random.key(seed), 6)
    return {
        "members": bell_draw(splits[0], (K, TILES, NF, TC), 1.0, 6.0, ((0, 32), (1, 8)), jnp.float32),
        "obs_ens": draw_obs_ens(jax.random.fold_in(splits[5], 71), 0),
        "obs_count": draw_obs_count(jax.random.fold_in(splits[5], 71), 0),
        "obs_value": bell_draw(splits[3], (TILES, OBS_MAX), 1.0, 6.0, ((0, 256),), jnp.float32),
        "obs_weight": draw_obs_weight(jax.random.fold_in(splits[5], 71), 0),
    }


def analyse(members_t, obs_t, live_count, value_row, weight_row):
    highest = lax.Precision.HIGHEST
    mean_t = lax.optimization_barrier(jnp.mean(members_t, axis=0))
    pert_t = (members_t - mean_t[None, :]).astype(jnp.bfloat16)
    observed = obs_t.astype(jnp.float32)
    obs_mean = lax.optimization_barrier(jnp.mean(observed, axis=0))
    live_mask = lax.iota(jnp.int32, OBS_MAX) < live_count
    innovation = jnp.where(live_mask, value_row - obs_mean, jnp.float32(0.0))
    root_weight = jnp.sqrt(weight_row)
    masked_weight = jnp.where(live_mask, root_weight, jnp.float32(0.0))
    root_matrix = (masked_weight[None, :] * (observed - obs_mean[None, :])).astype(jnp.bfloat16)
    scaled_innov = (root_weight * innovation).astype(jnp.bfloat16)
    gram_matrix = jnp.dot(root_matrix, root_matrix.T, preferred_element_type=jnp.float32)
    obs_vector = jnp.dot(root_matrix, scaled_innov, preferred_element_type=jnp.float32)
    identity = jnp.eye(K, dtype=jnp.float32)
    scale_bound = K - 1.0 + jnp.trace(gram_matrix)
    y_matrix = ((K - 1.0) * identity + gram_matrix) / scale_bound
    z_matrix = identity
    for iteration in range(NEWTON):
        middle = 1.5 * identity - 0.5 * jnp.dot(z_matrix, y_matrix, precision=highest)
        y_matrix = jnp.dot(y_matrix, middle, precision=highest)
        z_matrix = jnp.dot(middle, z_matrix, precision=highest)
    inner_vec = jnp.dot(z_matrix, obs_vector, precision=highest)
    shift_vec = jnp.dot(z_matrix, inner_vec, precision=highest) / scale_bound
    weights = (jnp.sqrt(K - 1.0) / jnp.sqrt(scale_bound) * z_matrix + shift_vec[:, None]).astype(jnp.bfloat16)
    return mean_t[None, :] + jnp.dot(weights.T, pert_t, preferred_element_type=jnp.float32)

def reference(members, obs_ens, obs_count, obs_value, obs_weight):

    def one_tile(tile_index):
        members_t = lax.dynamic_index_in_dim(members, tile_index, 1, keepdims=False).reshape(K, NF * TC)
        obs_t = lax.dynamic_index_in_dim(obs_ens, tile_index, 1, keepdims=False)
        return analyse(members_t, obs_t, obs_count[tile_index], obs_value[tile_index], obs_weight[tile_index])
    result = lax.map(one_tile, jnp.arange(TILES, dtype=jnp.int32))
    return result.transpose(1, 0, 2).reshape(K, TILES, NF, TC)
```

```python
import functools

import jax
import jax.numpy as jnp
from jax import lax
from jax.experimental import pallas as pl
from jax.experimental.pallas import tpu as pltpu
from jax.sharding import PartitionSpec as P

NEWTON = 5
MESH = pl.DeviceIdType.MESH
WAYS = 32
GROUP = 128
LANES = 128
SLOT_BLOCKS = 16
HELD = 3
CAPACITY = 24
ROWS = 8
ENS = 256
CODE = 32767.0 / 6.0


def solve_weights(gram_matrix, obs_vector):
    highest = lax.Precision.HIGHEST
    ens_size = gram_matrix.shape[0]
    identity = jnp.eye(ens_size, dtype=jnp.float32)
    scale_bound = ens_size - 1.0 + jnp.trace(gram_matrix)
    y_matrix = ((ens_size - 1.0) * identity + gram_matrix) / scale_bound
    z_matrix = identity
    for iteration in range(NEWTON):
        middle = 1.5 * identity - 0.5 * jnp.dot(z_matrix, y_matrix, precision=highest)
        y_matrix = jnp.dot(y_matrix, middle, precision=highest)
        z_matrix = jnp.dot(middle, z_matrix, precision=highest)
    inner_vec = jnp.dot(z_matrix, obs_vector, precision=highest)
    shift_vec = jnp.dot(z_matrix, inner_vec, precision=highest) / scale_bound
    factor = jnp.sqrt(ens_size - 1.0) / jnp.sqrt(scale_bound)
    return (factor * z_matrix + shift_vec[:, None]).astype(jnp.bfloat16)


def unit_weights(gram_matrix, obs_vector):
    return jnp.eye(gram_matrix.shape[0], dtype=jnp.bfloat16)


def tile_weights(operands):
    gram_matrix, obs_vector = operands
    return lax.cond(
        jnp.trace(gram_matrix) > 0.0, solve_weights, unit_weights, gram_matrix, obs_vector
    )


def tile_gram(obs_rows, centre_row, weight_row, innov_row, live_count, ens_size):
    zero_sums = (jnp.zeros((ens_size, ens_size), jnp.float32), jnp.zeros((ens_size,), jnp.float32))
    block_count = (live_count + 127) // 128

    def add_block(index_block, totals):
        first_slot = index_block * 128
        obs_piece = lax.dynamic_slice_in_dim(obs_rows, first_slot, 128, 1)
        centre_piece = lax.dynamic_slice_in_dim(centre_row, first_slot, 128, 0)
        weight_piece = lax.dynamic_slice_in_dim(weight_row, first_slot, 128, 0)
        rhs_piece = lax.dynamic_slice_in_dim(innov_row, first_slot, 128, 0)
        root_piece = (
            weight_piece[None, :] * (obs_piece.astype(jnp.float32) - centre_piece[None, :])
        ).astype(jnp.bfloat16)
        gram_piece = lax.dot_general(
            root_piece, root_piece, (((1,), (1,)), ((), ())), preferred_element_type=jnp.float32
        )
        vector_piece = jnp.dot(root_piece, rhs_piece, preferred_element_type=jnp.float32)
        return (totals[0] + gram_piece, totals[1] + vector_piece)

    return lax.fori_loop(0, block_count, add_block, zero_sums)


def static_body(members, obs_ens, obs_count, obs_value, obs_weight):
    member_block, tile_block, nfield, columns = members.shape
    ens_ways = lax.axis_size("ens")
    ens_size = member_block * ens_ways
    per_device, slot_count = obs_value.shape
    state_width = nfield * columns
    first_tile = (lax.axis_index("bal") * ens_ways + lax.axis_index("ens")) * per_device
    ensemble = lax.all_to_all(members, "ens", split_axis=1, concat_axis=0, tiled=True)
    observed = lax.all_to_all(obs_ens, "ens", split_axis=1, concat_axis=0, tiled=True)
    mean_tiles = jnp.mean(ensemble, axis=0)
    pert_tiles = (ensemble - mean_tiles[None]).astype(jnp.bfloat16)
    pert_tiles = pert_tiles.reshape(ens_size, per_device, state_width)
    mean_tiles = mean_tiles.reshape(per_device, state_width)
    obs_mean = jnp.sum(observed, axis=0, dtype=jnp.float32) / ens_size
    counts = lax.dynamic_slice_in_dim(obs_count, first_tile, per_device, 0)
    positions = lax.broadcasted_iota(jnp.int32, (per_device, slot_count), 1)
    live_mask = positions < counts[:, None]
    innovation = jnp.where(live_mask, obs_value - obs_mean, 0.0)
    root_weight = jnp.sqrt(obs_weight)
    masked_weight = jnp.where(live_mask, root_weight, 0.0)
    scaled_innov = (root_weight * innovation).astype(jnp.bfloat16)
    grams = []
    vectors = []
    for tile_index in range(per_device):
        gram_one, vector_one = tile_gram(
            observed[:, tile_index],
            obs_mean[tile_index],
            masked_weight[tile_index],
            scaled_innov[tile_index],
            counts[tile_index],
            ens_size,
        )
        grams.append(gram_one)
        vectors.append(vector_one)
    gram_tiles = jnp.stack(grams)
    vector_tiles = jnp.stack(vectors)
    weights = lax.map(tile_weights, (gram_tiles, vector_tiles))
    result = mean_tiles[None] + jnp.einsum(
        "tjk,jtf->ktf", weights, pert_tiles, preferred_element_type=jnp.float32
    )
    result = result.reshape(ens_size, per_device, nfield, columns)
    return lax.all_to_all(result, "ens", split_axis=0, concat_axis=1, tiled=True)


def ranks_of(sizes):
    width = sizes.shape[-1]
    here, there = sizes[..., :, None], sizes[..., None, :]
    at = lax.broadcasted_iota(jnp.int32, (width, width), 0)
    other = lax.broadcasted_iota(jnp.int32, (width, width), 1)
    ahead = (there > here) | ((there == here) & (other < at))
    return jnp.sum(ahead.astype(jnp.int32), axis=-1)


def by_rank(ranks, values):
    width = ranks.shape[-1]
    place = lax.broadcasted_iota(jnp.int32, (width, width), 0)
    hit = ranks[..., None, :] == place
    return jnp.sum(jnp.where(hit, values[..., None, :], 0), axis=-1)


def make_plan(obs_count):
    counts = obs_count.reshape(-1, GROUP)
    blocks = (counts + LANES - 1) // LANES
    ranks = ranks_of(blocks)
    ordered = by_rank(ranks, blocks)
    tile_ids = jnp.broadcast_to(lax.iota(jnp.int32, GROUP), counts.shape)
    ordered_tile = by_rank(ranks, tile_ids)
    ordered_count = by_rank(ranks, counts)
    first, second = ordered[:, :WAYS], ordered[:, 2 * WAYS - 1 : WAYS - 1 : -1]
    pair_rank = ranks_of(first + second)
    reverse = slice(3 * WAYS - 1, 2 * WAYS - 1, -1)
    hit = pair_rank[..., :, None] == lax.iota(jnp.int32, WAYS)[None, None, :]

    def third_of(array):
        return jnp.sum(jnp.where(hit, array[:, None, reverse], 0), axis=-1)

    third = third_of(ordered)
    load = first + second + third
    fits = (jnp.max(load) <= CAPACITY) & (jnp.max(ordered[:, HELD * WAYS]) == 0)
    mine = lax.axis_index("bal")

    def pick(array):
        return lax.dynamic_index_in_dim(array, mine, 0, keepdims=False)

    def three(array):
        return jnp.stack(
            [array[:, :WAYS], array[:, 2 * WAYS - 1 : WAYS - 1 : -1], third_of(array)], axis=-1
        )

    tiles = pick(three(ordered_tile))
    tile_counts = pick(three(ordered_count))
    tile_blocks = pick(jnp.stack([first, second, third], axis=-1))
    place = lax.broadcasted_iota(jnp.int32, (WAYS, CAPACITY), 1)
    one, two = tile_blocks[:, 0:1], tile_blocks[:, 0:1] + tile_blocks[:, 1:2]
    end = two + tile_blocks[:, 2:3]
    which = (place >= one).astype(jnp.int32) + (place >= two).astype(jnp.int32)

    def chosen(array):
        return jnp.where(which == 0, array[:, 0:1], jnp.where(which == 1, array[:, 1:2], array[:, 2:3]))

    live = place < end
    at_block = place - jnp.where(which == 0, 0, jnp.where(which == 1, one, two))
    at_block = jnp.where(live, at_block, 0)
    at_tile = chosen(tiles)
    at_count = jnp.where(live, chosen(tile_counts) - at_block * LANES, 0)
    source = at_block * GROUP + at_tile
    weight_row = at_tile * SLOT_BLOCKS + at_block
    return fits, tiles, tile_blocks, source, weight_row, at_count, which


def pack_kernel(source, tiles, obs_hbm, members, obs_out, mem_out, obs_in, wide, sems):
    pairs = CAPACITY // 2
    copies = [
        pltpu.make_async_copy(obs_hbm.at[m], obs_in.at[m], sems.at[m]) for m in range(ROWS)
    ]
    for copy in copies:
        copy.start()

    def pack_members(dest, carry):
        for slot in range(HELD):
            row = tiles[dest * HELD + slot] * 4
            parts = [members[pl.ds(row + f, ROWS, stride=4 * GROUP), :] for f in range(4)]
            coded = jnp.round(jnp.concatenate(parts, axis=0) * CODE)
            mem_out[dest, slot] = coded.astype(jnp.int32).astype(jnp.int16)
        return carry

    lax.fori_loop(0, WAYS, pack_members, 0)

    for m in range(ROWS):
        copies[m].wait()

        def widen(block, carry):
            first = pl.multiple_of((m * SLOT_BLOCKS + block) * GROUP, GROUP)
            lanes = pl.ds(pl.multiple_of(block * LANES, LANES), LANES)
            wide[pl.ds(first, GROUP), :] = obs_in[m, :, lanes].astype(jnp.float32)
            return carry

        lax.fori_loop(0, SLOT_BLOCKS, widen, 0)

    stride = SLOT_BLOCKS * GROUP

    def pack_obs(dest, carry):
        for pair in range(pairs):
            at = dest * CAPACITY + 2 * pair
            top = wide[pl.ds(source[at], ROWS, stride=stride), :]
            low = wide[pl.ds(source[at + 1], ROWS, stride=stride), :]
            obs_out[dest, pair] = jnp.concatenate([top, low], axis=0).astype(jnp.bfloat16)
        return carry

    lax.fori_loop(0, WAYS, pack_obs, 0)


def pack(source, tiles, obs_ens, members):
    smem = pl.BlockSpec(memory_space=pltpu.SMEM)
    vmem = pl.BlockSpec(memory_space=pltpu.VMEM)
    return pl.pallas_call(
        pack_kernel,
        out_shape=(
            jax.ShapeDtypeStruct((WAYS, CAPACITY // 2, 16, LANES), jnp.bfloat16),
            jax.ShapeDtypeStruct((WAYS, HELD, 32, LANES), jnp.int16),
        ),
        in_specs=[smem, smem, pl.BlockSpec(memory_space=pl.ANY), vmem],
        out_specs=(vmem, vmem),
        scratch_shapes=[
            pltpu.VMEM((ROWS, GROUP, SLOT_BLOCKS * LANES), jnp.bfloat16),
            pltpu.VMEM((ROWS * SLOT_BLOCKS * GROUP, LANES), jnp.float32),
            pltpu.SemaphoreType.DMA((ROWS,)),
        ],
        compiler_params=pltpu.CompilerParams(vmem_limit_bytes=40 << 20),
        name="pack",
    )(source.reshape(-1), tiles.reshape(-1), obs_ens, members)


def displacements():
    every = [(dx, dy, dc) for dx in range(4) for dy in range(4) for dc in range(2)][1:]
    return sorted(every, key=lambda d: -(min(d[0], 4 - d[0]) + min(d[1], 4 - d[1])))


def shifted(me, step):
    x, y, core = me // 8, (me // 2) % 4, me % 2
    return (((x + step[0]) % 4) * 4 + (y + step[1]) % 4) * 2 + (core + step[2]) % 2


def split(c, matrix, eye):
    mean = jnp.sum(matrix * eye) * (1.0 / ENS)
    deviation = matrix - mean * eye
    return c + mean, deviation, deviation.astype(jnp.bfloat16)


def times(left, right, eye):
    cross = left[0] * right[1] + right[0] * left[1]
    inner = jnp.dot(left[2], right[2], preferred_element_type=jnp.float32)
    return split(left[0] * right[0], cross + inner, eye)


def middle_of(product):
    return 1.5 - 0.5 * product[0], -0.5 * product[1], product[2] * jnp.bfloat16(-0.5)


def row_times(row, z):
    high = row.astype(jnp.bfloat16)
    low = (row - high.astype(jnp.float32)).astype(jnp.bfloat16)
    rest = (z[1] - z[2].astype(jnp.float32)).astype(jnp.bfloat16)
    out = jnp.dot(high, z[2], preferred_element_type=jnp.float32)
    out = out + jnp.dot(low, z[2], preferred_element_type=jnp.float32)
    out = out + jnp.dot(high, rest, preferred_element_type=jnp.float32)
    return z[0] * row + out


def analyse_kernel(
    weight_row, at_count, which,
    obs_send, mem_send, weights, values,
    out_recv,
    obs_recv, mem_recv, out_send, root, sel,
    obs_ssem, obs_rsem, mem_ssem, mem_rsem, out_ssem, out_rsem, own_sem,
):
    me = lax.axis_index("ens")
    steps = displacements()
    targets = [shifted(me, step) for step in steps]
    barrier = pltpu.get_barrier_semaphore()
    for target in targets:
        pl.semaphore_signal(barrier, inc=1, device_id={"ens": target}, device_id_type=MESH)
    pl.semaphore_wait(barrier, WAYS - 1)

    def exchange(src, dst, ssem, rsem, own):
        copies = [
            pltpu.make_async_remote_copy(
                src_ref=src.at[target],
                dst_ref=dst.at[me],
                send_sem=ssem.at[i],
                recv_sem=rsem.at[i],
                device_id={"ens": target},
                device_id_type=MESH,
            )
            for i, target in enumerate(targets)
        ]
        for copy in copies:
            copy.start()
        copies.append(pltpu.make_async_copy(src.at[me], dst.at[me], own))
        copies[-1].start()
        return copies

    obs_copies = exchange(obs_send, obs_recv, obs_ssem, obs_rsem, own_sem.at[0])
    mem_copies = exchange(mem_send, mem_recv, mem_ssem, mem_rsem, own_sem.at[1])
    for copy in obs_copies:
        copy.wait()

    lane = lax.broadcasted_iota(jnp.int32, (1, LANES), 1)
    for block in range(CAPACITY):
        half = (block % 2) * ROWS
        columns = pl.ds(block * LANES, LANES)
        seen = obs_recv[:, block // 2].astype(jnp.float32)[:, half : half + ROWS, :]
        seen = seen.reshape(ENS, LANES)
        mean = jnp.sum(seen, axis=0, keepdims=True) * (1.0 / ENS)
        at = me * CAPACITY + block
        live = lane < at_count[at]
        scale = jnp.where(live, jnp.sqrt(weights[pl.ds(weight_row[at], 1), :]), 0.0)
        innov = scale * (values[pl.ds(weight_row[at], 1), :] - mean)
        root[0:ENS, columns] = (scale * (seen - mean)).astype(jnp.bfloat16)
        root[ENS : ENS + 16, columns] = jnp.broadcast_to(innov, (16, LANES)).astype(jnp.bfloat16)
        for slot in range(HELD):
            mine = (which[at] == slot).astype(jnp.float32)
            sel[slot, :, columns] = jnp.full((16, LANES), mine, jnp.float32).astype(jnp.bfloat16)

    rows = lax.broadcasted_iota(jnp.int32, (ENS, ENS), 0)
    cols = lax.broadcasted_iota(jnp.int32, (ENS, ENS), 1)
    eye = (rows == cols).astype(jnp.float32)
    weight_t = []
    for slot in range(HELD):
        part = root[0:ENS, :] * sel[slot, 0:1, :]
        sums = lax.dot_general(
            root[...], part, (((1,), (1,)), ((), ())), preferred_element_type=jnp.float32
        )
        gram, vec = sums[0:ENS], sums[ENS : ENS + 8]
        bound = (ENS - 1.0) + jnp.sum(gram * eye)
        y = split((ENS - 1.0) / bound, gram * (1.0 / bound), eye)
        middle = middle_of(y)
        z = middle
        y = times(y, middle, eye)
        for iteration in range(1, NEWTON):
            middle = middle_of(times(z, y, eye))
            if iteration < NEWTON - 1:
                y = times(y, middle, eye)
            z = times(middle, z, eye)
        shift = row_times(row_times(vec, z), z)[0:1] * (1.0 / bound)
        factor = jnp.sqrt(jnp.float32(ENS - 1.0)) / jnp.sqrt(bound)
        weight_t.append((factor * z[1] + (factor * z[0]) * eye + shift).astype(jnp.bfloat16))

    for copy in mem_copies:
        copy.wait()
    out_copies = []
    for slot in range(HELD):
        coded = mem_recv[:, slot].astype(jnp.int32).astype(jnp.float32)
        fields = [coded[:, f * ROWS : (f + 1) * ROWS, :].reshape(ENS, LANES) for f in range(4)]
        state = jnp.concatenate(fields, axis=1) * (1.0 / CODE)
        mean = jnp.sum(state, axis=0, keepdims=True) * (1.0 / ENS)
        pert = (state - mean).astype(jnp.bfloat16)
        result = mean + jnp.dot(weight_t[slot], pert, preferred_element_type=jnp.float32)
        parts = [
            result[:, f * LANES : (f + 1) * LANES].reshape(WAYS, ROWS, LANES) for f in range(4)
        ]
        out_send[slot] = jnp.concatenate(parts, axis=1).astype(jnp.bfloat16)
        for i, target in enumerate(targets):
            copy = pltpu.make_async_remote_copy(
                src_ref=out_send.at[slot, target],
                dst_ref=out_recv.at[slot, me],
                send_sem=out_ssem.at[slot, i],
                recv_sem=out_rsem.at[slot, i],
                device_id={"ens": target},
                device_id_type=MESH,
            )
            copy.start()
            out_copies.append(copy)
        copy = pltpu.make_async_copy(
            out_send.at[slot, me], out_recv.at[slot, me], own_sem.at[2 + slot]
        )
        copy.start()
        out_copies.append(copy)
    for copy in out_copies:
        copy.wait()


def exchange_and_analyse(weight_row, at_count, which, obs_send, mem_send, weights, values):
    smem = pl.BlockSpec(memory_space=pltpu.SMEM)
    vmem = pl.BlockSpec(memory_space=pltpu.VMEM)
    anywhere = pl.BlockSpec(memory_space=pl.ANY)
    others = WAYS - 1
    return pl.pallas_call(
        analyse_kernel,
        out_shape=jax.ShapeDtypeStruct((HELD, WAYS, 32, LANES), jnp.bfloat16),
        in_specs=[smem, smem, smem, anywhere, anywhere, vmem, vmem],
        out_specs=anywhere,
        scratch_shapes=[
            pltpu.VMEM((WAYS, CAPACITY // 2, 16, LANES), jnp.bfloat16),
            pltpu.VMEM((WAYS, HELD, 32, LANES), jnp.int16),
            pltpu.VMEM((HELD, WAYS, 32, LANES), jnp.bfloat16),
            pltpu.VMEM((ENS + 16, CAPACITY * LANES), jnp.bfloat16),
            pltpu.VMEM((HELD, 16, CAPACITY * LANES), jnp.bfloat16),
            pltpu.SemaphoreType.DMA((others,)),
            pltpu.SemaphoreType.DMA((others,)),
            pltpu.SemaphoreType.DMA((others,)),
            pltpu.SemaphoreType.DMA((others,)),
            pltpu.SemaphoreType.DMA((HELD, others)),
            pltpu.SemaphoreType.DMA((HELD, others)),
            pltpu.SemaphoreType.DMA((2 + HELD,)),
        ],
        compiler_params=pltpu.CompilerParams(
            collective_id=0, has_side_effects=True, vmem_limit_bytes=48 << 20
        ),
        name="analyse",
    )(
        weight_row.reshape(-1), at_count.reshape(-1), which.reshape(-1),
        obs_send, mem_send, weights, values,
    )


def scatter_kernel(tiles, tile_blocks, members, recv, out):
    out[...] = members[...]

    def place(dest, carry):
        for slot in range(HELD):
            row = tiles[dest * HELD + slot] * 4

            @pl.when(tile_blocks[dest * HELD + slot] > 0)
            def _():
                wide = recv[slot, dest].astype(jnp.float32)
                for f in range(4):
                    out[pl.ds(row + f, ROWS, stride=4 * GROUP), :] = wide[f * ROWS : (f + 1) * ROWS]

        return carry

    lax.fori_loop(0, WAYS, place, 0)


def scatter(tiles, tile_blocks, members, recv):
    smem = pl.BlockSpec(memory_space=pltpu.SMEM)
    vmem = pl.BlockSpec(memory_space=pltpu.VMEM)
    return pl.pallas_call(
        scatter_kernel,
        out_shape=jax.ShapeDtypeStruct(members.shape, jnp.float32),
        in_specs=[smem, smem, vmem, vmem],
        out_specs=vmem,
        compiler_params=pltpu.CompilerParams(vmem_limit_bytes=40 << 20),
        name="scatter",
    )(tiles.reshape(-1), tile_blocks.reshape(-1), members, recv)


def body(members, obs_ens, obs_count, obs_value, obs_weight):
    fits, tiles, tile_blocks, source, weight_row, at_count, which = make_plan(obs_count)

    def compact(members, obs_ens, obs_count, obs_value, obs_weight):
        flat = members.reshape(-1, LANES)
        weights = lax.all_gather(obs_weight, "ens", axis=0, tiled=True).reshape(-1, LANES)
        values = lax.all_gather(obs_value, "ens", axis=0, tiled=True).reshape(-1, LANES)
        obs_send, mem_send = pack(source, tiles, obs_ens, flat)
        recv = exchange_and_analyse(
            weight_row, at_count, which, obs_send, mem_send, weights, values
        )
        return scatter(tiles, tile_blocks, flat, recv).reshape(members.shape)

    return lax.cond(
        fits, compact, static_body, members, obs_ens, obs_count, obs_value, obs_weight
    )


def solution(mesh):
    in_specs = (
        P("ens", "bal", None, None),
        P("ens", "bal", None),
        P(),
        P(("bal", "ens"), None),
        P(("bal", "ens"), None),
    )
    out_specs = P("ens", "bal", None, None)
    return jax.shard_map(body, mesh=mesh, in_specs=in_specs, out_specs=out_specs, check_vma=False)
```

```python
import functools

import jax
import jax.numpy as jnp
from jax import lax
from jax.experimental import pallas as pl
from jax.experimental.pallas import tpu as pltpu
from jax.sharding import PartitionSpec as P

NEWTON = 5
MESH = pl.DeviceIdType.MESH
WAYS = 32
GROUP = 128
LANES = 128
SLOT_BLOCKS = 16
HELD = 3
CAPACITY = 24
THIRD = 4
ROWS = 8
ENS = 256
CODE = 32767.0 / 6.0
ROOT_CODE = 32767.0 / 0.708
TILE_ROWS = 4 * SLOT_BLOCKS
AT_TILE, AT_BLOCKS, AT_COUNT = 32, 36, 64


def solve_weights(gram_matrix, obs_vector):
    highest = lax.Precision.HIGHEST
    ens_size = gram_matrix.shape[0]
    identity = jnp.eye(ens_size, dtype=jnp.float32)
    scale_bound = ens_size - 1.0 + jnp.trace(gram_matrix)
    y_matrix = ((ens_size - 1.0) * identity + gram_matrix) / scale_bound
    z_matrix = identity
    for iteration in range(NEWTON):
        middle = 1.5 * identity - 0.5 * jnp.dot(z_matrix, y_matrix, precision=highest)
        y_matrix = jnp.dot(y_matrix, middle, precision=highest)
        z_matrix = jnp.dot(middle, z_matrix, precision=highest)
    inner_vec = jnp.dot(z_matrix, obs_vector, precision=highest)
    shift_vec = jnp.dot(z_matrix, inner_vec, precision=highest) / scale_bound
    factor = jnp.sqrt(ens_size - 1.0) / jnp.sqrt(scale_bound)
    return (factor * z_matrix + shift_vec[:, None]).astype(jnp.bfloat16)


def unit_weights(gram_matrix, obs_vector):
    return jnp.eye(gram_matrix.shape[0], dtype=jnp.bfloat16)


def tile_weights(operands):
    gram_matrix, obs_vector = operands
    return lax.cond(
        jnp.trace(gram_matrix) > 0.0, solve_weights, unit_weights, gram_matrix, obs_vector
    )


def tile_gram(obs_rows, centre_row, weight_row, innov_row, live_count, ens_size):
    zero_sums = (jnp.zeros((ens_size, ens_size), jnp.float32), jnp.zeros((ens_size,), jnp.float32))
    block_count = (live_count + 127) // 128

    def add_block(index_block, totals):
        first_slot = index_block * 128
        obs_piece = lax.dynamic_slice_in_dim(obs_rows, first_slot, 128, 1)
        centre_piece = lax.dynamic_slice_in_dim(centre_row, first_slot, 128, 0)
        weight_piece = lax.dynamic_slice_in_dim(weight_row, first_slot, 128, 0)
        rhs_piece = lax.dynamic_slice_in_dim(innov_row, first_slot, 128, 0)
        root_piece = (
            weight_piece[None, :] * (obs_piece.astype(jnp.float32) - centre_piece[None, :])
        ).astype(jnp.bfloat16)
        gram_piece = lax.dot_general(
            root_piece, root_piece, (((1,), (1,)), ((), ())), preferred_element_type=jnp.float32
        )
        vector_piece = jnp.dot(root_piece, rhs_piece, preferred_element_type=jnp.float32)
        return (totals[0] + gram_piece, totals[1] + vector_piece)

    return lax.fori_loop(0, block_count, add_block, zero_sums)


def static_body(members, obs_ens, obs_count, obs_value, obs_weight):
    member_block, tile_block, nfield, columns = members.shape
    ens_ways = lax.axis_size("ens")
    ens_size = member_block * ens_ways
    per_device, slot_count = obs_value.shape
    state_width = nfield * columns
    first_tile = (lax.axis_index("bal") * ens_ways + lax.axis_index("ens")) * per_device
    ensemble = lax.all_to_all(members, "ens", split_axis=1, concat_axis=0, tiled=True)
    observed = lax.all_to_all(obs_ens, "ens", split_axis=1, concat_axis=0, tiled=True)
    mean_tiles = jnp.mean(ensemble, axis=0)
    pert_tiles = (ensemble - mean_tiles[None]).astype(jnp.bfloat16)
    pert_tiles = pert_tiles.reshape(ens_size, per_device, state_width)
    mean_tiles = mean_tiles.reshape(per_device, state_width)
    obs_mean = jnp.sum(observed, axis=0, dtype=jnp.float32) / ens_size
    counts = lax.dynamic_slice_in_dim(obs_count, first_tile, per_device, 0)
    positions = lax.broadcasted_iota(jnp.int32, (per_device, slot_count), 1)
    live_mask = positions < counts[:, None]
    innovation = jnp.where(live_mask, obs_value - obs_mean, 0.0)
    root_weight = jnp.sqrt(obs_weight)
    masked_weight = jnp.where(live_mask, root_weight, 0.0)
    scaled_innov = (root_weight * innovation).astype(jnp.bfloat16)
    grams = []
    vectors = []
    for tile_index in range(per_device):
        gram_one, vector_one = tile_gram(
            observed[:, tile_index],
            obs_mean[tile_index],
            masked_weight[tile_index],
            scaled_innov[tile_index],
            counts[tile_index],
            ens_size,
        )
        grams.append(gram_one)
        vectors.append(vector_one)
    gram_tiles = jnp.stack(grams)
    vector_tiles = jnp.stack(vectors)
    weights = lax.map(tile_weights, (gram_tiles, vector_tiles))
    result = mean_tiles[None] + jnp.einsum(
        "tjk,jtf->ktf", weights, pert_tiles, preferred_element_type=jnp.float32
    )
    result = result.reshape(ens_size, per_device, nfield, columns)
    return lax.all_to_all(result, "ens", split_axis=0, concat_axis=1, tiled=True)


def plan_kernel(counts, table, fits):
    lane = lax.broadcasted_iota(jnp.int32, (8, LANES), 1)
    device = lane % WAYS
    tiles = counts[...]
    key = tiles * GROUP + lane
    rank = jnp.zeros_like(key)
    for step in range(1, GROUP):
        rank += (pltpu.roll(key, step, 1) > key).astype(jnp.int32)
    first, second, third = jnp.zeros_like(key), jnp.zeros_like(key), jnp.zeros_like(key)
    third_rank = jnp.where(device % 2 == 0, 79 - device // 2, -1)
    for step in range(GROUP):
        there = pltpu.roll(rank, step, 1) if step else rank
        value = pltpu.roll(key, step, 1) if step else key
        first = jnp.where(there == device, value, first)
        second = jnp.where(there == 2 * WAYS - 1 - device, value, second)
        third = jnp.where(there == third_rank, value, third)

    def blocks_of(array):
        return (array // GROUP + LANES - 1) // LANES

    pair = (blocks_of(first) + blocks_of(second)) * WAYS + device
    pair_rank = jnp.zeros_like(pair)
    for step in range(1, WAYS):
        pair_rank += (pltpu.roll(pair, step, 1) > pair).astype(jnp.int32)
    wanted = device // 2 + jnp.where(device % 2 == 0, WAYS // 2, 0)
    one, two = jnp.zeros_like(key), jnp.zeros_like(key)
    for step in range(WAYS):
        hit = (pltpu.roll(pair_rank, step, 1) if step else pair_rank) == wanted
        one = jnp.where(hit, pltpu.roll(first, step, 1) if step else first, one)
        two = jnp.where(hit, pltpu.roll(second, step, 1) if step else second, two)
    load = blocks_of(one) + blocks_of(two) + blocks_of(third)
    over = (load > CAPACITY) | (blocks_of(third) > THIRD) | ((rank >= 80) & (tiles > 0))
    fits[0, 0] = 1 - jnp.max(over.astype(jnp.int32))

    row = lax.broadcasted_iota(jnp.int32, (8, LANES), 0)
    wide_lane = lax.broadcasted_iota(jnp.int32, (WAYS, LANES), 1)
    wide_row = lax.broadcasted_iota(jnp.int32, (WAYS, LANES), 0)

    def column(array):
        mine = jnp.sum(jnp.where(row == lax.axis_index("bal"), array, 0), axis=0, keepdims=True)
        mine = jnp.broadcast_to(mine, (WAYS, LANES))
        return jnp.sum(jnp.where(wide_lane == wide_row, mine, 0), axis=1, keepdims=True)

    keys = [column(array) for array in (one, two, third)]
    size = [blocks_of(array) for array in keys]
    start = [jnp.zeros_like(size[0]), CAPACITY - size[2] - size[1], CAPACITY - size[2]]

    def table_of(place):
        at_key, at_block = jnp.broadcast_to(keys[0], place.shape), jnp.full_like(place, -1)
        for slot in range(HELD):
            here = (place >= start[slot]) & (place < start[slot] + size[slot])
            at_key = jnp.where(here, keys[slot], at_key)
            at_block = jnp.where(here, place - start[slot], at_block)
        return at_key, at_block

    at_key, at_block = table_of(wide_lane)
    out = jnp.maximum(at_block, 0) * GROUP + at_key % GROUP
    at_key, at_block = table_of(wide_lane - AT_COUNT)
    left = jnp.where(at_block >= 0, at_key // GROUP - at_block * LANES, 0)
    out = jnp.where(wide_lane >= AT_COUNT, left, out)
    for slot in range(HELD):
        out = jnp.where(wide_lane == AT_TILE + slot, keys[slot] % GROUP, out)
        out = jnp.where(wide_lane == AT_BLOCKS + slot, size[slot], out)
    table[...] = out


def make_plan(obs_count):
    return pl.pallas_call(
        plan_kernel,
        out_shape=(
            jax.ShapeDtypeStruct((WAYS, LANES), jnp.int32),
            jax.ShapeDtypeStruct((1, 1), jnp.int32),
        ),
        in_specs=[pl.BlockSpec(memory_space=pltpu.VMEM)],
        out_specs=(
            pl.BlockSpec(memory_space=pltpu.VMEM),
            pl.BlockSpec(memory_space=pltpu.SMEM),
        ),
        name="plan",
    )(obs_count.reshape(8, GROUP))


def displacements():
    every = [(dx, dy, dc) for dx in range(4) for dy in range(4) for dc in range(2)][1:]
    return sorted(every, key=lambda d: -(min(d[0], 4 - d[0]) + min(d[1], 4 - d[1])))


def shifted(me, step, sign=1):
    x, y, core = me // 8, (me // 2) % 4, me % 2
    dx, dy = (step[0], step[1]) if sign > 0 else ((4 - step[0]) % 4, (4 - step[1]) % 4)
    return (((x + dx) % 4) * 4 + (y + dy) % 4) * 2 + (core + step[2]) % 2


def centred(c, matrix, eye):
    half = ENS // 2
    top, low = matrix[:half, :half], matrix[half:, half:]
    mean = jnp.sum((top + low) * eye) * (1.0 / ENS)
    upper = jnp.concatenate([top - mean * eye, matrix[:half, half:]], axis=1)
    lower = jnp.concatenate([matrix[half:, :half], low - mean * eye], axis=1)
    deviation = jnp.concatenate([upper, lower], axis=0)
    return c + mean, deviation, deviation.astype(jnp.bfloat16)


def times(left, right, eye):
    cross = left[0] * right[1] + right[0] * left[1]
    inner = jnp.dot(left[2], right[2], preferred_element_type=jnp.float32)
    return centred(left[0] * right[0], cross + inner, eye)


def middle_of(product):
    return 1.5 - 0.5 * product[0], -0.5 * product[1], product[2] * jnp.bfloat16(-0.5)


def row_times(row, z):
    high = row.astype(jnp.bfloat16)
    low = (row - high.astype(jnp.float32)).astype(jnp.bfloat16)
    rest = (z[1] - z[2].astype(jnp.float32)).astype(jnp.bfloat16)
    out = jnp.dot(high, z[2], preferred_element_type=jnp.float32)
    out = out + jnp.dot(low, z[2], preferred_element_type=jnp.float32)
    out = out + jnp.dot(high, rest, preferred_element_type=jnp.float32)
    return z[0] * row + out


def coded(array, scale):
    return jnp.round(array * scale).astype(jnp.int32).astype(jnp.int16)


def decoded(array, scale):
    return array.astype(jnp.int32).astype(jnp.float32) * (1.0 / scale)


def analyse_kernel(
    table, obs_hbm, mem_hbm, values, weights,
    out_recv,
    obs_in, wide, mem_in, obs_send, mem_send, side_send, obs_recv, mem_recv, side_recv, side,
    out_send, root, root_t,
    in_sem, obs_ssem, obs_rsem, mem_ssem, mem_rsem, side_ssem, side_rsem, out_ssem, out_rsem, own_sem,
):
    me = lax.axis_index("ens")
    core = me % 2
    steps = displacements()
    targets = [shifted(me, step) for step in steps]
    sources = [shifted(me, step, -1) for step in steps]

    def remote(src, dst, ssem, rsem, target):
        return pltpu.make_async_remote_copy(
            src_ref=src, dst_ref=dst, send_sem=ssem, recv_sem=rsem,
            device_id={"ens": target}, device_id_type=MESH,
        )

    mem_load = pltpu.make_async_copy(mem_hbm, mem_in, in_sem.at[ROWS])
    obs_loads = [
        pltpu.make_async_copy(obs_hbm.at[m], obs_in.at[m], in_sem.at[m]) for m in range(ROWS)
    ]
    for copy in obs_loads:
        copy.start()
    mem_load.start()

    barrier = pltpu.get_barrier_semaphore()
    for target in targets:
        pl.semaphore_signal(barrier, inc=1, device_id={"ens": target}, device_id_type=MESH)
    side_send[0:TILE_ROWS] = coded(values[...], CODE)
    side_send[TILE_ROWS : 2 * TILE_ROWS] = coded(jnp.sqrt(weights[...]), ROOT_CODE)
    pl.semaphore_wait(barrier, WAYS - 1)

    side_copies = []
    for i, (step, target) in enumerate(zip(steps, targets)):
        if step[2] == 0:
            copy = remote(
                side_send, side_recv.at[core, me // 2], side_ssem.at[i], side_rsem.at[i], target
            )
            copy.start()
            side_copies.append(copy)
    own_side = pltpu.make_async_copy(side_send, side_recv.at[core, me // 2], own_sem.at[0])
    own_side.start()

    for m in range(ROWS):
        obs_loads[m].wait()

        def widen(block, carry):
            first = pl.multiple_of((m * SLOT_BLOCKS + block) * GROUP, GROUP)
            lanes = pl.ds(pl.multiple_of(block * LANES, LANES), LANES)
            wide[pl.ds(first, GROUP), :] = obs_in[m, :, lanes].astype(jnp.float32)
            return carry

        lax.fori_loop(0, SLOT_BLOCKS, widen, 0)

    def pack_obs(dest):
        for pair in range(CAPACITY // 2):
            rows = [
                wide[pl.ds(table[dest, 2 * pair + j], ROWS, stride=SLOT_BLOCKS * GROUP), :]
                for j in range(2)
            ]
            obs_send[dest, pair] = jnp.concatenate(rows, axis=0).astype(jnp.bfloat16)

    def pack_members(dest, slot):
        row = table[dest, AT_TILE + slot] * 4
        parts = [mem_in[pl.ds(row + f, ROWS, stride=4 * GROUP), :] for f in range(4)]
        mem_send[slot, dest] = coded(jnp.concatenate(parts, axis=0), CODE)

    obs_copies = []
    for i, target in enumerate(targets):
        pack_obs(target)
        copy = remote(
            obs_send.at[target], obs_recv.at[me], obs_ssem.at[i], obs_rsem.at[i], target
        )
        copy.start()
        obs_copies.append(copy)
    pack_obs(me)
    copy = pltpu.make_async_copy(obs_send.at[me], obs_recv.at[me], own_sem.at[1])
    copy.start()
    obs_copies.append(copy)

    mem_load.wait()
    mem_copies = []
    for slot in range(HELD):
        for i, target in enumerate(targets):
            pack_members(target, slot)
            copy = remote(
                mem_send.at[slot, target], mem_recv.at[slot, me],
                mem_ssem.at[slot, i], mem_rsem.at[slot, i], target,
            )
            mem_copies.append(copy)
            if slot < 2:
                copy.start()
            else:
                pl.when(target % 2 == 0)(copy.start)
        pack_members(me, slot)
        copy = pltpu.make_async_copy(
            mem_send.at[slot, me], mem_recv.at[slot, me], own_sem.at[2 + slot]
        )
        copy.start()
        mem_copies.append(copy)

    for copy in side_copies:
        copy.wait()
    own_side.wait()
    partner = me + 1 - 2 * core
    copy = remote(
        side_recv.at[core], side_recv.at[core], side_ssem.at[WAYS - 1], side_rsem.at[WAYS - 1], partner
    )
    copy.start()
    copy.wait()
    for c in range(2):
        for chip in range(WAYS // 2):
            first = (chip * 2 + c) * 2 * TILE_ROWS
            side[first : first + 2 * TILE_ROWS, :] = (
                side_recv[c, chip].astype(jnp.int32).astype(jnp.float32)
            )

    for copy in obs_copies:
        copy.wait()
    lane = lax.broadcasted_iota(jnp.int32, (1, LANES), 1)
    for block in range(CAPACITY):
        half = (block % 2) * ROWS
        columns = pl.ds(block * LANES, LANES)
        seen = obs_recv[:, block // 2].astype(jnp.float32)[:, half : half + ROWS, :]
        seen = seen.reshape(ENS, LANES)
        mean = jnp.sum(seen, axis=0, keepdims=True) * (1.0 / ENS)
        source = table[me, block]
        tile, part = source % GROUP, source // GROUP
        side_row = (tile // 4) * 2 * TILE_ROWS + (tile % 4) * SLOT_BLOCKS + part
        live = lane < table[me, AT_COUNT + block]
        scale = side[pl.ds(side_row + TILE_ROWS, 1), :] * (1.0 / ROOT_CODE)
        scale = jnp.where(live, scale, 0.0)
        innov = scale * (side[pl.ds(side_row, 1), :] * (1.0 / CODE) - mean)
        rows = scale * (seen - mean)
        root[0:ENS, columns] = rows.astype(jnp.bfloat16)
        root[ENS : ENS + 16, columns] = jnp.broadcast_to(innov, (16, LANES)).astype(jnp.bfloat16)
        root_t[block * LANES : (block + 1) * LANES, :] = rows.T.astype(jnp.bfloat16)

    reach = [
        (0, SLOT_BLOCKS),
        ((CAPACITY - THIRD - CAPACITY // 2) // 2 * 2, CAPACITY),
        (CAPACITY - THIRD, CAPACITY),
    ]
    size = [table[me, AT_BLOCKS + slot] for slot in range(HELD)]
    start = [jnp.int32(0), CAPACITY - size[2] - size[1], CAPACITY - size[2]]
    half = ENS // 2
    eye = (
        lax.broadcasted_iota(jnp.int32, (half, half), 0)
        == lax.broadcasted_iota(jnp.int32, (half, half), 1)
    ).astype(jnp.float32)
    held = range(HELD)
    vecs, bounds, ys = [], [], []
    for slot in held:
        low, high = reach[slot]
        place = low + lax.broadcasted_iota(jnp.int32, (1, (high - low) * LANES), 1) // LANES
        mine = (place >= start[slot]) & (place < start[slot] + size[slot])
        part = root[:, low * LANES : high * LANES] * mine.astype(jnp.float32).astype(jnp.bfloat16)
        sums = jnp.dot(
            part, root_t[low * LANES : high * LANES, :], preferred_element_type=jnp.float32
        )
        gram = sums[0:ENS]
        vecs.append(sums[ENS : ENS + 8])
        trace = jnp.sum((gram[:half, :half] + gram[half:, half:]) * eye)
        bound = (ENS - 1.0) + trace
        bounds.append(bound)
        ys.append(centred((ENS - 1.0) / bound, gram * (1.0 / bound), eye))
    zs = middles = [middle_of(y) for y in ys]
    ys = [times(ys[slot], middles[slot], eye) for slot in held]
    for iteration in range(1, NEWTON):
        middles = [middle_of(times(zs[slot], ys[slot], eye)) for slot in held]
        if iteration < NEWTON - 1:
            ys = [times(ys[slot], middles[slot], eye) for slot in held]
        zs = [times(middles[slot], zs[slot], eye) for slot in held]
    weight_t = []
    for slot in held:
        z, bound = zs[slot], bounds[slot]
        shift = row_times(row_times(vecs[slot], z), z)[0:1] * (1.0 / bound)
        factor = jnp.sqrt(jnp.float32(ENS - 1.0)) / jnp.sqrt(bound)
        diagonal = (factor * z[0]) * eye
        full = factor * z[1] + shift
        upper = jnp.concatenate([full[:half, :half] + diagonal, full[:half, half:]], axis=1)
        lower = jnp.concatenate([full[half:, :half], full[half:, half:] + diagonal], axis=1)
        weight_t.append(jnp.concatenate([upper, lower], axis=0).astype(jnp.bfloat16))

    others = WAYS - 1
    out_copies = []
    for slot in range(HELD):
        for i in range(others):
            copy = mem_copies[slot * WAYS + i]
            if slot < 2:
                copy.wait()
            else:
                pl.when(targets[i] % 2 == 0)(copy.wait_send)
                pl.when(core == 0)(copy.wait_recv)
        mem_copies[slot * WAYS + others].wait()
        raw = decoded(mem_recv[slot], CODE)
        fields = [raw[:, f * ROWS : (f + 1) * ROWS, :].reshape(ENS, LANES) for f in range(4)]
        state = jnp.concatenate(fields, axis=1)
        mean = jnp.sum(state, axis=0, keepdims=True) * (1.0 / ENS)
        pert = (state - mean).astype(jnp.bfloat16)
        result = mean + jnp.dot(weight_t[slot], pert, preferred_element_type=jnp.float32)
        parts = [
            result[:, f * LANES : (f + 1) * LANES].reshape(WAYS, ROWS, LANES) for f in range(4)
        ]
        out_send[slot] = jnp.concatenate(parts, axis=1).astype(jnp.bfloat16)
        for i, target in enumerate(targets):
            copy = remote(
                out_send.at[slot, target], out_recv.at[slot, me],
                out_ssem.at[slot, i], out_rsem.at[slot, i], target,
            )
            out_copies.append(copy)
            if slot < 2:
                copy.start()
            else:
                pl.when(core == 0)(copy.start)
        copy = pltpu.make_async_copy(
            out_send.at[slot, me], out_recv.at[slot, me], own_sem.at[2 + HELD + slot]
        )
        copy.start()
        out_copies.append(copy)
    for slot in range(HELD):
        for i in range(others):
            copy = out_copies[slot * WAYS + i]
            if slot < 2:
                copy.wait()
            else:
                pl.when(core == 0)(copy.wait_send)
                pl.when(sources[i] % 2 == 0)(copy.wait_recv)
        out_copies[slot * WAYS + others].wait()


def exchange_and_analyse(table, obs_ens, members, values, weights):
    smem = pl.BlockSpec(memory_space=pltpu.SMEM)
    vmem = pl.BlockSpec(memory_space=pltpu.VMEM)
    anywhere = pl.BlockSpec(memory_space=pl.ANY)
    others = WAYS - 1
    dma = pltpu.SemaphoreType.DMA
    pairs = CAPACITY // 2
    return pl.pallas_call(
        analyse_kernel,
        out_shape=jax.ShapeDtypeStruct((HELD, WAYS, 32, LANES), jnp.bfloat16),
        in_specs=[smem, anywhere, anywhere, vmem, vmem],
        out_specs=anywhere,
        scratch_shapes=[
            pltpu.VMEM((ROWS, GROUP, SLOT_BLOCKS * LANES), jnp.bfloat16),
            pltpu.VMEM((ROWS * SLOT_BLOCKS * GROUP, LANES), jnp.float32),
            pltpu.VMEM((ROWS * GROUP * 4, LANES), jnp.float32),
            pltpu.VMEM((WAYS, pairs, 16, LANES), jnp.bfloat16),
            pltpu.VMEM((HELD, WAYS, 32, LANES), jnp.int16),
            pltpu.VMEM((2 * TILE_ROWS, LANES), jnp.int16),
            pltpu.VMEM((WAYS, pairs, 16, LANES), jnp.bfloat16),
            pltpu.VMEM((HELD, WAYS, 32, LANES), jnp.int16),
            pltpu.VMEM((2, WAYS // 2, 2 * TILE_ROWS, LANES), jnp.int16),
            pltpu.VMEM((WAYS * 2 * TILE_ROWS, LANES), jnp.float32),
            pltpu.VMEM((HELD, WAYS, 32, LANES), jnp.bfloat16),
            pltpu.VMEM((ENS + 16, CAPACITY * LANES), jnp.bfloat16),
            pltpu.VMEM((CAPACITY * LANES, ENS), jnp.bfloat16),
            dma((ROWS + 1,)),
            dma((others,)),
            dma((others,)),
            dma((HELD, others)),
            dma((HELD, others)),
            dma((WAYS,)),
            dma((WAYS,)),
            dma((HELD, others)),
            dma((HELD, others)),
            dma((2 + 2 * HELD,)),
        ],
        compiler_params=pltpu.CompilerParams(
            collective_id=0, has_side_effects=True, vmem_limit_bytes=56 << 20
        ),
        name="analyse",
    )(table, obs_ens, members, values, weights)


def scatter_kernel(table, members, recv, out):
    out[...] = members[...]

    def place(dest, carry):
        for slot in range(HELD):
            row = table[dest, AT_TILE + slot] * 4

            @pl.when(table[dest, AT_BLOCKS + slot] > 0)
            def _():
                tall = recv[slot, dest].astype(jnp.float32)
                for f in range(4):
                    out[pl.ds(row + f, ROWS, stride=4 * GROUP), :] = tall[f * ROWS : (f + 1) * ROWS]

        return carry

    lax.fori_loop(0, WAYS, place, 0)


def scatter(table, members, recv):
    smem = pl.BlockSpec(memory_space=pltpu.SMEM)
    vmem = pl.BlockSpec(memory_space=pltpu.VMEM)
    return pl.pallas_call(
        scatter_kernel,
        out_shape=jax.ShapeDtypeStruct(members.shape, jnp.float32),
        in_specs=[smem, vmem, vmem],
        out_specs=vmem,
        compiler_params=pltpu.CompilerParams(vmem_limit_bytes=40 << 20),
        name="scatter",
    )(table, members, recv)


def body(members, obs_ens, obs_count, obs_value, obs_weight):
    table, fits = make_plan(obs_count)

    def compact(members, obs_ens, obs_count, obs_value, obs_weight):
        flat = members.reshape(-1, LANES)
        recv = exchange_and_analyse(
            table, obs_ens, flat, obs_value.reshape(-1, LANES), obs_weight.reshape(-1, LANES)
        )
        return scatter(table, flat, recv).reshape(members.shape)

    return lax.cond(
        fits[0, 0] > 0, compact, static_body, members, obs_ens, obs_count, obs_value, obs_weight
    )


def solution(mesh):
    in_specs = (
        P("ens", "bal", None, None),
        P("ens", "bal", None),
        P(),
        P(("bal", "ens"), None),
        P(("bal", "ens"), None),
    )
    out_specs = P("ens", "bal", None, None)
    return jax.shard_map(body, mesh=mesh, in_specs=in_specs, out_specs=out_specs, check_vma=False)
```

```python
import functools

import jax
import jax.numpy as jnp
from jax import lax
from jax.experimental import pallas as pl
from jax.experimental.pallas import tpu as pltpu
from jax.sharding import PartitionSpec as P

NEWTON = 5
MESH = pl.DeviceIdType.MESH
WAYS = 32
GROUP = 128
LANES = 128
SLOT_BLOCKS = 16
HELD = 3
CAPACITY = 24
THIRD = 6
ROWS = 8
ENS = 256
CODE = 32767.0 / 6.0
ROOT_CODE = 32767.0 / 0.708
SIDE_ROWS = 8 * SLOT_BLOCKS
AT_TILE, AT_BLOCKS, AT_COUNT = 32, 36, 64


def solve_weights(gram_matrix, obs_vector):
    highest = lax.Precision.HIGHEST
    ens_size = gram_matrix.shape[0]
    identity = jnp.eye(ens_size, dtype=jnp.float32)
    scale_bound = ens_size - 1.0 + jnp.trace(gram_matrix)
    y_matrix = ((ens_size - 1.0) * identity + gram_matrix) / scale_bound
    z_matrix = identity
    for iteration in range(NEWTON):
        middle = 1.5 * identity - 0.5 * jnp.dot(z_matrix, y_matrix, precision=highest)
        y_matrix = jnp.dot(y_matrix, middle, precision=highest)
        z_matrix = jnp.dot(middle, z_matrix, precision=highest)
    inner_vec = jnp.dot(z_matrix, obs_vector, precision=highest)
    shift_vec = jnp.dot(z_matrix, inner_vec, precision=highest) / scale_bound
    factor = jnp.sqrt(ens_size - 1.0) / jnp.sqrt(scale_bound)
    return (factor * z_matrix + shift_vec[:, None]).astype(jnp.bfloat16)


def unit_weights(gram_matrix, obs_vector):
    return jnp.eye(gram_matrix.shape[0], dtype=jnp.bfloat16)


def tile_weights(operands):
    gram_matrix, obs_vector = operands
    return lax.cond(
        jnp.trace(gram_matrix) > 0.0, solve_weights, unit_weights, gram_matrix, obs_vector
    )


def tile_gram(obs_rows, centre_row, weight_row, innov_row, live_count, ens_size):
    zero_sums = (jnp.zeros((ens_size, ens_size), jnp.float32), jnp.zeros((ens_size,), jnp.float32))
    block_count = (live_count + 127) // 128

    def add_block(index_block, totals):
        first_slot = index_block * 128
        obs_piece = lax.dynamic_slice_in_dim(obs_rows, first_slot, 128, 1)
        centre_piece = lax.dynamic_slice_in_dim(centre_row, first_slot, 128, 0)
        weight_piece = lax.dynamic_slice_in_dim(weight_row, first_slot, 128, 0)
        rhs_piece = lax.dynamic_slice_in_dim(innov_row, first_slot, 128, 0)
        root_piece = (
            weight_piece[None, :] * (obs_piece.astype(jnp.float32) - centre_piece[None, :])
        ).astype(jnp.bfloat16)
        gram_piece = lax.dot_general(
            root_piece, root_piece, (((1,), (1,)), ((), ())), preferred_element_type=jnp.float32
        )
        vector_piece = jnp.dot(root_piece, rhs_piece, preferred_element_type=jnp.float32)
        return (totals[0] + gram_piece, totals[1] + vector_piece)

    return lax.fori_loop(0, block_count, add_block, zero_sums)


def static_body(members, obs_ens, obs_count, obs_value, obs_weight):
    member_block, tile_block, nfield, columns = members.shape
    ens_ways = lax.axis_size("ens")
    ens_size = member_block * ens_ways
    per_device, slot_count = obs_value.shape
    state_width = nfield * columns
    first_tile = (lax.axis_index("bal") * ens_ways + lax.axis_index("ens")) * per_device
    ensemble = lax.all_to_all(members, "ens", split_axis=1, concat_axis=0, tiled=True)
    observed = lax.all_to_all(obs_ens, "ens", split_axis=1, concat_axis=0, tiled=True)
    mean_tiles = jnp.mean(ensemble, axis=0)
    pert_tiles = (ensemble - mean_tiles[None]).astype(jnp.bfloat16)
    pert_tiles = pert_tiles.reshape(ens_size, per_device, state_width)
    mean_tiles = mean_tiles.reshape(per_device, state_width)
    obs_mean = jnp.sum(observed, axis=0, dtype=jnp.float32) / ens_size
    counts = lax.dynamic_slice_in_dim(obs_count, first_tile, per_device, 0)
    positions = lax.broadcasted_iota(jnp.int32, (per_device, slot_count), 1)
    live_mask = positions < counts[:, None]
    innovation = jnp.where(live_mask, obs_value - obs_mean, 0.0)
    root_weight = jnp.sqrt(obs_weight)
    masked_weight = jnp.where(live_mask, root_weight, 0.0)
    scaled_innov = (root_weight * innovation).astype(jnp.bfloat16)
    grams = []
    vectors = []
    for tile_index in range(per_device):
        gram_one, vector_one = tile_gram(
            observed[:, tile_index],
            obs_mean[tile_index],
            masked_weight[tile_index],
            scaled_innov[tile_index],
            counts[tile_index],
            ens_size,
        )
        grams.append(gram_one)
        vectors.append(vector_one)
    gram_tiles = jnp.stack(grams)
    vector_tiles = jnp.stack(vectors)
    weights = lax.map(tile_weights, (gram_tiles, vector_tiles))
    result = mean_tiles[None] + jnp.einsum(
        "tjk,jtf->ktf", weights, pert_tiles, preferred_element_type=jnp.float32
    )
    result = result.reshape(ens_size, per_device, nfield, columns)
    return lax.all_to_all(result, "ens", split_axis=0, concat_axis=1, tiled=True)


def write_plan(counts, table, fits):
    lane = lax.broadcasted_iota(jnp.int32, (8, LANES), 1)
    device = lane % WAYS
    tiles = counts[...]
    key = tiles * GROUP + lane
    rank = jnp.zeros_like(key)
    for step in range(1, GROUP):
        rank += (pltpu.roll(key, step, 1) > key).astype(jnp.int32)
    first, second, third = jnp.zeros_like(key), jnp.zeros_like(key), jnp.zeros_like(key)
    third_rank = jnp.where(device % 2 == 0, 79 - device // 2, -1)
    for step in range(GROUP):
        there = pltpu.roll(rank, step, 1) if step else rank
        value = pltpu.roll(key, step, 1) if step else key
        first = jnp.where(there == device, value, first)
        second = jnp.where(there == 2 * WAYS - 1 - device, value, second)
        third = jnp.where(there == third_rank, value, third)

    def blocks_of(array):
        return (array // GROUP + LANES - 1) // LANES

    pair = (blocks_of(first) + blocks_of(second)) * WAYS + device
    pair_rank = jnp.zeros_like(pair)
    for step in range(1, WAYS):
        pair_rank += (pltpu.roll(pair, step, 1) > pair).astype(jnp.int32)
    wanted = device // 2 + jnp.where(device % 2 == 0, WAYS // 2, 0)
    one, two = jnp.zeros_like(key), jnp.zeros_like(key)
    for step in range(WAYS):
        hit = (pltpu.roll(pair_rank, step, 1) if step else pair_rank) == wanted
        one = jnp.where(hit, pltpu.roll(first, step, 1) if step else first, one)
        two = jnp.where(hit, pltpu.roll(second, step, 1) if step else second, two)
    load = blocks_of(one) + blocks_of(two) + blocks_of(third)
    over = (load > CAPACITY) | (blocks_of(third) > THIRD) | ((rank >= 80) & (tiles > 0))
    fits[0, 0] = 1 - jnp.max(over.astype(jnp.int32))

    row = lax.broadcasted_iota(jnp.int32, (8, LANES), 0)
    wide_lane = lax.broadcasted_iota(jnp.int32, (WAYS, LANES), 1)
    wide_row = lax.broadcasted_iota(jnp.int32, (WAYS, LANES), 0)

    def column(array):
        mine = jnp.sum(jnp.where(row == lax.axis_index("bal"), array, 0), axis=0, keepdims=True)
        mine = jnp.broadcast_to(mine, (WAYS, LANES))
        return jnp.sum(jnp.where(wide_lane == wide_row, mine, 0), axis=1, keepdims=True)

    keys = [column(array) for array in (one, two, third)]
    size = [blocks_of(array) for array in keys]
    start = [jnp.zeros_like(size[0]), CAPACITY - size[2] - size[1], CAPACITY - size[2]]

    def table_of(place):
        at_key, at_block = jnp.broadcast_to(keys[0], place.shape), jnp.full_like(place, -1)
        for slot in range(HELD):
            here = (place >= start[slot]) & (place < start[slot] + size[slot])
            at_key = jnp.where(here, keys[slot], at_key)
            at_block = jnp.where(here, place - start[slot], at_block)
        return at_key, at_block

    at_key, at_block = table_of(wide_lane)
    out = jnp.maximum(at_block, 0) * GROUP + at_key % GROUP
    at_key, at_block = table_of(wide_lane - AT_COUNT)
    left = jnp.where(at_block >= 0, at_key // GROUP - at_block * LANES, 0)
    out = jnp.where(wide_lane >= AT_COUNT, left, out)
    for slot in range(HELD):
        out = jnp.where(wide_lane == AT_TILE + slot, keys[slot] % GROUP, out)
        out = jnp.where(wide_lane == AT_BLOCKS + slot, size[slot], out)
    table[...] = out


def displacements():
    every = [(dx, dy, dc) for dx in range(4) for dy in range(4) for dc in range(2)][1:]
    return sorted(every, key=lambda d: -(min(d[0], 4 - d[0]) + min(d[1], 4 - d[1])))


def shifted(me, step, sign=1):
    x, y, core = me // 8, (me // 2) % 4, me % 2
    dx, dy = (step[0], step[1]) if sign > 0 else ((4 - step[0]) % 4, (4 - step[1]) % 4)
    return (((x + dx) % 4) * 4 + (y + dy) % 4) * 2 + (core + step[2]) % 2


def centred(c, matrix, eye):
    half = ENS // 2
    top, low = matrix[:half, :half], matrix[half:, half:]
    mean = jnp.sum((top + low) * eye) * (1.0 / ENS)
    upper = jnp.concatenate([top - mean * eye, matrix[:half, half:]], axis=1)
    lower = jnp.concatenate([matrix[half:, :half], low - mean * eye], axis=1)
    deviation = jnp.concatenate([upper, lower], axis=0)
    return c + mean, deviation, deviation.astype(jnp.bfloat16)


def times(left, right, eye):
    cross = left[0] * right[1] + right[0] * left[1]
    inner = jnp.dot(left[2], right[2], preferred_element_type=jnp.float32)
    return centred(left[0] * right[0], cross + inner, eye)


def middle_of(product):
    return 1.5 - 0.5 * product[0], -0.5 * product[1], product[2] * jnp.bfloat16(-0.5)


def row_times(row, z):
    high = row.astype(jnp.bfloat16)
    low = (row - high.astype(jnp.float32)).astype(jnp.bfloat16)
    rest = (z[1] - z[2].astype(jnp.float32)).astype(jnp.bfloat16)
    out = jnp.dot(high, z[2], preferred_element_type=jnp.float32)
    out = out + jnp.dot(low, z[2], preferred_element_type=jnp.float32)
    out = out + jnp.dot(high, rest, preferred_element_type=jnp.float32)
    return z[0] * row + out


def coded(array, scale):
    return jnp.round(array * scale).astype(jnp.int32).astype(jnp.int16)


def decoded(array, scale):
    return array.astype(jnp.int32).astype(jnp.float32) * (1.0 / scale)


def analyse_kernel(
    counts, obs_hbm, mem_hbm, values, weights,
    out_recv, plan, fits,
    table, obs_in, wide, mem_in, obs_send, mem_send, side_send, obs_recv, mem_recv, side_recv, side,
    out_send, root, root_t,
    in_sem, side_ssem, side_rsem, phase_sem,
):
    me = lax.axis_index("ens")
    core = me % 2
    steps = displacements()
    targets = [shifted(me, step) for step in steps]

    def remote(src, dst, ssem, rsem, target):
        return pltpu.make_async_remote_copy(
            src_ref=src, dst_ref=dst, send_sem=ssem, recv_sem=rsem,
            device_id={"ens": target}, device_id_type=MESH,
        )

    barrier = pltpu.get_barrier_semaphore()
    for target in targets:
        pl.semaphore_signal(barrier, inc=1, device_id={"ens": target}, device_id_type=MESH)
    def drain(ref, sem):
        pltpu.make_async_copy(ref, ref, sem).wait()

    mem_load = pltpu.make_async_copy(mem_hbm, mem_in, in_sem.at[ROWS])
    obs_loads = [
        pltpu.make_async_copy(obs_hbm.at[m], obs_in.at[m], in_sem.at[m]) for m in range(ROWS)
    ]
    for copy in obs_loads:
        copy.start()
    mem_load.start()

    parts = []
    for part in range(SLOT_BLOCKS):
        lanes = slice(part * LANES, (part + 1) * LANES)
        parts += [values[:, lanes] * CODE, jnp.sqrt(weights[:, lanes]) * ROOT_CODE]
    side_send[...] = coded(jnp.concatenate(parts, axis=0), 1.0)
    write_plan(counts, plan, fits)
    table_copy = pltpu.make_async_copy(plan, table, in_sem.at[ROWS + 1])
    table_copy.start()
    pl.semaphore_wait(barrier, WAYS - 1)

    x, y = me // 8, (me // 2) % 4
    outer, inner = y + core * (x - y), x + core * (y - x)
    side_copies = []
    for step in range(1, 4):
        target = ((x + step * (1 - core)) % 4) * 8 + ((y + step * core) % 4) * 2 + core
        copy = remote(
            side_send, side_recv.at[core, outer, inner], side_ssem.at[step], side_rsem.at[step], target
        )
        copy.start()
        side_copies.append(copy)
    copy = pltpu.make_async_copy(side_send, side_recv.at[core, outer, inner], side_rsem.at[0])
    copy.start()
    side_copies.append(copy)

    for m in range(ROWS):
        obs_loads[m].wait()

        def widen(block, carry):
            first = pl.multiple_of((m * SLOT_BLOCKS + block) * GROUP, GROUP)
            lanes = pl.ds(pl.multiple_of(block * LANES, LANES), LANES)
            wide[pl.ds(first, GROUP), :] = obs_in[m, :, lanes].astype(jnp.float32)
            return carry

        lax.fori_loop(0, SLOT_BLOCKS, widen, 0)

    for copy in side_copies:
        copy.wait()
    side_copies = []
    for step in range(1, 4):
        target = ((x + step * core) % 4) * 8 + ((y + step * (1 - core)) % 4) * 2 + core
        copy = remote(
            side_recv.at[core, outer], side_recv.at[core, outer],
            side_ssem.at[3 + step], side_rsem.at[3 + step], target,
        )
        copy.start()
        side_copies.append(copy)
    table_copy.wait()

    def pack_obs(dest):
        for pair in range(CAPACITY // 2):
            rows = [
                wide[pl.ds(table[dest, 2 * pair + j], ROWS, stride=SLOT_BLOCKS * GROUP), :]
                for j in range(2)
            ]
            obs_send[dest, pair] = jnp.concatenate(rows, axis=0).astype(jnp.bfloat16)

    def pack_members(dest, slot):
        row = table[dest, AT_TILE + slot] * 4
        parts = [mem_in[pl.ds(row + f, ROWS, stride=4 * GROUP), :] for f in range(4)]
        mem_send[slot, dest] = coded(jnp.concatenate(parts, axis=0), CODE)

    for target in targets:
        pack_obs(target)
        remote(
            obs_send.at[target], obs_recv.at[me], phase_sem.at[0], phase_sem.at[1], target
        ).start()
    pack_obs(me)
    pltpu.make_async_copy(obs_send.at[me], obs_recv.at[me], phase_sem.at[1]).start()

    mem_load.wait()
    for slot in range(HELD):

        def send_members(target, slot=slot):
            remote(
                mem_send.at[slot, target], mem_recv.at[slot, me],
                phase_sem.at[2 + slot], phase_sem.at[5 + slot], target,
            ).start()

        def keep_members(slot=slot):
            pltpu.make_async_copy(
                mem_send.at[slot, me], mem_recv.at[slot, me], phase_sem.at[5 + slot]
            ).start()

        for target in targets:
            pack_members(target, slot)
            if slot < 2:
                send_members(target)
            else:
                pl.when(target % 2 == 0)(functools.partial(send_members, target))
        pack_members(me, slot)
        if slot < 2:
            keep_members()
        else:
            pl.when(core == 0)(keep_members)

    for copy in side_copies:
        copy.wait()
    copy = remote(
        side_recv.at[core], side_recv.at[core], side_ssem.at[7], side_rsem.at[7], me + 1 - 2 * core
    )
    copy.start()
    copy.wait()
    for c in range(2):
        for far in range(4):
            for near in range(4):
                chip = near * 4 + far if c == 0 else far * 4 + near
                first = (chip * 2 + c) * SIDE_ROWS
                side[first : first + SIDE_ROWS, :] = (
                    side_recv[c, far, near].astype(jnp.int32).astype(jnp.float32)
                )

    drain(obs_recv, phase_sem.at[1])
    lane = lax.broadcasted_iota(jnp.int32, (1, LANES), 1)
    for block in range(CAPACITY):
        half = (block % 2) * ROWS
        columns = pl.ds(block * LANES, LANES)
        seen = obs_recv[:, block // 2].astype(jnp.float32)[:, half : half + ROWS, :]
        seen = seen.reshape(ENS, LANES)
        mean = jnp.sum(seen, axis=0, keepdims=True) * (1.0 / ENS)
        source = table[me, block]
        tile, part = source % GROUP, source // GROUP
        side_row = (tile // 4) * SIDE_ROWS + part * 8 + tile % 4
        live = lane < table[me, AT_COUNT + block]
        scale = side[pl.ds(side_row + 4, 1), :] * (1.0 / ROOT_CODE)
        scale = jnp.where(live, scale, 0.0)
        innov = scale * (side[pl.ds(side_row, 1), :] * (1.0 / CODE) - mean)
        rows = scale * (seen - mean)
        root[0:ENS, columns] = rows.astype(jnp.bfloat16)
        root[ENS : ENS + 16, columns] = jnp.broadcast_to(innov, (16, LANES)).astype(jnp.bfloat16)
        root_t[block * LANES : (block + 1) * LANES, :] = rows.T.astype(jnp.bfloat16)

    reach = [
        (0, SLOT_BLOCKS),
        ((CAPACITY - THIRD - CAPACITY // 2) // 2 * 2, CAPACITY),
        (CAPACITY - THIRD, CAPACITY),
    ]
    size = [table[me, AT_BLOCKS + slot] for slot in range(HELD)]
    start = [jnp.int32(0), CAPACITY - size[2] - size[1], CAPACITY - size[2]]
    half = ENS // 2
    eye = (
        lax.broadcasted_iota(jnp.int32, (half, half), 0)
        == lax.broadcasted_iota(jnp.int32, (half, half), 1)
    ).astype(jnp.float32)
    held = range(HELD)
    vecs, bounds, ys = [], [], []
    for slot in held:
        low, high = reach[slot]
        place = low + lax.broadcasted_iota(jnp.int32, (1, (high - low) * LANES), 1) // LANES
        mine = (place >= start[slot]) & (place < start[slot] + size[slot])
        part = root[:, low * LANES : high * LANES] * mine.astype(jnp.float32).astype(jnp.bfloat16)
        sums = jnp.dot(
            part, root_t[low * LANES : high * LANES, :], preferred_element_type=jnp.float32
        )
        gram = sums[0:ENS]
        vecs.append(sums[ENS : ENS + 8])
        trace = jnp.sum((gram[:half, :half] + gram[half:, half:]) * eye)
        bound = (ENS - 1.0) + trace
        bounds.append(bound)
        ys.append(centred((ENS - 1.0) / bound, gram * (1.0 / bound), eye))
    zs = middles = [middle_of(y) for y in ys]
    ys = [times(ys[slot], middles[slot], eye) for slot in held]
    for iteration in range(1, NEWTON):
        middles = [middle_of(times(zs[slot], ys[slot], eye)) for slot in held]
        if iteration < NEWTON - 1:
            ys = [times(ys[slot], middles[slot], eye) for slot in held]
        zs = [times(middles[slot], zs[slot], eye) for slot in held]
    weight_t = []
    for slot in held:
        z, bound = zs[slot], bounds[slot]
        shift = row_times(row_times(vecs[slot], z), z)[0:1] * (1.0 / bound)
        factor = jnp.sqrt(jnp.float32(ENS - 1.0)) / jnp.sqrt(bound)
        diagonal = (factor * z[0]) * eye
        full = factor * z[1] + shift
        upper = jnp.concatenate([full[:half, :half] + diagonal, full[:half, half:]], axis=1)
        lower = jnp.concatenate([full[half:, :half], full[half:, half:] + diagonal], axis=1)
        weight_t.append(jnp.concatenate([upper, lower], axis=0).astype(jnp.bfloat16))

    half_ways = WAYS // 2
    for slot in range(HELD):
        if slot < 2:
            drain(mem_recv.at[slot], phase_sem.at[5 + slot])
        else:
            pl.when(core == 0)(lambda: drain(mem_recv.at[2], phase_sem.at[7]))
        raw = decoded(mem_recv[slot], CODE)
        fields = [raw[:, f * ROWS : (f + 1) * ROWS, :].reshape(ENS, LANES) for f in range(4)]
        state = jnp.concatenate(fields, axis=1)
        mean = jnp.sum(state, axis=0, keepdims=True) * (1.0 / ENS)
        pert = (state - mean).astype(jnp.bfloat16)
        result = mean + jnp.dot(weight_t[slot], pert, preferred_element_type=jnp.float32)
        parts = [
            result[:, f * LANES : (f + 1) * LANES].reshape(WAYS, ROWS, LANES) for f in range(4)
        ]
        out_send[slot] = jnp.concatenate(parts, axis=1).astype(jnp.bfloat16)

        def send_result(slot=slot):
            for target in targets:
                remote(
                    out_send.at[slot, target], out_recv.at[slot, me],
                    phase_sem.at[8 + slot], phase_sem.at[11 + slot], target,
                ).start()
            pltpu.make_async_copy(
                out_send.at[slot, me], out_recv.at[slot, me], phase_sem.at[11 + slot]
            ).start()

        if slot < 2:
            send_result()
        else:
            pl.when(core == 0)(send_result)

    sent = pl.ds(0, WAYS - 1)
    drain(obs_send.at[sent], phase_sem.at[0])
    for slot in range(2):
        drain(mem_send.at[slot, sent], phase_sem.at[2 + slot])
        drain(out_send.at[slot, sent], phase_sem.at[8 + slot])
        drain(out_recv.at[slot], phase_sem.at[11 + slot])
    drain(mem_send.at[2, pl.ds(0, half_ways - 1)], phase_sem.at[4])
    pl.when(core == 1)(lambda: drain(mem_send.at[2, 0], phase_sem.at[4]))
    pl.when(core == 0)(lambda: drain(out_send.at[2, sent], phase_sem.at[10]))
    drain(out_recv.at[2, pl.ds(0, half_ways)], phase_sem.at[13])


def exchange_and_analyse(counts, obs_ens, members, values, weights):
    smem = pl.BlockSpec(memory_space=pltpu.SMEM)
    vmem = pl.BlockSpec(memory_space=pltpu.VMEM)
    anywhere = pl.BlockSpec(memory_space=pl.ANY)
    dma = pltpu.SemaphoreType.DMA
    pairs = CAPACITY // 2
    return pl.pallas_call(
        analyse_kernel,
        out_shape=(
            jax.ShapeDtypeStruct((HELD, WAYS, 32, LANES), jnp.bfloat16),
            jax.ShapeDtypeStruct((WAYS, LANES), jnp.int32),
            jax.ShapeDtypeStruct((1, 1), jnp.int32),
        ),
        in_specs=[vmem, anywhere, anywhere, vmem, vmem],
        out_specs=(anywhere, vmem, smem),
        scratch_shapes=[
            pltpu.SMEM((WAYS, LANES), jnp.int32),
            pltpu.VMEM((ROWS, GROUP, SLOT_BLOCKS * LANES), jnp.bfloat16),
            pltpu.VMEM((ROWS * SLOT_BLOCKS * GROUP, LANES), jnp.float32),
            pltpu.VMEM((ROWS * GROUP * 4, LANES), jnp.float32),
            pltpu.VMEM((WAYS, pairs, 16, LANES), jnp.bfloat16),
            pltpu.VMEM((HELD, WAYS, 32, LANES), jnp.int16),
            pltpu.VMEM((SIDE_ROWS, LANES), jnp.int16),
            pltpu.VMEM((WAYS, pairs, 16, LANES), jnp.bfloat16),
            pltpu.VMEM((HELD, WAYS, 32, LANES), jnp.int16),
            pltpu.VMEM((2, 4, 4, SIDE_ROWS, LANES), jnp.int16),
            pltpu.VMEM((WAYS * SIDE_ROWS, LANES), jnp.float32),
            pltpu.VMEM((HELD, WAYS, 32, LANES), jnp.bfloat16),
            pltpu.VMEM((ENS + 16, CAPACITY * LANES), jnp.bfloat16),
            pltpu.VMEM((CAPACITY * LANES, ENS), jnp.bfloat16),
            dma((ROWS + 2,)),
            dma((8,)),
            dma((8,)),
            dma((14,)),
        ],
        compiler_params=pltpu.CompilerParams(
            collective_id=0, has_side_effects=True, vmem_limit_bytes=56 << 20
        ),
        name="analyse",
    )(counts, obs_ens, members, values, weights)


def scatter_kernel(table, members, recv_hbm, out_hbm, recv, out, sems):
    loads = [
        pltpu.make_async_copy(members, out, sems.at[0]),
        pltpu.make_async_copy(recv_hbm, recv, sems.at[1]),
    ]
    for copy in loads:
        copy.start()
    for copy in loads:
        copy.wait()

    def place(dest, carry):
        for slot in range(HELD):
            row = table[dest, AT_TILE + slot] * 4

            @pl.when(table[dest, AT_BLOCKS + slot] > 0)
            def _():
                tall = recv[slot, dest].astype(jnp.float32)
                for f in range(4):
                    out[pl.ds(row + f, ROWS, stride=4 * GROUP), :] = tall[f * ROWS : (f + 1) * ROWS]

        return carry

    lax.fori_loop(0, WAYS, place, 0)
    store = pltpu.make_async_copy(out, out_hbm, sems.at[2])
    store.start()
    store.wait()


def scatter(table, members, recv):
    smem = pl.BlockSpec(memory_space=pltpu.SMEM)
    anywhere = pl.BlockSpec(memory_space=pl.ANY)
    return pl.pallas_call(
        scatter_kernel,
        out_shape=jax.ShapeDtypeStruct(members.shape, jnp.float32),
        in_specs=[smem, anywhere, anywhere],
        out_specs=anywhere,
        scratch_shapes=[
            pltpu.VMEM(recv.shape, recv.dtype),
            pltpu.VMEM(members.shape, jnp.float32),
            pltpu.SemaphoreType.DMA((3,)),
        ],
        compiler_params=pltpu.CompilerParams(vmem_limit_bytes=60 << 20),
        name="scatter",
    )(table, members, recv)


def body(members, obs_ens, obs_count, obs_value, obs_weight):
    flat = members.reshape(-1, LANES)
    recv, table, fits = exchange_and_analyse(
        obs_count.reshape(-1, GROUP), obs_ens, flat, obs_value, obs_weight
    )
    result = scatter(table, flat, recv).reshape(members.shape)
    return lax.cond(
        fits[0, 0] > 0,
        lambda result, *_: result,
        lambda _, *inputs: static_body(*inputs),
        result, members, obs_ens, obs_count, obs_value, obs_weight,
    )


def solution(mesh):
    in_specs = (
        P("ens", "bal", None, None),
        P("ens", "bal", None),
        P(),
        P(("bal", "ens"), None),
        P(("bal", "ens"), None),
    )
    out_specs = P("ens", "bal", None, None)
    return jax.shard_map(body, mesh=mesh, in_specs=in_specs, out_specs=out_specs, check_vma=False)
```

```python
import functools

import jax
import jax.numpy as jnp
from jax import lax
from jax.experimental import pallas as pl
from jax.experimental.pallas import tpu as pltpu
from jax.sharding import PartitionSpec as P

NEWTON = 5
MESH = pl.DeviceIdType.MESH
WAYS = 32
GROUP = 128
LANES = 128
SLOT_BLOCKS = 16
HELD = 3
CAPACITY = 24
PART = 12
THIRD = 6
ROWS = 8
ENS = 256
CODE = 32767.0 / 6.0
ROOT_CODE = 32767.0 / 0.708
SIDE_ROWS = 8 * SLOT_BLOCKS
AT_TILE, AT_BLOCKS, AT_COUNT, AT_SIDE = 32, 36, 64, 96


def solve_weights(gram_matrix, obs_vector):
    highest = lax.Precision.HIGHEST
    ens_size = gram_matrix.shape[0]
    identity = jnp.eye(ens_size, dtype=jnp.float32)
    scale_bound = ens_size - 1.0 + jnp.trace(gram_matrix)
    y_matrix = ((ens_size - 1.0) * identity + gram_matrix) / scale_bound
    z_matrix = identity
    for iteration in range(NEWTON):
        middle = 1.5 * identity - 0.5 * jnp.dot(z_matrix, y_matrix, precision=highest)
        y_matrix = jnp.dot(y_matrix, middle, precision=highest)
        z_matrix = jnp.dot(middle, z_matrix, precision=highest)
    inner_vec = jnp.dot(z_matrix, obs_vector, precision=highest)
    shift_vec = jnp.dot(z_matrix, inner_vec, precision=highest) / scale_bound
    factor = jnp.sqrt(ens_size - 1.0) / jnp.sqrt(scale_bound)
    return (factor * z_matrix + shift_vec[:, None]).astype(jnp.bfloat16)


def unit_weights(gram_matrix, obs_vector):
    return jnp.eye(gram_matrix.shape[0], dtype=jnp.bfloat16)


def tile_weights(operands):
    gram_matrix, obs_vector = operands
    return lax.cond(
        jnp.trace(gram_matrix) > 0.0, solve_weights, unit_weights, gram_matrix, obs_vector
    )


def tile_gram(obs_rows, centre_row, weight_row, innov_row, live_count, ens_size):
    zero_sums = (jnp.zeros((ens_size, ens_size), jnp.float32), jnp.zeros((ens_size,), jnp.float32))
    block_count = (live_count + 127) // 128

    def add_block(index_block, totals):
        first_slot = index_block * 128
        obs_piece = lax.dynamic_slice_in_dim(obs_rows, first_slot, 128, 1)
        centre_piece = lax.dynamic_slice_in_dim(centre_row, first_slot, 128, 0)
        weight_piece = lax.dynamic_slice_in_dim(weight_row, first_slot, 128, 0)
        rhs_piece = lax.dynamic_slice_in_dim(innov_row, first_slot, 128, 0)
        root_piece = (
            weight_piece[None, :] * (obs_piece.astype(jnp.float32) - centre_piece[None, :])
        ).astype(jnp.bfloat16)
        gram_piece = lax.dot_general(
            root_piece, root_piece, (((1,), (1,)), ((), ())), preferred_element_type=jnp.float32
        )
        vector_piece = jnp.dot(root_piece, rhs_piece, preferred_element_type=jnp.float32)
        return (totals[0] + gram_piece, totals[1] + vector_piece)

    return lax.fori_loop(0, block_count, add_block, zero_sums)


def static_body(members, obs_ens, obs_count, obs_value, obs_weight):
    member_block, tile_block, nfield, columns = members.shape
    ens_ways = lax.axis_size("ens")
    ens_size = member_block * ens_ways
    per_device, slot_count = obs_value.shape
    state_width = nfield * columns
    first_tile = (lax.axis_index("bal") * ens_ways + lax.axis_index("ens")) * per_device
    ensemble = lax.all_to_all(members, "ens", split_axis=1, concat_axis=0, tiled=True)
    observed = lax.all_to_all(obs_ens, "ens", split_axis=1, concat_axis=0, tiled=True)
    mean_tiles = jnp.mean(ensemble, axis=0)
    pert_tiles = (ensemble - mean_tiles[None]).astype(jnp.bfloat16)
    pert_tiles = pert_tiles.reshape(ens_size, per_device, state_width)
    mean_tiles = mean_tiles.reshape(per_device, state_width)
    obs_mean = jnp.sum(observed, axis=0, dtype=jnp.float32) / ens_size
    counts = lax.dynamic_slice_in_dim(obs_count, first_tile, per_device, 0)
    positions = lax.broadcasted_iota(jnp.int32, (per_device, slot_count), 1)
    live_mask = positions < counts[:, None]
    innovation = jnp.where(live_mask, obs_value - obs_mean, 0.0)
    root_weight = jnp.sqrt(obs_weight)
    masked_weight = jnp.where(live_mask, root_weight, 0.0)
    scaled_innov = (root_weight * innovation).astype(jnp.bfloat16)
    grams = []
    vectors = []
    for tile_index in range(per_device):
        gram_one, vector_one = tile_gram(
            observed[:, tile_index],
            obs_mean[tile_index],
            masked_weight[tile_index],
            scaled_innov[tile_index],
            counts[tile_index],
            ens_size,
        )
        grams.append(gram_one)
        vectors.append(vector_one)
    gram_tiles = jnp.stack(grams)
    vector_tiles = jnp.stack(vectors)
    weights = lax.map(tile_weights, (gram_tiles, vector_tiles))
    result = mean_tiles[None] + jnp.einsum(
        "tjk,jtf->ktf", weights, pert_tiles, preferred_element_type=jnp.float32
    )
    result = result.reshape(ens_size, per_device, nfield, columns)
    return lax.all_to_all(result, "ens", split_axis=0, concat_axis=1, tiled=True)


def write_plan(counts, table, fits):
    lane = lax.broadcasted_iota(jnp.int32, (8, LANES), 1)
    device = lane % WAYS
    tiles = counts[...]
    key = tiles * GROUP + lane
    rank = jnp.zeros_like(key)
    for step in range(1, GROUP):
        rank += (pltpu.roll(key, step, 1) > key).astype(jnp.int32)
    first, second, third = jnp.zeros_like(key), jnp.zeros_like(key), jnp.zeros_like(key)
    third_rank = jnp.where(device % 2 == 0, 79 - device // 2, -1)
    for step in range(GROUP):
        there = pltpu.roll(rank, step, 1) if step else rank
        value = pltpu.roll(key, step, 1) if step else key
        first = jnp.where(there == device, value, first)
        second = jnp.where(there == 2 * WAYS - 1 - device, value, second)
        third = jnp.where(there == third_rank, value, third)

    def blocks_of(array):
        return ((array >> 7) + LANES - 1) >> 7

    pair = (blocks_of(first) + blocks_of(second)) * WAYS + device
    pair_rank = jnp.zeros_like(pair)
    for step in range(1, WAYS):
        pair_rank += (pltpu.roll(pair, step, 1) > pair).astype(jnp.int32)
    wanted = device // 2 + jnp.where(device % 2 == 0, WAYS // 2, 0)
    one, two = jnp.zeros_like(key), jnp.zeros_like(key)
    for step in range(WAYS):
        hit = (pltpu.roll(pair_rank, step, 1) if step else pair_rank) == wanted
        one = jnp.where(hit, pltpu.roll(first, step, 1) if step else first, one)
        two = jnp.where(hit, pltpu.roll(second, step, 1) if step else second, two)
    load = blocks_of(one) + blocks_of(two) + blocks_of(third)
    over = (load > CAPACITY) | (blocks_of(third) > THIRD) | ((rank >= 80) & (tiles > 0))
    fits[0, 0] = 1 - jnp.max(over.astype(jnp.int32))

    row = lax.broadcasted_iota(jnp.int32, (8, LANES), 0)
    wide_lane = lax.broadcasted_iota(jnp.int32, (WAYS, LANES), 1)
    wide_row = lax.broadcasted_iota(jnp.int32, (WAYS, LANES), 0)

    def column(array):
        mine = jnp.sum(jnp.where(row == lax.axis_index("bal"), array, 0), axis=0, keepdims=True)
        mine = jnp.broadcast_to(mine, (WAYS, LANES))
        return jnp.sum(jnp.where(wide_lane == wide_row, mine, 0), axis=1, keepdims=True)

    keys = [column(array) for array in (one, two, third)]
    size = [blocks_of(array) for array in keys]
    start = [jnp.zeros_like(size[0]), CAPACITY - size[2] - size[1], CAPACITY - size[2]]

    def table_of(place):
        at_key, at_block = jnp.broadcast_to(keys[0], place.shape), jnp.full_like(place, -1)
        for slot in range(HELD):
            here = (place >= start[slot]) & (place < start[slot] + size[slot])
            at_key = jnp.where(here, keys[slot], at_key)
            at_block = jnp.where(here, place - start[slot], at_block)
        return at_key, at_block

    at_key, at_block = table_of(wide_lane)
    out = jnp.maximum(at_block, 0) * GROUP + (at_key & (GROUP - 1))
    at_key, at_block = table_of(wide_lane - AT_COUNT)
    left = jnp.where(at_block >= 0, (at_key >> 7) - at_block * LANES, 0)
    out = jnp.where(wide_lane >= AT_COUNT, left, out)
    at_key, at_block = table_of(wide_lane - AT_SIDE)
    tile = at_key & (GROUP - 1)
    near = jnp.where(lax.axis_index("ens") % 2 == 0, tile >> 5, (tile >> 3) & 3)
    side_row = near * SIDE_ROWS + jnp.maximum(at_block, 0) * 8 + (tile & 3)
    out = jnp.where(wide_lane >= AT_SIDE, side_row, out)
    for slot in range(HELD):
        out = jnp.where(wide_lane == AT_TILE + slot, keys[slot] & (GROUP - 1), out)
        out = jnp.where(wide_lane == AT_BLOCKS + slot, size[slot], out)
    table[...] = out


def displacements():
    every = [(dx, dy, dc) for dx in range(4) for dy in range(4) for dc in range(2)][1:]
    return sorted(every, key=lambda d: -(min(d[0], 4 - d[0]) + min(d[1], 4 - d[1])))


def shifted(me, step, sign=1):
    x, y, core = me // 8, (me // 2) % 4, me % 2
    dx, dy = (step[0], step[1]) if sign > 0 else ((4 - step[0]) % 4, (4 - step[1]) % 4)
    return (((x + dx) % 4) * 4 + (y + dy) % 4) * 2 + (core + step[2]) % 2


def centred(c, matrix, eye):
    half = ENS // 2
    top, low = matrix[:half, :half], matrix[half:, half:]
    mean = jnp.sum((top + low) * eye) * (1.0 / ENS)
    upper = jnp.concatenate([top - mean * eye, matrix[:half, half:]], axis=1)
    lower = jnp.concatenate([matrix[half:, :half], low - mean * eye], axis=1)
    deviation = jnp.concatenate([upper, lower], axis=0)
    return c + mean, deviation, deviation.astype(jnp.bfloat16)


def times(left, right, eye):
    cross = left[0] * right[1] + right[0] * left[1]
    inner = jnp.dot(left[2], right[2], preferred_element_type=jnp.float32)
    return centred(left[0] * right[0], cross + inner, eye)


def middle_of(product):
    return 1.5 - 0.5 * product[0], -0.5 * product[1], product[2] * jnp.bfloat16(-0.5)


def row_times(row, z):
    high = row.astype(jnp.bfloat16)
    low = (row - high.astype(jnp.float32)).astype(jnp.bfloat16)
    rest = (z[1] - z[2].astype(jnp.float32)).astype(jnp.bfloat16)
    out = jnp.dot(high, z[2], preferred_element_type=jnp.float32)
    out = out + jnp.dot(low, z[2], preferred_element_type=jnp.float32)
    out = out + jnp.dot(high, rest, preferred_element_type=jnp.float32)
    return z[0] * row + out


def coded(array, scale):
    return jnp.round(array * scale).astype(jnp.int32).astype(jnp.int16)


def decoded(array, scale):
    return array.astype(jnp.int32).astype(jnp.float32) * (1.0 / scale)


def analyse_kernel(
    counts, obs_hbm, mem_hbm, values, weights,
    out_recv, plan, fits,
    table, obs_in, wide, mem_in, obs_send, mem_send, side_send, row_send, obs_recv, mem_recv,
    side_recv, row_recv, side, rows, out_send, root, root_t, pert,
    in_sem, phase_sem,
):
    me = lax.axis_index("ens")
    core = me % 2
    steps = displacements()
    targets = [shifted(me, step) for step in steps]

    def remote(src, dst, ssem, rsem, target):
        return pltpu.make_async_remote_copy(
            src_ref=src, dst_ref=dst, send_sem=ssem, recv_sem=rsem,
            device_id={"ens": target}, device_id_type=MESH,
        )

    barrier = pltpu.get_barrier_semaphore()
    for target in targets:
        pl.semaphore_signal(barrier, inc=1, device_id={"ens": target}, device_id_type=MESH)
    def drain(ref, sem):
        pltpu.make_async_copy(ref, ref, sem).wait()

    mem_load = pltpu.make_async_copy(mem_hbm, mem_in, in_sem.at[ROWS])
    obs_loads = [
        pltpu.make_async_copy(obs_hbm.at[m], obs_in.at[m], in_sem.at[m]) for m in range(ROWS)
    ]
    for copy in obs_loads:
        copy.start()
    mem_load.start()

    parts = []
    for part in range(SLOT_BLOCKS):
        lanes = slice(part * LANES, (part + 1) * LANES)
        parts += [values[:, lanes] * CODE, jnp.sqrt(weights[:, lanes]) * ROOT_CODE]
    side_send[...] = coded(jnp.concatenate(parts, axis=0), 1.0)
    write_plan(counts, plan, fits)
    table_copy = pltpu.make_async_copy(plan, table, in_sem.at[ROWS + 1])
    table_copy.start()
    pl.semaphore_wait(barrier, WAYS - 1)

    x, y = me // 8, (me // 2) % 4
    near = x + core * (y - x)
    for step in range(1, 4):
        target = ((x + step * (1 - core)) % 4) * 8 + ((y + step * core) % 4) * 2 + core
        remote(
            side_send, side_recv.at[near], phase_sem.at[14], phase_sem.at[15], target
        ).start()
    pltpu.make_async_copy(side_send, side_recv.at[near], phase_sem.at[15]).start()

    for m in range(ROWS):
        obs_loads[m].wait()

        def widen(block, carry):
            first = pl.multiple_of((m * SLOT_BLOCKS + block) * GROUP, GROUP)
            lanes = pl.ds(pl.multiple_of(block * LANES, LANES), LANES)
            wide[pl.ds(first, GROUP), :] = obs_in[m, :, lanes].astype(jnp.float32)
            return carry

        lax.fori_loop(0, SLOT_BLOCKS, widen, 0)

    table_copy.wait()

    def pack_obs(dest, part):
        for pair in range(PART // 2):
            at = part * PART + 2 * pair
            rows = [
                wide[pl.ds(table[dest, at + j], ROWS, stride=SLOT_BLOCKS * GROUP), :]
                for j in range(2)
            ]
            obs_send[part, dest, pair] = jnp.concatenate(rows, axis=0).astype(jnp.bfloat16)

    def send_obs(part):
        for target in targets:
            pack_obs(target, part)
            remote(
                obs_send.at[part, target], obs_recv.at[part, me],
                phase_sem.at[part], phase_sem.at[16 + part], target,
            ).start()
        pack_obs(me, part)
        pltpu.make_async_copy(
            obs_send.at[part, me], obs_recv.at[part, me], phase_sem.at[16 + part]
        ).start()

    def pack_members(dest, slot):
        row = table[dest, AT_TILE + slot] * 4
        parts = [mem_in[pl.ds(row + f, ROWS, stride=4 * GROUP), :] for f in range(4)]
        mem_send[slot, dest] = coded(jnp.concatenate(parts, axis=0), CODE)

    send_obs(0)

    drain(side_recv, phase_sem.at[15])
    side[...] = side_recv[...].reshape(4 * SIDE_ROWS, LANES).astype(jnp.int32).astype(jnp.float32)
    own_slot = y + core * (4 + x - y)
    for step in range(4):
        for other in range(2):
            dest = ((x + step * core) % 4) * 8 + ((y + step * (1 - core)) % 4) * 2
            dest = dest + (core + other) % 2
            picked = [
                side[pl.ds(table[dest, AT_SIDE + block], 2, stride=4), :] for block in range(CAPACITY)
            ]
            at = step * 2 + other
            row_send[at] = coded(jnp.concatenate(picked, axis=0), 1.0)
            if at:
                remote(
                    row_send.at[at], row_recv.at[own_slot], phase_sem.at[18], phase_sem.at[19], dest
                ).start()
            else:
                pltpu.make_async_copy(
                    row_send.at[at], row_recv.at[own_slot], phase_sem.at[19]
                ).start()

    send_obs(1)

    mem_load.wait()
    for slot in range(HELD):

        def send_members(target, slot=slot):
            remote(
                mem_send.at[slot, target], mem_recv.at[slot, me],
                phase_sem.at[2 + slot], phase_sem.at[5 + slot], target,
            ).start()

        def keep_members(slot=slot):
            pltpu.make_async_copy(
                mem_send.at[slot, me], mem_recv.at[slot, me], phase_sem.at[5 + slot]
            ).start()

        for target in targets:
            pack_members(target, slot)
            if slot < 2:
                send_members(target)
            else:
                pl.when(target % 2 == 0)(functools.partial(send_members, target))
        pack_members(me, slot)
        if slot < 2:
            keep_members()
        else:
            pl.when(core == 0)(keep_members)

    drain(row_recv, phase_sem.at[19])
    rows[...] = row_recv[...].reshape(8 * 2 * CAPACITY, LANES).astype(jnp.int32).astype(jnp.float32)

    lane = lax.broadcasted_iota(jnp.int32, (1, LANES), 1)

    def form_roots(block):
        part, place = block // PART, block % PART
        half = (place % 2) * ROWS
        columns = pl.ds(block * LANES, LANES)
        seen = obs_recv[part, :, place // 2].astype(jnp.float32)[:, half : half + ROWS, :]
        seen = seen.reshape(ENS, LANES)
        mean = jnp.sum(seen, axis=0, keepdims=True) * (1.0 / ENS)
        owner = (table[me, block] & (GROUP - 1)) >> 2
        owner_core = owner & 1
        slot = (1 - owner_core) * ((owner >> 1) & 3) + owner_core * (4 + (owner >> 3))
        pair = rows[pl.ds(slot * 2 * CAPACITY + 2 * block, 2), :]
        live = lane < table[me, AT_COUNT + block]
        scale = jnp.where(live, pair[1:2] * (1.0 / ROOT_CODE), 0.0)
        innov = scale * (pair[0:1] * (1.0 / CODE) - mean)
        scaled = scale * (seen - mean)
        root[0:ENS, columns] = scaled.astype(jnp.bfloat16)
        root[ENS : ENS + 16, columns] = jnp.broadcast_to(innov, (16, LANES)).astype(jnp.bfloat16)
        root_t[block * LANES : (block + 1) * LANES, :] = scaled.T.astype(jnp.bfloat16)

    reach = [
        (0, SLOT_BLOCKS),
        ((CAPACITY - THIRD - CAPACITY // 2) // 2 * 2, CAPACITY),
        (CAPACITY - THIRD, CAPACITY),
    ]
    size = [table[me, AT_BLOCKS + slot] for slot in range(HELD)]
    start = [jnp.int32(0), CAPACITY - size[2] - size[1], CAPACITY - size[2]]
    half = ENS // 2
    eye = (
        lax.broadcasted_iota(jnp.int32, (half, half), 0)
        == lax.broadcasted_iota(jnp.int32, (half, half), 1)
    ).astype(jnp.float32)
    held = range(HELD)
    vecs, bounds, ys = [], [], []

    def sums_of(slot, part):
        low, high = max(reach[slot][0], part * PART), min(reach[slot][1], (part + 1) * PART)
        if low >= high:
            return None
        place = low + lax.broadcasted_iota(jnp.int32, (1, (high - low) * LANES), 1) // LANES
        mine = (place >= start[slot]) & (place < start[slot] + size[slot])
        masked = root[:, low * LANES : high * LANES] * mine.astype(jnp.float32).astype(jnp.bfloat16)
        return jnp.dot(
            masked, root_t[low * LANES : high * LANES, :], preferred_element_type=jnp.float32
        )

    drain(obs_recv.at[0], phase_sem.at[16])
    for block in range(PART):
        form_roots(block)
    early = [sums_of(slot, 0) for slot in held]
    drain(obs_recv.at[1], phase_sem.at[17])
    for block in range(PART, CAPACITY):
        form_roots(block)
    for slot in held:
        sums = sums_of(slot, 1)
        if early[slot] is not None:
            sums = sums + early[slot]
        gram = sums[0:ENS]
        vecs.append(sums[ENS : ENS + 8])
        trace = jnp.sum((gram[:half, :half] + gram[half:, half:]) * eye)
        bound = (ENS - 1.0) + trace
        bounds.append(bound)
        ys.append(centred((ENS - 1.0) / bound, gram * (1.0 / bound), eye))
    zs = middles = [middle_of(y) for y in ys]
    ys = [times(ys[slot], middles[slot], eye) for slot in held]

    def centre_members(slot):
        if slot < 2:
            drain(mem_recv.at[slot], phase_sem.at[5 + slot])
        else:
            pl.when(core == 0)(lambda: drain(mem_recv.at[2], phase_sem.at[7]))
        raw = decoded(mem_recv[slot], CODE)
        fields = [raw[:, f * ROWS : (f + 1) * ROWS, :].reshape(ENS, LANES) for f in range(4)]
        state = jnp.concatenate(fields, axis=1)
        mean = jnp.sum(state, axis=0, keepdims=True) * (1.0 / ENS)
        pert[slot] = (state - mean).astype(jnp.bfloat16)
        return mean

    means = []
    for iteration in range(1, NEWTON):
        if iteration >= 3:
            means.append(centre_members(iteration - 3))
        middles = [middle_of(times(zs[slot], ys[slot], eye)) for slot in held]
        if iteration < NEWTON - 1:
            ys = [times(ys[slot], middles[slot], eye) for slot in held]
        zs = [times(middles[slot], zs[slot], eye) for slot in held]
    weight_t = []
    for slot in held:
        z, bound = zs[slot], bounds[slot]
        shift = row_times(row_times(vecs[slot], z), z)[0:1] * (1.0 / bound)
        factor = jnp.sqrt(jnp.float32(ENS - 1.0)) / jnp.sqrt(bound)
        diagonal = (factor * z[0]) * eye
        full = factor * z[1] + shift
        upper = jnp.concatenate([full[:half, :half] + diagonal, full[:half, half:]], axis=1)
        lower = jnp.concatenate([full[half:, :half], full[half:, half:] + diagonal], axis=1)
        weight_t.append(jnp.concatenate([upper, lower], axis=0).astype(jnp.bfloat16))

    half_ways = WAYS // 2
    for slot in range(HELD):
        if slot == 2:
            means.append(centre_members(2))
        result = jnp.dot(weight_t[slot], pert[slot], preferred_element_type=jnp.float32)
        result = means[slot] + result
        parts = [
            result[:, f * LANES : (f + 1) * LANES].reshape(WAYS, ROWS, LANES) for f in range(4)
        ]
        out_send[slot] = jnp.concatenate(parts, axis=1).astype(jnp.bfloat16)

        def send_result(slot=slot):
            for target in targets:
                remote(
                    out_send.at[slot, target], out_recv.at[slot, me],
                    phase_sem.at[8 + slot], phase_sem.at[11 + slot], target,
                ).start()
            pltpu.make_async_copy(
                out_send.at[slot, me], out_recv.at[slot, me], phase_sem.at[11 + slot]
            ).start()

        if slot < 2:
            send_result()
        else:
            pl.when(core == 0)(send_result)

    sent = pl.ds(0, WAYS - 1)
    for part in range(2):
        drain(obs_send.at[part, sent], phase_sem.at[part])
    drain(side_recv.at[pl.ds(0, 3)], phase_sem.at[14])
    drain(row_send.at[pl.ds(0, 7)], phase_sem.at[18])
    for slot in range(2):
        drain(mem_send.at[slot, sent], phase_sem.at[2 + slot])
        drain(out_send.at[slot, sent], phase_sem.at[8 + slot])
        drain(out_recv.at[slot], phase_sem.at[11 + slot])
    drain(mem_send.at[2, pl.ds(0, half_ways - 1)], phase_sem.at[4])
    pl.when(core == 1)(lambda: drain(mem_send.at[2, 0], phase_sem.at[4]))
    pl.when(core == 0)(lambda: drain(out_send.at[2, sent], phase_sem.at[10]))
    drain(out_recv.at[2, pl.ds(0, half_ways)], phase_sem.at[13])


def exchange_and_analyse(counts, obs_ens, members, values, weights):
    smem = pl.BlockSpec(memory_space=pltpu.SMEM)
    vmem = pl.BlockSpec(memory_space=pltpu.VMEM)
    anywhere = pl.BlockSpec(memory_space=pl.ANY)
    dma = pltpu.SemaphoreType.DMA
    return pl.pallas_call(
        analyse_kernel,
        out_shape=(
            jax.ShapeDtypeStruct((HELD, WAYS, 32, LANES), jnp.bfloat16),
            jax.ShapeDtypeStruct((WAYS, LANES), jnp.int32),
            jax.ShapeDtypeStruct((1, 1), jnp.int32),
        ),
        in_specs=[vmem, anywhere, anywhere, vmem, vmem],
        out_specs=(anywhere, vmem, smem),
        scratch_shapes=[
            pltpu.SMEM((WAYS, LANES), jnp.int32),
            pltpu.VMEM((ROWS, GROUP, SLOT_BLOCKS * LANES), jnp.bfloat16),
            pltpu.VMEM((ROWS * SLOT_BLOCKS * GROUP, LANES), jnp.float32),
            pltpu.VMEM((ROWS * GROUP * 4, LANES), jnp.float32),
            pltpu.VMEM((2, WAYS, PART // 2, 16, LANES), jnp.bfloat16),
            pltpu.VMEM((HELD, WAYS, 32, LANES), jnp.int16),
            pltpu.VMEM((SIDE_ROWS, LANES), jnp.int16),
            pltpu.VMEM((8, 2 * CAPACITY, LANES), jnp.int16),
            pltpu.VMEM((2, WAYS, PART // 2, 16, LANES), jnp.bfloat16),
            pltpu.VMEM((HELD, WAYS, 32, LANES), jnp.int16),
            pltpu.VMEM((4, SIDE_ROWS, LANES), jnp.int16),
            pltpu.VMEM((8, 2 * CAPACITY, LANES), jnp.int16),
            pltpu.VMEM((4 * SIDE_ROWS, LANES), jnp.float32),
            pltpu.VMEM((16 * CAPACITY, LANES), jnp.float32),
            pltpu.VMEM((HELD, WAYS, 32, LANES), jnp.bfloat16),
            pltpu.VMEM((ENS + 16, CAPACITY * LANES), jnp.bfloat16),
            pltpu.VMEM((CAPACITY * LANES, ENS), jnp.bfloat16),
            pltpu.VMEM((HELD, ENS, 4 * LANES), jnp.bfloat16),
            dma((ROWS + 2,)),
            dma((20,)),
        ],
        compiler_params=pltpu.CompilerParams(
            collective_id=0, has_side_effects=True, vmem_limit_bytes=56 << 20
        ),
        name="analyse",
    )(counts, obs_ens, members, values, weights)


def scatter_kernel(table, members, recv_hbm, out_hbm, recv, out, sems):
    loads = [
        pltpu.make_async_copy(members, out, sems.at[0]),
        pltpu.make_async_copy(recv_hbm, recv, sems.at[1]),
    ]
    for copy in loads:
        copy.start()
    for copy in loads:
        copy.wait()

    def place(dest, carry):
        for slot in range(HELD):
            row = table[dest, AT_TILE + slot] * 4

            @pl.when(table[dest, AT_BLOCKS + slot] > 0)
            def _():
                tall = recv[slot, dest].astype(jnp.float32)
                for f in range(4):
                    out[pl.ds(row + f, ROWS, stride=4 * GROUP), :] = tall[f * ROWS : (f + 1) * ROWS]

        return carry

    lax.fori_loop(0, WAYS, place, 0)
    store = pltpu.make_async_copy(out, out_hbm, sems.at[2])
    store.start()
    store.wait()


def scatter(table, members, recv):
    smem = pl.BlockSpec(memory_space=pltpu.SMEM)
    anywhere = pl.BlockSpec(memory_space=pl.ANY)
    return pl.pallas_call(
        scatter_kernel,
        out_shape=jax.ShapeDtypeStruct(members.shape, jnp.float32),
        in_specs=[smem, anywhere, anywhere],
        out_specs=anywhere,
        scratch_shapes=[
            pltpu.VMEM(recv.shape, recv.dtype),
            pltpu.VMEM(members.shape, jnp.float32),
            pltpu.SemaphoreType.DMA((3,)),
        ],
        compiler_params=pltpu.CompilerParams(vmem_limit_bytes=60 << 20),
        name="scatter",
    )(table, members, recv)


def body(members, obs_ens, obs_count, obs_value, obs_weight):
    flat = members.reshape(-1, LANES)
    recv, table, fits = exchange_and_analyse(
        obs_count.reshape(-1, GROUP), obs_ens, flat, obs_value, obs_weight
    )
    result = scatter(table, flat, recv).reshape(members.shape)
    return lax.cond(
        fits[0, 0] > 0,
        lambda result, *_: result,
        lambda _, *inputs: static_body(*inputs),
        result, members, obs_ens, obs_count, obs_value, obs_weight,
    )


def solution(mesh):
    in_specs = (
        P("ens", "bal", None, None),
        P("ens", "bal", None),
        P(),
        P(("bal", "ens"), None),
        P(("bal", "ens"), None),
    )
    out_specs = P("ens", "bal", None, None)
    return jax.shard_map(body, mesh=mesh, in_specs=in_specs, out_specs=out_specs, check_vma=False)
```

```python
import functools

import jax
import jax.numpy as jnp
from jax import lax
from jax.experimental import pallas as pl
from jax.experimental.pallas import tpu as pltpu
from jax.sharding import PartitionSpec as P

NEWTON = 5
MESH = pl.DeviceIdType.MESH
WAYS = 32
GROUP = 128
LANES = 128
SLOT_BLOCKS = 16
HELD = 3
CAPACITY = 24
PART = 12
THIRD = 6
CHUNKS = 4
ROWS = 8
ENS = 256
CODE = 32767.0 / 6.0
ROOT_CODE = 32767.0 / 0.708
SIDE_ROWS = 8 * SLOT_BLOCKS
AT_TILE, AT_BLOCKS, AT_COUNT, AT_SIDE = 32, 36, 64, 96


def solve_weights(gram_matrix, obs_vector):
    highest = lax.Precision.HIGHEST
    ens_size = gram_matrix.shape[0]
    identity = jnp.eye(ens_size, dtype=jnp.float32)
    scale_bound = ens_size - 1.0 + jnp.trace(gram_matrix)
    y_matrix = ((ens_size - 1.0) * identity + gram_matrix) / scale_bound
    z_matrix = identity
    for iteration in range(NEWTON):
        middle = 1.5 * identity - 0.5 * jnp.dot(z_matrix, y_matrix, precision=highest)
        y_matrix = jnp.dot(y_matrix, middle, precision=highest)
        z_matrix = jnp.dot(middle, z_matrix, precision=highest)
    inner_vec = jnp.dot(z_matrix, obs_vector, precision=highest)
    shift_vec = jnp.dot(z_matrix, inner_vec, precision=highest) / scale_bound
    factor = jnp.sqrt(ens_size - 1.0) / jnp.sqrt(scale_bound)
    return (factor * z_matrix + shift_vec[:, None]).astype(jnp.bfloat16)


def unit_weights(gram_matrix, obs_vector):
    return jnp.eye(gram_matrix.shape[0], dtype=jnp.bfloat16)


def tile_weights(operands):
    gram_matrix, obs_vector = operands
    return lax.cond(
        jnp.trace(gram_matrix) > 0.0, solve_weights, unit_weights, gram_matrix, obs_vector
    )


def tile_gram(obs_rows, centre_row, weight_row, innov_row, live_count, ens_size):
    zero_sums = (jnp.zeros((ens_size, ens_size), jnp.float32), jnp.zeros((ens_size,), jnp.float32))
    block_count = (live_count + 127) // 128

    def add_block(index_block, totals):
        first_slot = index_block * 128
        obs_piece = lax.dynamic_slice_in_dim(obs_rows, first_slot, 128, 1)
        centre_piece = lax.dynamic_slice_in_dim(centre_row, first_slot, 128, 0)
        weight_piece = lax.dynamic_slice_in_dim(weight_row, first_slot, 128, 0)
        rhs_piece = lax.dynamic_slice_in_dim(innov_row, first_slot, 128, 0)
        root_piece = (
            weight_piece[None, :] * (obs_piece.astype(jnp.float32) - centre_piece[None, :])
        ).astype(jnp.bfloat16)
        gram_piece = lax.dot_general(
            root_piece, root_piece, (((1,), (1,)), ((), ())), preferred_element_type=jnp.float32
        )
        vector_piece = jnp.dot(root_piece, rhs_piece, preferred_element_type=jnp.float32)
        return (totals[0] + gram_piece, totals[1] + vector_piece)

    return lax.fori_loop(0, block_count, add_block, zero_sums)


def static_body(members, obs_ens, obs_count, obs_value, obs_weight):
    member_block, tile_block, nfield, columns = members.shape
    ens_ways = lax.axis_size("ens")
    ens_size = member_block * ens_ways
    per_device, slot_count = obs_value.shape
    state_width = nfield * columns
    first_tile = (lax.axis_index("bal") * ens_ways + lax.axis_index("ens")) * per_device
    ensemble = lax.all_to_all(members, "ens", split_axis=1, concat_axis=0, tiled=True)
    observed = lax.all_to_all(obs_ens, "ens", split_axis=1, concat_axis=0, tiled=True)
    mean_tiles = jnp.mean(ensemble, axis=0)
    pert_tiles = (ensemble - mean_tiles[None]).astype(jnp.bfloat16)
    pert_tiles = pert_tiles.reshape(ens_size, per_device, state_width)
    mean_tiles = mean_tiles.reshape(per_device, state_width)
    obs_mean = jnp.sum(observed, axis=0, dtype=jnp.float32) / ens_size
    counts = lax.dynamic_slice_in_dim(obs_count, first_tile, per_device, 0)
    positions = lax.broadcasted_iota(jnp.int32, (per_device, slot_count), 1)
    live_mask = positions < counts[:, None]
    innovation = jnp.where(live_mask, obs_value - obs_mean, 0.0)
    root_weight = jnp.sqrt(obs_weight)
    masked_weight = jnp.where(live_mask, root_weight, 0.0)
    scaled_innov = (root_weight * innovation).astype(jnp.bfloat16)
    grams = []
    vectors = []
    for tile_index in range(per_device):
        gram_one, vector_one = tile_gram(
            observed[:, tile_index],
            obs_mean[tile_index],
            masked_weight[tile_index],
            scaled_innov[tile_index],
            counts[tile_index],
            ens_size,
        )
        grams.append(gram_one)
        vectors.append(vector_one)
    gram_tiles = jnp.stack(grams)
    vector_tiles = jnp.stack(vectors)
    weights = lax.map(tile_weights, (gram_tiles, vector_tiles))
    result = mean_tiles[None] + jnp.einsum(
        "tjk,jtf->ktf", weights, pert_tiles, preferred_element_type=jnp.float32
    )
    result = result.reshape(ens_size, per_device, nfield, columns)
    return lax.all_to_all(result, "ens", split_axis=0, concat_axis=1, tiled=True)


def write_plan(counts, table, fits):
    lane = lax.broadcasted_iota(jnp.int32, (8, LANES), 1)
    device = lane % WAYS
    tiles = counts[...]
    key = tiles * GROUP + lane
    rank = jnp.zeros_like(key)
    for step in range(1, GROUP):
        rank += (pltpu.roll(key, step, 1) > key).astype(jnp.int32)
    first, second, third = jnp.zeros_like(key), jnp.zeros_like(key), jnp.zeros_like(key)
    third_rank = jnp.where(device % 2 == 0, 79 - device // 2, -1)
    for step in range(GROUP):
        there = pltpu.roll(rank, step, 1) if step else rank
        value = pltpu.roll(key, step, 1) if step else key
        first = jnp.where(there == device, value, first)
        second = jnp.where(there == 2 * WAYS - 1 - device, value, second)
        third = jnp.where(there == third_rank, value, third)

    def blocks_of(array):
        return ((array >> 7) + LANES - 1) >> 7

    pair = (blocks_of(first) + blocks_of(second)) * WAYS + device
    pair_rank = jnp.zeros_like(pair)
    for step in range(1, WAYS):
        pair_rank += (pltpu.roll(pair, step, 1) > pair).astype(jnp.int32)
    wanted = device // 2 + jnp.where(device % 2 == 0, WAYS // 2, 0)
    one, two = jnp.zeros_like(key), jnp.zeros_like(key)
    for step in range(WAYS):
        hit = (pltpu.roll(pair_rank, step, 1) if step else pair_rank) == wanted
        one = jnp.where(hit, pltpu.roll(first, step, 1) if step else first, one)
        two = jnp.where(hit, pltpu.roll(second, step, 1) if step else second, two)
    load = blocks_of(one) + blocks_of(two) + blocks_of(third)
    over = (load > CAPACITY) | (blocks_of(third) > THIRD) | ((rank >= 80) & (tiles > 0))
    fits[0, 0] = 1 - jnp.max(over.astype(jnp.int32))

    row = lax.broadcasted_iota(jnp.int32, (8, LANES), 0)
    wide_lane = lax.broadcasted_iota(jnp.int32, (WAYS, LANES), 1)
    wide_row = lax.broadcasted_iota(jnp.int32, (WAYS, LANES), 0)

    def column(array):
        mine = jnp.sum(jnp.where(row == lax.axis_index("bal"), array, 0), axis=0, keepdims=True)
        mine = jnp.broadcast_to(mine, (WAYS, LANES))
        return jnp.sum(jnp.where(wide_lane == wide_row, mine, 0), axis=1, keepdims=True)

    keys = [column(array) for array in (one, two, third)]
    size = [blocks_of(array) for array in keys]
    start = [jnp.zeros_like(size[0]), CAPACITY - size[2] - size[1], CAPACITY - size[2]]

    def table_of(place):
        at_key, at_block = jnp.broadcast_to(keys[0], place.shape), jnp.full_like(place, -1)
        for slot in range(HELD):
            here = (place >= start[slot]) & (place < start[slot] + size[slot])
            at_key = jnp.where(here, keys[slot], at_key)
            at_block = jnp.where(here, place - start[slot], at_block)
        return at_key, at_block

    at_key, at_block = table_of(wide_lane)
    out = jnp.maximum(at_block, 0) * GROUP + (at_key & (GROUP - 1))
    at_key, at_block = table_of(wide_lane - AT_COUNT)
    left = jnp.where(at_block >= 0, (at_key >> 7) - at_block * LANES, 0)
    out = jnp.where(wide_lane >= AT_COUNT, left, out)
    at_key, at_block = table_of(wide_lane - AT_SIDE)
    tile = at_key & (GROUP - 1)
    near = jnp.where(lax.axis_index("ens") % 2 == 0, tile >> 5, (tile >> 3) & 3)
    side_row = near * SIDE_ROWS + jnp.maximum(at_block, 0) * 8 + (tile & 3)
    out = jnp.where(wide_lane >= AT_SIDE, side_row, out)
    for slot in range(HELD):
        out = jnp.where(wide_lane == AT_TILE + slot, keys[slot] & (GROUP - 1), out)
        out = jnp.where(wide_lane == AT_BLOCKS + slot, size[slot], out)
    table[0:WAYS, :] = out
    found = jnp.zeros_like(wide_lane)
    for slot in range(HELD):
        hit = (keys[slot] & (GROUP - 1) == wide_lane) & (size[slot] > 0)
        found += jnp.where(hit, slot * WAYS + wide_row + 1, 0)
    table[WAYS : WAYS + 8, :] = jnp.broadcast_to(jnp.sum(found, axis=0, keepdims=True), (8, LANES))


def displacements():
    every = [(dx, dy, dc) for dx in range(4) for dy in range(4) for dc in range(2)][1:]
    return sorted(every, key=lambda d: -(min(d[0], 4 - d[0]) + min(d[1], 4 - d[1])))


def shifted(me, step, sign=1):
    x, y, core = me // 8, (me // 2) % 4, me % 2
    dx, dy = (step[0], step[1]) if sign > 0 else ((4 - step[0]) % 4, (4 - step[1]) % 4)
    return (((x + dx) % 4) * 4 + (y + dy) % 4) * 2 + (core + step[2]) % 2


def centred(c, matrix, eye):
    half = ENS // 2
    top, low = matrix[:half, :half], matrix[half:, half:]
    mean = jnp.sum((top + low) * eye) * (1.0 / ENS)
    upper = jnp.concatenate([top - mean * eye, matrix[:half, half:]], axis=1)
    lower = jnp.concatenate([matrix[half:, :half], low - mean * eye], axis=1)
    deviation = jnp.concatenate([upper, lower], axis=0)
    return c + mean, deviation, deviation.astype(jnp.bfloat16)


def times(left, right, eye):
    cross = left[0] * right[1] + right[0] * left[1]
    inner = jnp.dot(left[2], right[2], preferred_element_type=jnp.float32)
    return centred(left[0] * right[0], cross + inner, eye)


def middle_of(product):
    return 1.5 - 0.5 * product[0], -0.5 * product[1], product[2] * jnp.bfloat16(-0.5)


def row_times(row, z):
    high = row.astype(jnp.bfloat16)
    low = (row - high.astype(jnp.float32)).astype(jnp.bfloat16)
    rest = (z[1] - z[2].astype(jnp.float32)).astype(jnp.bfloat16)
    out = jnp.dot(high, z[2], preferred_element_type=jnp.float32)
    out = out + jnp.dot(low, z[2], preferred_element_type=jnp.float32)
    out = out + jnp.dot(high, rest, preferred_element_type=jnp.float32)
    return z[0] * row + out


def coded(array, scale):
    return jnp.round(array * scale).astype(jnp.int32).astype(jnp.int16)


def decoded(array, scale):
    return array.astype(jnp.int32).astype(jnp.float32) * (1.0 / scale)


def analyse_kernel(
    counts, obs_hbm, mem_hbm, values, weights,
    out_recv, plan, fits,
    table, obs_in, wide, mem_in, obs_send, mem_send, side_send, row_send, obs_recv, mem_recv,
    side_recv, row_recv, side, rows, out_send, root, root_t, pert,
    in_sem, phase_sem,
):
    me = lax.axis_index("ens")
    core = me % 2
    steps = displacements()
    targets = [shifted(me, step) for step in steps]

    def remote(src, dst, ssem, rsem, target):
        return pltpu.make_async_remote_copy(
            src_ref=src, dst_ref=dst, send_sem=ssem, recv_sem=rsem,
            device_id={"ens": target}, device_id_type=MESH,
        )

    barrier = pltpu.get_barrier_semaphore()
    for target in targets:
        pl.semaphore_signal(barrier, inc=1, device_id={"ens": target}, device_id_type=MESH)
    def drain(ref, sem):
        pltpu.make_async_copy(ref, ref, sem).wait()

    mem_load = pltpu.make_async_copy(mem_hbm, mem_in, in_sem.at[ROWS])
    obs_loads = [
        pltpu.make_async_copy(obs_hbm.at[m], obs_in.at[m], in_sem.at[m]) for m in range(ROWS)
    ]
    for copy in obs_loads:
        copy.start()
    mem_load.start()

    parts = []
    for part in range(SLOT_BLOCKS):
        lanes = slice(part * LANES, (part + 1) * LANES)
        parts += [values[:, lanes] * CODE, jnp.sqrt(weights[:, lanes]) * ROOT_CODE]
    side_send[...] = coded(jnp.concatenate(parts, axis=0), 1.0)
    write_plan(counts, plan, fits)
    table_copy = pltpu.make_async_copy(plan, table, in_sem.at[ROWS + 1])
    table_copy.start()
    for m in range(ROWS):
        obs_loads[m].wait()

        def widen(block, carry):
            first = pl.multiple_of((m * SLOT_BLOCKS + block) * GROUP, GROUP)
            lanes = pl.ds(pl.multiple_of(block * LANES, LANES), LANES)
            wide[pl.ds(first, GROUP), :] = obs_in[m, :, lanes].astype(jnp.float32)
            return carry

        lax.fori_loop(0, SLOT_BLOCKS, widen, 0)

    pl.semaphore_wait(barrier, WAYS - 1)

    x, y = me // 8, (me // 2) % 4
    near = x + core * (y - x)
    for step in range(1, 4):
        target = ((x + step * (1 - core)) % 4) * 8 + ((y + step * core) % 4) * 2 + core
        remote(
            side_send, side_recv.at[near], phase_sem.at[14], phase_sem.at[15], target
        ).start()
    pltpu.make_async_copy(side_send, side_recv.at[near], phase_sem.at[15]).start()

    table_copy.wait()

    def pack_obs(dest, part):
        for pair in range(PART // 2):
            at = part * PART + 2 * pair
            rows = [
                wide[pl.ds(table[dest, at + j], ROWS, stride=SLOT_BLOCKS * GROUP), :]
                for j in range(2)
            ]
            obs_send[part, dest, pair] = jnp.concatenate(rows, axis=0).astype(jnp.bfloat16)

    def send_obs(part):
        for target in targets:
            pack_obs(target, part)
            remote(
                obs_send.at[part, target], obs_recv.at[part, me],
                phase_sem.at[part], phase_sem.at[16 + part], target,
            ).start()
        pack_obs(me, part)
        pltpu.make_async_copy(
            obs_send.at[part, me], obs_recv.at[part, me], phase_sem.at[16 + part]
        ).start()

    def pack_members(dest, slot):
        row = table[dest, AT_TILE + slot] * 4
        parts = [mem_in[pl.ds(row + f, ROWS, stride=4 * GROUP), :] for f in range(4)]
        mem_send[slot, dest] = coded(jnp.concatenate(parts, axis=0), CODE)

    send_obs(0)

    drain(side_recv, phase_sem.at[15])
    side[...] = side_recv[...].reshape(4 * SIDE_ROWS, LANES).astype(jnp.int32).astype(jnp.float32)
    own_slot = y + core * (4 + x - y)
    for step in range(4):
        for other in range(2):
            dest = ((x + step * core) % 4) * 8 + ((y + step * (1 - core)) % 4) * 2
            dest = dest + (core + other) % 2
            picked = [
                side[pl.ds(table[dest, AT_SIDE + block], 2, stride=4), :] for block in range(CAPACITY)
            ]
            at = step * 2 + other
            row_send[at] = coded(jnp.concatenate(picked, axis=0), 1.0)
            if at:
                remote(
                    row_send.at[at], row_recv.at[own_slot], phase_sem.at[18], phase_sem.at[19], dest
                ).start()
            else:
                pltpu.make_async_copy(
                    row_send.at[at], row_recv.at[own_slot], phase_sem.at[19]
                ).start()

    send_obs(1)

    mem_load.wait()
    for slot in range(HELD):

        def send_members(target, slot=slot):
            remote(
                mem_send.at[slot, target], mem_recv.at[slot, me],
                phase_sem.at[2 + slot], phase_sem.at[5 + slot], target,
            ).start()

        def keep_members(slot=slot):
            pltpu.make_async_copy(
                mem_send.at[slot, me], mem_recv.at[slot, me], phase_sem.at[5 + slot]
            ).start()

        for target in targets:
            pack_members(target, slot)
            if slot < 2:
                send_members(target)
            else:
                pl.when(target % 2 == 0)(functools.partial(send_members, target))
        pack_members(me, slot)
        if slot < 2:
            keep_members()
        else:
            pl.when(core == 0)(keep_members)

    drain(row_recv, phase_sem.at[19])
    rows[...] = row_recv[...].reshape(8 * 2 * CAPACITY, LANES).astype(jnp.int32).astype(jnp.float32)

    lane = lax.broadcasted_iota(jnp.int32, (1, LANES), 1)

    def form_roots(block):
        part, place = block // PART, block % PART
        half = (place % 2) * ROWS
        columns = pl.ds(block * LANES, LANES)
        seen = obs_recv[part, :, place // 2].astype(jnp.float32)[:, half : half + ROWS, :]
        seen = seen.reshape(ENS, LANES)
        mean = jnp.sum(seen, axis=0, keepdims=True) * (1.0 / ENS)
        owner = (table[me, block] & (GROUP - 1)) >> 2
        owner_core = owner & 1
        slot = (1 - owner_core) * ((owner >> 1) & 3) + owner_core * (4 + (owner >> 3))
        pair = rows[pl.ds(slot * 2 * CAPACITY + 2 * block, 2), :]
        live = lane < table[me, AT_COUNT + block]
        scale = jnp.where(live, pair[1:2] * (1.0 / ROOT_CODE), 0.0)
        innov = scale * (pair[0:1] * (1.0 / CODE) - mean)
        scaled = scale * (seen - mean)
        root[0:ENS, columns] = scaled.astype(jnp.bfloat16)
        root[ENS : ENS + 16, columns] = jnp.broadcast_to(innov, (16, LANES)).astype(jnp.bfloat16)
        root_t[block * LANES : (block + 1) * LANES, :] = scaled.T.astype(jnp.bfloat16)

    reach = [
        (0, SLOT_BLOCKS),
        ((CAPACITY - THIRD - CAPACITY // 2) // 2 * 2, CAPACITY),
        (CAPACITY - THIRD, CAPACITY),
    ]
    size = [table[me, AT_BLOCKS + slot] for slot in range(HELD)]
    start = [jnp.int32(0), CAPACITY - size[2] - size[1], CAPACITY - size[2]]
    half = ENS // 2
    eye = (
        lax.broadcasted_iota(jnp.int32, (half, half), 0)
        == lax.broadcasted_iota(jnp.int32, (half, half), 1)
    ).astype(jnp.float32)
    held = range(HELD)

    def sums_of(slot, part):
        low, high = max(reach[slot][0], part * PART), min(reach[slot][1], (part + 1) * PART)
        if low >= high:
            return None
        place = low + lax.broadcasted_iota(jnp.int32, (1, (high - low) * LANES), 1) // LANES
        mine = (place >= start[slot]) & (place < start[slot] + size[slot])
        masked = root[:, low * LANES : high * LANES] * mine.astype(jnp.float32).astype(jnp.bfloat16)
        return jnp.dot(
            masked, root_t[low * LANES : high * LANES, :], preferred_element_type=jnp.float32
        )

    drain(obs_recv.at[0], phase_sem.at[16])
    for block in range(PART):
        form_roots(block)
    early = [sums_of(slot, 0) for slot in held]
    drain(obs_recv.at[1], phase_sem.at[17])
    for block in range(PART, CAPACITY):
        form_roots(block)

    def centre_members(slot):
        if slot < 2:
            drain(mem_recv.at[slot], phase_sem.at[5 + slot])
        else:
            pl.when(core == 0)(lambda: drain(mem_recv.at[2], phase_sem.at[7]))
        raw = decoded(mem_recv[slot], CODE)
        fields = [raw[:, f * ROWS : (f + 1) * ROWS, :].reshape(ENS, LANES) for f in range(4)]
        state = jnp.concatenate(fields, axis=1)
        mean = jnp.sum(state, axis=0, keepdims=True) * (1.0 / ENS)
        pert[slot] = (state - mean).astype(jnp.bfloat16)
        return mean

    def weights_of(slots):
        vecs, bounds, ys, means = [], [], [], []
        for slot in slots:
            sums = sums_of(slot, 1)
            if early[slot] is not None:
                sums = sums + early[slot]
            gram = sums[0:ENS]
            vecs.append(sums[ENS : ENS + 8])
            trace = jnp.sum((gram[:half, :half] + gram[half:, half:]) * eye)
            bound = (ENS - 1.0) + trace
            bounds.append(bound)
            ys.append(centred((ENS - 1.0) / bound, gram * (1.0 / bound), eye))
        zs = middles = [middle_of(y) for y in ys]
        ys = [times(y, middle, eye) for y, middle in zip(ys, middles)]
        for iteration in range(1, NEWTON):
            if NEWTON - iteration <= len(slots):
                means.append(centre_members(slots[len(means)]))
            middles = [middle_of(times(z, y, eye)) for z, y in zip(zs, ys)]
            if iteration < NEWTON - 1:
                ys = [times(y, middle, eye) for y, middle in zip(ys, middles)]
            zs = [times(middle, z, eye) for middle, z in zip(middles, zs)]
        out = []
        for z, bound, vec in zip(zs, bounds, vecs):
            shift = row_times(row_times(vec, z), z)[0:1] * (1.0 / bound)
            factor = jnp.sqrt(jnp.float32(ENS - 1.0)) / jnp.sqrt(bound)
            diagonal = (factor * z[0]) * eye
            full = factor * z[1] + shift
            upper = jnp.concatenate([full[:half, :half] + diagonal, full[:half, half:]], axis=1)
            lower = jnp.concatenate([full[half:, :half], full[half:, half:] + diagonal], axis=1)
            out.append(jnp.concatenate([upper, lower], axis=0).astype(jnp.bfloat16))
        return out, means

    half_ways = WAYS // 2
    for slots in ((0, 1), (2,)):
        for slot, weight_t, mean in zip(slots, *weights_of(slots)):
            result = mean + jnp.dot(weight_t, pert[slot], preferred_element_type=jnp.float32)
            parts = [
                result[:, f * LANES : (f + 1) * LANES].reshape(WAYS, ROWS, LANES) for f in range(4)
            ]
            out_send[slot] = jnp.concatenate(parts, axis=1).astype(jnp.bfloat16)

            def send_result(slot=slot):
                for target in targets:
                    remote(
                        out_send.at[slot, target], out_recv.at[slot, me],
                        phase_sem.at[8 + slot], phase_sem.at[11 + slot], target,
                    ).start()
                pltpu.make_async_copy(
                    out_send.at[slot, me], out_recv.at[slot, me], phase_sem.at[11 + slot]
                ).start()

            if slot < 2:
                send_result()
            else:
                pl.when(core == 0)(send_result)

    sent = pl.ds(0, WAYS - 1)
    for part in range(2):
        drain(obs_send.at[part, sent], phase_sem.at[part])
    drain(side_recv.at[pl.ds(0, 3)], phase_sem.at[14])
    drain(row_send.at[pl.ds(0, 7)], phase_sem.at[18])
    for slot in range(2):
        drain(mem_send.at[slot, sent], phase_sem.at[2 + slot])
        drain(out_send.at[slot, sent], phase_sem.at[8 + slot])
        drain(out_recv.at[slot], phase_sem.at[11 + slot])
    drain(mem_send.at[2, pl.ds(0, half_ways - 1)], phase_sem.at[4])
    pl.when(core == 1)(lambda: drain(mem_send.at[2, 0], phase_sem.at[4]))
    pl.when(core == 0)(lambda: drain(out_send.at[2, sent], phase_sem.at[10]))
    drain(out_recv.at[2, pl.ds(0, half_ways)], phase_sem.at[13])


def exchange_and_analyse(counts, obs_ens, members, values, weights):
    smem = pl.BlockSpec(memory_space=pltpu.SMEM)
    vmem = pl.BlockSpec(memory_space=pltpu.VMEM)
    anywhere = pl.BlockSpec(memory_space=pl.ANY)
    dma = pltpu.SemaphoreType.DMA
    return pl.pallas_call(
        analyse_kernel,
        out_shape=(
            jax.ShapeDtypeStruct((HELD, WAYS, 32, LANES), jnp.bfloat16),
            jax.ShapeDtypeStruct((WAYS + 8, LANES), jnp.int32),
            jax.ShapeDtypeStruct((1, 1), jnp.int32),
        ),
        in_specs=[vmem, anywhere, anywhere, vmem, vmem],
        out_specs=(anywhere, vmem, smem),
        scratch_shapes=[
            pltpu.SMEM((WAYS + 8, LANES), jnp.int32),
            pltpu.VMEM((ROWS, GROUP, SLOT_BLOCKS * LANES), jnp.bfloat16),
            pltpu.VMEM((ROWS * SLOT_BLOCKS * GROUP, LANES), jnp.float32),
            pltpu.VMEM((ROWS * GROUP * 4, LANES), jnp.float32),
            pltpu.VMEM((2, WAYS, PART // 2, 16, LANES), jnp.bfloat16),
            pltpu.VMEM((HELD, WAYS, 32, LANES), jnp.int16),
            pltpu.VMEM((SIDE_ROWS, LANES), jnp.int16),
            pltpu.VMEM((8, 2 * CAPACITY, LANES), jnp.int16),
            pltpu.VMEM((2, WAYS, PART // 2, 16, LANES), jnp.bfloat16),
            pltpu.VMEM((HELD, WAYS, 32, LANES), jnp.int16),
            pltpu.VMEM((4, SIDE_ROWS, LANES), jnp.int16),
            pltpu.VMEM((8, 2 * CAPACITY, LANES), jnp.int16),
            pltpu.VMEM((4 * SIDE_ROWS, LANES), jnp.float32),
            pltpu.VMEM((16 * CAPACITY, LANES), jnp.float32),
            pltpu.VMEM((HELD, WAYS, 32, LANES), jnp.bfloat16),
            pltpu.VMEM((ENS + 16, CAPACITY * LANES), jnp.bfloat16),
            pltpu.VMEM((CAPACITY * LANES, ENS), jnp.bfloat16),
            pltpu.VMEM((HELD, ENS, 4 * LANES), jnp.bfloat16),
            dma((ROWS + 2,)),
            dma((20,)),
        ],
        compiler_params=pltpu.CompilerParams(
            collective_id=0, has_side_effects=True, vmem_limit_bytes=56 << 20
        ),
        name="analyse",
    )(counts, obs_ens, members, values, weights)


def scatter_kernel(table, members, recv_hbm, out_hbm, recv, out, sems):
    width = 4 * GROUP // CHUNKS
    recv_load = pltpu.make_async_copy(recv_hbm, recv, sems.at[0])
    recv_load.start()

    members = members.reshape(ROWS, 4 * GROUP, LANES)
    out_hbm = out_hbm.reshape(ROWS, 4 * GROUP, LANES)

    def rows(chunk):
        return pl.ds(chunk * width, width)

    loads = [
        pltpu.make_async_copy(members.at[:, rows(c)], out.at[c], sems.at[1 + c])
        for c in range(CHUNKS)
    ]
    stores = [
        pltpu.make_async_copy(out.at[c], out_hbm.at[:, rows(c)], sems.at[1 + CHUNKS + c])
        for c in range(CHUNKS)
    ]
    for copy in loads:
        copy.start()
    recv_load.wait()
    for c in range(CHUNKS):
        loads[c].wait()
        flat = out.at[c].reshape(ROWS * width, LANES)

        def place(index, carry):
            at = table[WAYS, c * (GROUP // CHUNKS) + index]

            @pl.when(at > 0)
            def _():
                tall = recv[at - 1].astype(jnp.float32)
                for f in range(4):
                    flat[pl.ds(index * 4 + f, ROWS, stride=width), :] = tall[f * ROWS : (f + 1) * ROWS]

            return carry

        lax.fori_loop(0, GROUP // CHUNKS, place, 0, unroll=4)
        stores[c].start()
    for copy in stores:
        copy.wait()


def scatter(table, members, recv):
    smem = pl.BlockSpec(memory_space=pltpu.SMEM)
    anywhere = pl.BlockSpec(memory_space=pl.ANY)
    return pl.pallas_call(
        scatter_kernel,
        out_shape=jax.ShapeDtypeStruct(members.shape, jnp.float32),
        in_specs=[smem, anywhere, anywhere],
        out_specs=anywhere,
        scratch_shapes=[
            pltpu.VMEM(recv.shape, recv.dtype),
            pltpu.VMEM((CHUNKS, ROWS, 4 * GROUP // CHUNKS, LANES), jnp.float32),
            pltpu.SemaphoreType.DMA((1 + 2 * CHUNKS,)),
        ],
        compiler_params=pltpu.CompilerParams(vmem_limit_bytes=60 << 20),
        name="scatter",
    )(table, members, recv)


def body(members, obs_ens, obs_count, obs_value, obs_weight):
    flat = members.reshape(-1, LANES)
    recv, table, fits = exchange_and_analyse(
        obs_count.reshape(-1, GROUP), obs_ens, flat, obs_value, obs_weight
    )
    recv = recv.reshape(HELD * WAYS, 32, LANES)
    result = scatter(table, flat, recv).reshape(members.shape)
    return lax.cond(
        fits[0, 0] > 0,
        lambda result, *_: result,
        lambda _, *inputs: static_body(*inputs),
        result, members, obs_ens, obs_count, obs_value, obs_weight,
    )


def solution(mesh):
    in_specs = (
        P("ens", "bal", None, None),
        P("ens", "bal", None),
        P(),
        P(("bal", "ens"), None),
        P(("bal", "ens"), None),
    )
    out_specs = P("ens", "bal", None, None)
    return jax.shard_map(body, mesh=mesh, in_specs=in_specs, out_specs=out_specs, check_vma=False)
```

```python
import functools

import jax
import jax.numpy as jnp
from jax import lax
from jax.experimental import pallas as pl
from jax.experimental.pallas import tpu as pltpu
from jax.sharding import PartitionSpec as P

NEWTON = 5
MESH = pl.DeviceIdType.MESH
WAYS = 32
GROUP = 128
LANES = 128
SLOT_BLOCKS = 16
HELD = 3
CAPACITY = 24
PART = 12
THIRD = 6
CHUNKS = 4
ROWS = 8
ENS = 256
CODE = 32767.0 / 6.0
ROOT_CODE = 32767.0 / 0.708
SIDE_ROWS = 8 * SLOT_BLOCKS
AT_TILE, AT_BLOCKS, AT_COUNT, AT_SIDE = 32, 36, 64, 96


def solve_weights(gram_matrix, obs_vector):
    highest = lax.Precision.HIGHEST
    ens_size = gram_matrix.shape[0]
    identity = jnp.eye(ens_size, dtype=jnp.float32)
    scale_bound = ens_size - 1.0 + jnp.trace(gram_matrix)
    y_matrix = ((ens_size - 1.0) * identity + gram_matrix) / scale_bound
    z_matrix = identity
    for iteration in range(NEWTON):
        middle = 1.5 * identity - 0.5 * jnp.dot(z_matrix, y_matrix, precision=highest)
        y_matrix = jnp.dot(y_matrix, middle, precision=highest)
        z_matrix = jnp.dot(middle, z_matrix, precision=highest)
    inner_vec = jnp.dot(z_matrix, obs_vector, precision=highest)
    shift_vec = jnp.dot(z_matrix, inner_vec, precision=highest) / scale_bound
    factor = jnp.sqrt(ens_size - 1.0) / jnp.sqrt(scale_bound)
    return (factor * z_matrix + shift_vec[:, None]).astype(jnp.bfloat16)


def unit_weights(gram_matrix, obs_vector):
    return jnp.eye(gram_matrix.shape[0], dtype=jnp.bfloat16)


def tile_weights(operands):
    gram_matrix, obs_vector = operands
    return lax.cond(
        jnp.trace(gram_matrix) > 0.0, solve_weights, unit_weights, gram_matrix, obs_vector
    )


def tile_gram(obs_rows, centre_row, weight_row, innov_row, live_count, ens_size):
    zero_sums = (jnp.zeros((ens_size, ens_size), jnp.float32), jnp.zeros((ens_size,), jnp.float32))
    block_count = (live_count + 127) // 128

    def add_block(index_block, totals):
        first_slot = index_block * 128
        obs_piece = lax.dynamic_slice_in_dim(obs_rows, first_slot, 128, 1)
        centre_piece = lax.dynamic_slice_in_dim(centre_row, first_slot, 128, 0)
        weight_piece = lax.dynamic_slice_in_dim(weight_row, first_slot, 128, 0)
        rhs_piece = lax.dynamic_slice_in_dim(innov_row, first_slot, 128, 0)
        root_piece = (
            weight_piece[None, :] * (obs_piece.astype(jnp.float32) - centre_piece[None, :])
        ).astype(jnp.bfloat16)
        gram_piece = lax.dot_general(
            root_piece, root_piece, (((1,), (1,)), ((), ())), preferred_element_type=jnp.float32
        )
        vector_piece = jnp.dot(root_piece, rhs_piece, preferred_element_type=jnp.float32)
        return (totals[0] + gram_piece, totals[1] + vector_piece)

    return lax.fori_loop(0, block_count, add_block, zero_sums)


def static_body(members, obs_ens, obs_count, obs_value, obs_weight):
    member_block, tile_block, nfield, columns = members.shape
    ens_ways = lax.axis_size("ens")
    ens_size = member_block * ens_ways
    per_device, slot_count = obs_value.shape
    state_width = nfield * columns
    first_tile = (lax.axis_index("bal") * ens_ways + lax.axis_index("ens")) * per_device
    ensemble = lax.all_to_all(members, "ens", split_axis=1, concat_axis=0, tiled=True)
    observed = lax.all_to_all(obs_ens, "ens", split_axis=1, concat_axis=0, tiled=True)
    mean_tiles = jnp.mean(ensemble, axis=0)
    pert_tiles = (ensemble - mean_tiles[None]).astype(jnp.bfloat16)
    pert_tiles = pert_tiles.reshape(ens_size, per_device, state_width)
    mean_tiles = mean_tiles.reshape(per_device, state_width)
    obs_mean = jnp.sum(observed, axis=0, dtype=jnp.float32) / ens_size
    counts = lax.dynamic_slice_in_dim(obs_count, first_tile, per_device, 0)
    positions = lax.broadcasted_iota(jnp.int32, (per_device, slot_count), 1)
    live_mask = positions < counts[:, None]
    innovation = jnp.where(live_mask, obs_value - obs_mean, 0.0)
    root_weight = jnp.sqrt(obs_weight)
    masked_weight = jnp.where(live_mask, root_weight, 0.0)
    scaled_innov = (root_weight * innovation).astype(jnp.bfloat16)
    grams = []
    vectors = []
    for tile_index in range(per_device):
        gram_one, vector_one = tile_gram(
            observed[:, tile_index],
            obs_mean[tile_index],
            masked_weight[tile_index],
            scaled_innov[tile_index],
            counts[tile_index],
            ens_size,
        )
        grams.append(gram_one)
        vectors.append(vector_one)
    gram_tiles = jnp.stack(grams)
    vector_tiles = jnp.stack(vectors)
    weights = lax.map(tile_weights, (gram_tiles, vector_tiles))
    result = mean_tiles[None] + jnp.einsum(
        "tjk,jtf->ktf", weights, pert_tiles, preferred_element_type=jnp.float32
    )
    result = result.reshape(ens_size, per_device, nfield, columns)
    return lax.all_to_all(result, "ens", split_axis=0, concat_axis=1, tiled=True)


def write_plan(counts, table):
    lane = lax.broadcasted_iota(jnp.int32, (8, LANES), 1)
    device = lane % WAYS
    tiles = counts[...]
    key = tiles * GROUP + lane
    rank = jnp.zeros_like(key)
    for step in range(1, GROUP):
        rank += (pltpu.roll(key, step, 1) > key).astype(jnp.int32)
    first, second, third = jnp.zeros_like(key), jnp.zeros_like(key), jnp.zeros_like(key)
    third_rank = jnp.where(device % 2 == 0, 79 - device // 2, -1)
    for step in range(GROUP):
        there = pltpu.roll(rank, step, 1) if step else rank
        value = pltpu.roll(key, step, 1) if step else key
        first = jnp.where(there == device, value, first)
        second = jnp.where(there == 2 * WAYS - 1 - device, value, second)
        third = jnp.where(there == third_rank, value, third)

    def blocks_of(array):
        return ((array >> 7) + LANES - 1) >> 7

    pair = (blocks_of(first) + blocks_of(second)) * WAYS + device
    pair_rank = jnp.zeros_like(pair)
    for step in range(1, WAYS):
        pair_rank += (pltpu.roll(pair, step, 1) > pair).astype(jnp.int32)
    wanted = device // 2 + jnp.where(device % 2 == 0, WAYS // 2, 0)
    one, two = jnp.zeros_like(key), jnp.zeros_like(key)
    for step in range(WAYS):
        hit = (pltpu.roll(pair_rank, step, 1) if step else pair_rank) == wanted
        one = jnp.where(hit, pltpu.roll(first, step, 1) if step else first, one)
        two = jnp.where(hit, pltpu.roll(second, step, 1) if step else second, two)
    load = blocks_of(one) + blocks_of(two) + blocks_of(third)
    over = (load > CAPACITY) | (blocks_of(third) > THIRD) | ((rank >= 80) & (tiles > 0))
    over = jnp.max(jnp.max(over.astype(jnp.int32), axis=1, keepdims=True), axis=0, keepdims=True)

    row = lax.broadcasted_iota(jnp.int32, (8, LANES), 0)
    wide_lane = lax.broadcasted_iota(jnp.int32, (WAYS, LANES), 1)
    wide_row = lax.broadcasted_iota(jnp.int32, (WAYS, LANES), 0)

    def column(array):
        mine = jnp.sum(jnp.where(row == lax.axis_index("bal"), array, 0), axis=0, keepdims=True)
        mine = jnp.broadcast_to(mine, (WAYS, LANES))
        return jnp.sum(jnp.where(wide_lane == wide_row, mine, 0), axis=1, keepdims=True)

    keys = [column(array) for array in (one, two, third)]
    size = [blocks_of(array) for array in keys]
    start = [jnp.zeros_like(size[0]), CAPACITY - size[2] - size[1], CAPACITY - size[2]]

    def table_of(place):
        at_key, at_block = jnp.broadcast_to(keys[0], place.shape), jnp.full_like(place, -1)
        for slot in range(HELD):
            here = (place >= start[slot]) & (place < start[slot] + size[slot])
            at_key = jnp.where(here, keys[slot], at_key)
            at_block = jnp.where(here, place - start[slot], at_block)
        return at_key, at_block

    at_key, at_block = table_of(wide_lane)
    out = jnp.maximum(at_block, 0) * GROUP + (at_key & (GROUP - 1))
    at_key, at_block = table_of(wide_lane - AT_COUNT)
    left = jnp.where(at_block >= 0, (at_key >> 7) - at_block * LANES, 0)
    out = jnp.where(wide_lane >= AT_COUNT, left, out)
    at_key, at_block = table_of(wide_lane - AT_SIDE)
    tile = at_key & (GROUP - 1)
    near = jnp.where(lax.axis_index("ens") % 2 == 0, tile >> 5, (tile >> 3) & 3)
    side_row = near * SIDE_ROWS + jnp.maximum(at_block, 0) * 8 + (tile & 3)
    out = jnp.where(wide_lane >= AT_SIDE, side_row, out)
    for slot in range(HELD):
        out = jnp.where(wide_lane == AT_TILE + slot, keys[slot] & (GROUP - 1), out)
        out = jnp.where(wide_lane == AT_BLOCKS + slot, size[slot], out)
    table[0:WAYS, :] = out
    found = jnp.zeros_like(wide_lane)
    for slot in range(HELD):
        hit = (keys[slot] & (GROUP - 1) == wide_lane) & (size[slot] > 0)
        found += jnp.where(hit, slot * WAYS + wide_row + 1, 0)
    table[WAYS : WAYS + 8, :] = jnp.where(row == 0, jnp.sum(found, axis=0, keepdims=True), 1 - over)


def displacements():
    every = [(dx, dy, dc) for dx in range(4) for dy in range(4) for dc in range(2)][1:]
    return sorted(every, key=lambda d: -(min(d[0], 4 - d[0]) + min(d[1], 4 - d[1])))


def shifted(me, step, sign=1):
    x, y, core = me // 8, (me // 2) % 4, me % 2
    dx, dy = (step[0], step[1]) if sign > 0 else ((4 - step[0]) % 4, (4 - step[1]) % 4)
    return (((x + dx) % 4) * 4 + (y + dy) % 4) * 2 + (core + step[2]) % 2


def centred(c, matrix, eye):
    half = ENS // 2
    top, low = matrix[:half, :half], matrix[half:, half:]
    mean = jnp.sum((top + low) * eye) * (1.0 / ENS)
    upper = jnp.concatenate([top - mean * eye, matrix[:half, half:]], axis=1)
    lower = jnp.concatenate([matrix[half:, :half], low - mean * eye], axis=1)
    deviation = jnp.concatenate([upper, lower], axis=0)
    return c + mean, deviation, deviation.astype(jnp.bfloat16)


def times(left, right, eye):
    cross = left[0] * right[1] + right[0] * left[1]
    inner = jnp.dot(left[2], right[2], preferred_element_type=jnp.float32)
    return centred(left[0] * right[0], cross + inner, eye)


def middle_of(product):
    return 1.5 - 0.5 * product[0], -0.5 * product[1], product[2] * jnp.bfloat16(-0.5)


def row_times(row, z):
    high = row.astype(jnp.bfloat16)
    low = (row - high.astype(jnp.float32)).astype(jnp.bfloat16)
    rest = (z[1] - z[2].astype(jnp.float32)).astype(jnp.bfloat16)
    out = jnp.dot(high, z[2], preferred_element_type=jnp.float32)
    out = out + jnp.dot(low, z[2], preferred_element_type=jnp.float32)
    out = out + jnp.dot(high, rest, preferred_element_type=jnp.float32)
    return z[0] * row + out


def coded(array, scale):
    return jnp.round(array * scale).astype(jnp.int32).astype(jnp.int16)


def decoded(array, scale):
    return array.astype(jnp.int32).astype(jnp.float32) * (1.0 / scale)


def analyse_kernel(
    counts_hbm, obs_hbm, mem_hbm, values_hbm, weights_hbm,
    out_recv, plan_hbm, fits,
    counts, values, weights, plan, table, obs_in, wide, mem_in, obs_send, mem_send, side_send, row_send, obs_recv, mem_recv,
    side_recv, row_recv, side, rows, out_send, root, root_t, pert,
    in_sem, phase_sem,
):
    me = lax.axis_index("ens")
    core = me % 2
    steps = displacements()
    targets = [shifted(me, step) for step in steps]

    def remote(src, dst, ssem, rsem, target):
        return pltpu.make_async_remote_copy(
            src_ref=src, dst_ref=dst, send_sem=ssem, recv_sem=rsem,
            device_id={"ens": target}, device_id_type=MESH,
        )

    barrier = pltpu.get_barrier_semaphore()
    for target in targets:
        pl.semaphore_signal(barrier, inc=1, device_id={"ens": target}, device_id_type=MESH)
    def drain(ref, sem):
        pltpu.make_async_copy(ref, ref, sem).wait()

    mem_load = pltpu.make_async_copy(mem_hbm, mem_in, in_sem.at[ROWS])
    obs_loads = [
        pltpu.make_async_copy(obs_hbm.at[m], obs_in.at[m], in_sem.at[m]) for m in range(ROWS)
    ]
    small_loads = [
        pltpu.make_async_copy(values_hbm, values, in_sem.at[ROWS + 2]),
        pltpu.make_async_copy(weights_hbm, weights, in_sem.at[ROWS + 3]),
        pltpu.make_async_copy(counts_hbm, counts, in_sem.at[ROWS + 4]),
    ]
    for copy in small_loads + obs_loads:
        copy.start()
    mem_load.start()
    for copy in small_loads:
        copy.wait()

    parts = []
    for part in range(SLOT_BLOCKS):
        lanes = slice(part * LANES, (part + 1) * LANES)
        parts += [values[:, lanes] * CODE, jnp.sqrt(weights[:, lanes]) * ROOT_CODE]
    side_send[...] = coded(jnp.concatenate(parts, axis=0), 1.0)
    write_plan(counts, plan)
    table_copy = pltpu.make_async_copy(plan, table, in_sem.at[ROWS + 1])
    table_copy.start()
    plan_copy = pltpu.make_async_copy(plan, plan_hbm, in_sem.at[ROWS + 5])
    plan_copy.start()
    for m in range(ROWS):
        obs_loads[m].wait()

        def widen(block, carry):
            first = pl.multiple_of((m * SLOT_BLOCKS + block) * GROUP, GROUP)
            lanes = pl.ds(pl.multiple_of(block * LANES, LANES), LANES)
            wide[pl.ds(first, GROUP), :] = obs_in[m, :, lanes].astype(jnp.float32)
            return carry

        lax.fori_loop(0, SLOT_BLOCKS, widen, 0)

    pl.semaphore_wait(barrier, WAYS - 1)

    x, y = me // 8, (me // 2) % 4
    near = x + core * (y - x)
    for step in range(1, 4):
        target = ((x + step * (1 - core)) % 4) * 8 + ((y + step * core) % 4) * 2 + core
        remote(
            side_send, side_recv.at[near], phase_sem.at[14], phase_sem.at[15], target
        ).start()
    pltpu.make_async_copy(side_send, side_recv.at[near], phase_sem.at[15]).start()

    table_copy.wait()
    plan_copy.wait()
    fits[0, 0] = table[WAYS + 1, 0]

    def pack_obs(dest, part):
        for pair in range(PART // 2):
            at = part * PART + 2 * pair
            rows = [
                wide[pl.ds(table[dest, at + j], ROWS, stride=SLOT_BLOCKS * GROUP), :]
                for j in range(2)
            ]
            obs_send[part, dest, pair] = jnp.concatenate(rows, axis=0).astype(jnp.bfloat16)

    def send_obs(part):
        for target in targets:
            pack_obs(target, part)
            remote(
                obs_send.at[part, target], obs_recv.at[part, me],
                phase_sem.at[part], phase_sem.at[16 + part], target,
            ).start()
        pack_obs(me, part)
        pltpu.make_async_copy(
            obs_send.at[part, me], obs_recv.at[part, me], phase_sem.at[16 + part]
        ).start()

    def pack_members(dest, slot):
        row = table[dest, AT_TILE + slot] * 4
        parts = [mem_in[pl.ds(row + f, ROWS, stride=4 * GROUP), :] for f in range(4)]
        mem_send[slot, dest] = coded(jnp.concatenate(parts, axis=0), CODE)

    send_obs(0)

    drain(side_recv, phase_sem.at[15])
    side[...] = side_recv[...].reshape(4 * SIDE_ROWS, LANES).astype(jnp.int32).astype(jnp.float32)
    own_slot = y + core * (4 + x - y)
    for step in range(4):
        for other in range(2):
            dest = ((x + step * core) % 4) * 8 + ((y + step * (1 - core)) % 4) * 2
            dest = dest + (core + other) % 2
            picked = [
                side[pl.ds(table[dest, AT_SIDE + block], 2, stride=4), :] for block in range(CAPACITY)
            ]
            at = step * 2 + other
            row_send[at] = coded(jnp.concatenate(picked, axis=0), 1.0)
            if at:
                remote(
                    row_send.at[at], row_recv.at[own_slot], phase_sem.at[18], phase_sem.at[19], dest
                ).start()
            else:
                pltpu.make_async_copy(
                    row_send.at[at], row_recv.at[own_slot], phase_sem.at[19]
                ).start()

    send_obs(1)

    mem_load.wait()
    for slot in range(HELD):

        def send_members(target, slot=slot):
            remote(
                mem_send.at[slot, target], mem_recv.at[slot, me],
                phase_sem.at[2 + slot], phase_sem.at[5 + slot], target,
            ).start()

        def keep_members(slot=slot):
            pltpu.make_async_copy(
                mem_send.at[slot, me], mem_recv.at[slot, me], phase_sem.at[5 + slot]
            ).start()

        for target in targets:
            pack_members(target, slot)
            if slot < 2:
                send_members(target)
            else:
                pl.when(target % 2 == 0)(functools.partial(send_members, target))
        pack_members(me, slot)
        if slot < 2:
            keep_members()
        else:
            pl.when(core == 0)(keep_members)

    drain(row_recv, phase_sem.at[19])
    rows[...] = row_recv[...].reshape(8 * 2 * CAPACITY, LANES).astype(jnp.int32).astype(jnp.float32)

    lane = lax.broadcasted_iota(jnp.int32, (1, LANES), 1)

    def form_roots(block):
        part, place = block // PART, block % PART
        half = (place % 2) * ROWS
        columns = pl.ds(block * LANES, LANES)
        seen = obs_recv[part, :, place // 2].astype(jnp.float32)[:, half : half + ROWS, :]
        seen = seen.reshape(ENS, LANES)
        mean = jnp.sum(seen, axis=0, keepdims=True) * (1.0 / ENS)
        owner = (table[me, block] & (GROUP - 1)) >> 2
        owner_core = owner & 1
        slot = (1 - owner_core) * ((owner >> 1) & 3) + owner_core * (4 + (owner >> 3))
        pair = rows[pl.ds(slot * 2 * CAPACITY + 2 * block, 2), :]
        live = lane < table[me, AT_COUNT + block]
        scale = jnp.where(live, pair[1:2] * (1.0 / ROOT_CODE), 0.0)
        innov = scale * (pair[0:1] * (1.0 / CODE) - mean)
        scaled = scale * (seen - mean)
        root[0:ENS, columns] = scaled.astype(jnp.bfloat16)
        root[ENS : ENS + 16, columns] = jnp.broadcast_to(innov, (16, LANES)).astype(jnp.bfloat16)
        root_t[block * LANES : (block + 1) * LANES, :] = scaled.T.astype(jnp.bfloat16)

    reach = [
        (0, SLOT_BLOCKS),
        ((CAPACITY - THIRD - CAPACITY // 2) // 2 * 2, CAPACITY),
        (CAPACITY - THIRD, CAPACITY),
    ]
    size = [table[me, AT_BLOCKS + slot] for slot in range(HELD)]
    start = [jnp.int32(0), CAPACITY - size[2] - size[1], CAPACITY - size[2]]
    half = ENS // 2
    eye = (
        lax.broadcasted_iota(jnp.int32, (half, half), 0)
        == lax.broadcasted_iota(jnp.int32, (half, half), 1)
    ).astype(jnp.float32)
    held = range(HELD)

    def sums_of(slot, part):
        low, high = max(reach[slot][0], part * PART), min(reach[slot][1], (part + 1) * PART)
        if low >= high:
            return None
        place = low + lax.broadcasted_iota(jnp.int32, (1, (high - low) * LANES), 1) // LANES
        mine = (place >= start[slot]) & (place < start[slot] + size[slot])
        masked = root[:, low * LANES : high * LANES] * mine.astype(jnp.float32).astype(jnp.bfloat16)
        return jnp.dot(
            masked, root_t[low * LANES : high * LANES, :], preferred_element_type=jnp.float32
        )

    drain(obs_recv.at[0], phase_sem.at[16])
    for block in range(PART):
        form_roots(block)
    early = [sums_of(slot, 0) for slot in held]
    drain(obs_recv.at[1], phase_sem.at[17])
    for block in range(PART, CAPACITY):
        form_roots(block)

    def centre_members(slot):
        if slot < 2:
            drain(mem_recv.at[slot], phase_sem.at[5 + slot])
        else:
            pl.when(core == 0)(lambda: drain(mem_recv.at[2], phase_sem.at[7]))
        raw = decoded(mem_recv[slot], CODE)
        fields = [raw[:, f * ROWS : (f + 1) * ROWS, :].reshape(ENS, LANES) for f in range(4)]
        state = jnp.concatenate(fields, axis=1)
        mean = jnp.sum(state, axis=0, keepdims=True) * (1.0 / ENS)
        pert[slot] = (state - mean).astype(jnp.bfloat16)
        return mean

    def weights_of(slots):
        vecs, bounds, ys, means = [], [], [], []
        for slot in slots:
            sums = sums_of(slot, 1)
            if early[slot] is not None:
                sums = sums + early[slot]
            gram = sums[0:ENS]
            vecs.append(sums[ENS : ENS + 8])
            trace = jnp.sum((gram[:half, :half] + gram[half:, half:]) * eye)
            bound = (ENS - 1.0) + trace
            bounds.append(bound)
            ys.append(centred((ENS - 1.0) / bound, gram * (1.0 / bound), eye))
        zs = middles = [middle_of(y) for y in ys]
        ys = [times(y, middle, eye) for y, middle in zip(ys, middles)]
        for iteration in range(1, NEWTON):
            if NEWTON - iteration <= len(slots):
                means.append(centre_members(slots[len(means)]))
            middles = [middle_of(times(z, y, eye)) for z, y in zip(zs, ys)]
            if iteration < NEWTON - 1:
                ys = [times(y, middle, eye) for y, middle in zip(ys, middles)]
            zs = [times(middle, z, eye) for middle, z in zip(middles, zs)]
        out = []
        for z, bound, vec in zip(zs, bounds, vecs):
            shift = row_times(row_times(vec, z), z)[0:1] * (1.0 / bound)
            factor = jnp.sqrt(jnp.float32(ENS - 1.0)) / jnp.sqrt(bound)
            diagonal = (factor * z[0]) * eye
            full = factor * z[1] + shift
            upper = jnp.concatenate([full[:half, :half] + diagonal, full[:half, half:]], axis=1)
            lower = jnp.concatenate([full[half:, :half], full[half:, half:] + diagonal], axis=1)
            out.append(jnp.concatenate([upper, lower], axis=0).astype(jnp.bfloat16))
        return out, means

    half_ways = WAYS // 2
    for slots in ((0, 1), (2,)):
        for slot, weight_t, mean in zip(slots, *weights_of(slots)):
            result = mean + jnp.dot(weight_t, pert[slot], preferred_element_type=jnp.float32)
            parts = [
                result[:, f * LANES : (f + 1) * LANES].reshape(WAYS, ROWS, LANES) for f in range(4)
            ]
            out_send[slot] = jnp.concatenate(parts, axis=1).astype(jnp.bfloat16)

            def send_result(slot=slot):
                for target in targets:
                    remote(
                        out_send.at[slot, target], out_recv.at[slot, me],
                        phase_sem.at[8 + slot], phase_sem.at[11 + slot], target,
                    ).start()
                pltpu.make_async_copy(
                    out_send.at[slot, me], out_recv.at[slot, me], phase_sem.at[11 + slot]
                ).start()

            if slot < 2:
                send_result()
            else:
                pl.when(core == 0)(send_result)

    sent = pl.ds(0, WAYS - 1)
    for part in range(2):
        drain(obs_send.at[part, sent], phase_sem.at[part])
    drain(side_recv.at[pl.ds(0, 3)], phase_sem.at[14])
    drain(row_send.at[pl.ds(0, 7)], phase_sem.at[18])
    for slot in range(2):
        drain(mem_send.at[slot, sent], phase_sem.at[2 + slot])
        drain(out_send.at[slot, sent], phase_sem.at[8 + slot])
        drain(out_recv.at[slot], phase_sem.at[11 + slot])
    drain(mem_send.at[2, pl.ds(0, half_ways - 1)], phase_sem.at[4])
    pl.when(core == 1)(lambda: drain(mem_send.at[2, 0], phase_sem.at[4]))
    pl.when(core == 0)(lambda: drain(out_send.at[2, sent], phase_sem.at[10]))
    drain(out_recv.at[2, pl.ds(0, half_ways)], phase_sem.at[13])


def exchange_and_analyse(counts, obs_ens, members, values, weights):
    anywhere = pl.BlockSpec(memory_space=pl.ANY)
    dma = pltpu.SemaphoreType.DMA
    return pl.pallas_call(
        analyse_kernel,
        out_shape=(
            jax.ShapeDtypeStruct((HELD, WAYS, 32, LANES), jnp.bfloat16),
            jax.ShapeDtypeStruct((WAYS + 8, LANES), jnp.int32),
            jax.ShapeDtypeStruct((1, 1), jnp.int32),
        ),
        in_specs=[anywhere] * 5,
        out_specs=(anywhere, anywhere, pl.BlockSpec(memory_space=pltpu.SMEM)),
        scratch_shapes=[
            pltpu.VMEM((8, GROUP), jnp.int32),
            pltpu.VMEM(values.shape, jnp.float32),
            pltpu.VMEM(weights.shape, jnp.float32),
            pltpu.VMEM((WAYS + 8, LANES), jnp.int32),
            pltpu.SMEM((WAYS + 8, LANES), jnp.int32),
            pltpu.VMEM((ROWS, GROUP, SLOT_BLOCKS * LANES), jnp.bfloat16),
            pltpu.VMEM((ROWS * SLOT_BLOCKS * GROUP, LANES), jnp.float32),
            pltpu.VMEM((ROWS * GROUP * 4, LANES), jnp.float32),
            pltpu.VMEM((2, WAYS, PART // 2, 16, LANES), jnp.bfloat16),
            pltpu.VMEM((HELD, WAYS, 32, LANES), jnp.int16),
            pltpu.VMEM((SIDE_ROWS, LANES), jnp.int16),
            pltpu.VMEM((8, 2 * CAPACITY, LANES), jnp.int16),
            pltpu.VMEM((2, WAYS, PART // 2, 16, LANES), jnp.bfloat16),
            pltpu.VMEM((HELD, WAYS, 32, LANES), jnp.int16),
            pltpu.VMEM((4, SIDE_ROWS, LANES), jnp.int16),
            pltpu.VMEM((8, 2 * CAPACITY, LANES), jnp.int16),
            pltpu.VMEM((4 * SIDE_ROWS, LANES), jnp.float32),
            pltpu.VMEM((16 * CAPACITY, LANES), jnp.float32),
            pltpu.VMEM((HELD, WAYS, 32, LANES), jnp.bfloat16),
            pltpu.VMEM((ENS + 16, CAPACITY * LANES), jnp.bfloat16),
            pltpu.VMEM((CAPACITY * LANES, ENS), jnp.bfloat16),
            pltpu.VMEM((HELD, ENS, 4 * LANES), jnp.bfloat16),
            dma((ROWS + 6,)),
            dma((20,)),
        ],
        compiler_params=pltpu.CompilerParams(
            collective_id=0, has_side_effects=True, vmem_limit_bytes=56 << 20
        ),
        name="analyse",
    )(counts, obs_ens, members, values, weights)


def scatter_kernel(plan, members, recv_hbm, out_hbm, table, recv, out, sems):
    width = 4 * GROUP // CHUNKS
    recv_load = pltpu.make_async_copy(recv_hbm, recv, sems.at[0])
    table_load = pltpu.make_async_copy(plan, table, sems.at[1 + 2 * CHUNKS])
    table_load.start()
    recv_load.start()
    members = members.reshape(ROWS, 4 * GROUP, LANES)
    out_hbm = out_hbm.reshape(ROWS, 4 * GROUP, LANES)

    def rows(chunk):
        return pl.ds(chunk * width, width)

    loads = [
        pltpu.make_async_copy(
            members.at[:, rows(c)], out.at[c, :, pl.ds(0, width)], sems.at[1 + c]
        )
        for c in range(CHUNKS)
    ]
    stores = [
        pltpu.make_async_copy(
            out.at[c, :, pl.ds(0, width)], out_hbm.at[:, rows(c)], sems.at[1 + CHUNKS + c]
        )
        for c in range(CHUNKS)
    ]
    for copy in loads:
        copy.start()
    table_load.wait()
    recv_load.wait()
    for c in range(CHUNKS):
        loads[c].wait()
        flat = out.at[c].reshape(ROWS * (width + 8), LANES)

        def place(index, carry):
            at = table[WAYS, c * (GROUP // CHUNKS) + index]
            tall = recv[jnp.maximum(at - 1, 0)].astype(jnp.float32)
            row = jnp.where(at > 0, index * 4, width)
            for f in range(4):
                flat[pl.ds(row + f, ROWS, stride=width + 8), :] = tall[f * ROWS : (f + 1) * ROWS]
            return carry

        lax.fori_loop(0, GROUP // CHUNKS, place, 0, unroll=8)
        stores[c].start()
    for copy in stores:
        copy.wait()


def scatter(plan, members, recv):
    anywhere = pl.BlockSpec(memory_space=pl.ANY)
    return pl.pallas_call(
        scatter_kernel,
        out_shape=jax.ShapeDtypeStruct(members.shape, jnp.float32),
        in_specs=[anywhere] * 3,
        out_specs=anywhere,
        scratch_shapes=[
            pltpu.SMEM((WAYS + 8, LANES), jnp.int32),
            pltpu.VMEM(recv.shape, recv.dtype),
            pltpu.VMEM((CHUNKS, ROWS, 4 * GROUP // CHUNKS + 8, LANES), jnp.float32),
            pltpu.SemaphoreType.DMA((2 + 2 * CHUNKS,)),
        ],
        compiler_params=pltpu.CompilerParams(vmem_limit_bytes=60 << 20),
        name="scatter",
    )(plan, members, recv)


def body(members, obs_ens, obs_count, obs_value, obs_weight):
    flat = members.reshape(-1, LANES)
    recv, plan, fits = exchange_and_analyse(
        obs_count.reshape(-1, GROUP), obs_ens, flat, obs_value, obs_weight
    )
    recv = recv.reshape(HELD * WAYS, 32, LANES)
    result = scatter(plan, flat, recv).reshape(members.shape)
    return lax.cond(
        fits[0, 0] > 0,
        lambda result, *_: result,
        lambda _, *inputs: static_body(*inputs),
        result, members, obs_ens, obs_count, obs_value, obs_weight,
    )


def solution(mesh):
    in_specs = (
        P("ens", "bal", None, None),
        P("ens", "bal", None),
        P(),
        P(("bal", "ens"), None),
        P(("bal", "ens"), None),
    )
    out_specs = P("ens", "bal", None, None)
    return jax.shard_map(body, mesh=mesh, in_specs=in_specs, out_specs=out_specs, check_vma=False)
```

```python
import functools

import jax
import jax.numpy as jnp
from jax import lax
from jax.experimental import pallas as pl
from jax.experimental.pallas import tpu as pltpu
from jax.sharding import PartitionSpec as P

NEWTON = 5
MESH = pl.DeviceIdType.MESH
WAYS = 32
GROUP = 128
LANES = 128
SLOT_BLOCKS = 16
HELD = 3
CAPACITY = 24
PARTS = (0, 10, 20, 24)
THIRD = 6
CHUNKS = 4
ROWS = 8
ENS = 256
CODE = 32767.0 / 6.0
ROOT_CODE = 32767.0 / 0.708
SIDE_ROWS = 8 * SLOT_BLOCKS
AT_TILE, AT_BLOCKS, AT_COUNT, AT_SIDE = 32, 36, 64, 96


def solve_weights(gram_matrix, obs_vector):
    highest = lax.Precision.HIGHEST
    ens_size = gram_matrix.shape[0]
    identity = jnp.eye(ens_size, dtype=jnp.float32)
    scale_bound = ens_size - 1.0 + jnp.trace(gram_matrix)
    y_matrix = ((ens_size - 1.0) * identity + gram_matrix) / scale_bound
    z_matrix = identity
    for iteration in range(NEWTON):
        middle = 1.5 * identity - 0.5 * jnp.dot(z_matrix, y_matrix, precision=highest)
        y_matrix = jnp.dot(y_matrix, middle, precision=highest)
        z_matrix = jnp.dot(middle, z_matrix, precision=highest)
    inner_vec = jnp.dot(z_matrix, obs_vector, precision=highest)
    shift_vec = jnp.dot(z_matrix, inner_vec, precision=highest) / scale_bound
    factor = jnp.sqrt(ens_size - 1.0) / jnp.sqrt(scale_bound)
    return (factor * z_matrix + shift_vec[:, None]).astype(jnp.bfloat16)


def unit_weights(gram_matrix, obs_vector):
    return jnp.eye(gram_matrix.shape[0], dtype=jnp.bfloat16)


def tile_weights(operands):
    gram_matrix, obs_vector = operands
    return lax.cond(
        jnp.trace(gram_matrix) > 0.0, solve_weights, unit_weights, gram_matrix, obs_vector
    )


def tile_gram(obs_rows, centre_row, weight_row, innov_row, live_count, ens_size):
    zero_sums = (jnp.zeros((ens_size, ens_size), jnp.float32), jnp.zeros((ens_size,), jnp.float32))
    block_count = (live_count + 127) // 128

    def add_block(index_block, totals):
        first_slot = index_block * 128
        obs_piece = lax.dynamic_slice_in_dim(obs_rows, first_slot, 128, 1)
        centre_piece = lax.dynamic_slice_in_dim(centre_row, first_slot, 128, 0)
        weight_piece = lax.dynamic_slice_in_dim(weight_row, first_slot, 128, 0)
        rhs_piece = lax.dynamic_slice_in_dim(innov_row, first_slot, 128, 0)
        root_piece = (
            weight_piece[None, :] * (obs_piece.astype(jnp.float32) - centre_piece[None, :])
        ).astype(jnp.bfloat16)
        gram_piece = lax.dot_general(
            root_piece, root_piece, (((1,), (1,)), ((), ())), preferred_element_type=jnp.float32
        )
        vector_piece = jnp.dot(root_piece, rhs_piece, preferred_element_type=jnp.float32)
        return (totals[0] + gram_piece, totals[1] + vector_piece)

    return lax.fori_loop(0, block_count, add_block, zero_sums)


def static_body(members, obs_ens, obs_count, obs_value, obs_weight):
    member_block, tile_block, nfield, columns = members.shape
    ens_ways = lax.axis_size("ens")
    ens_size = member_block * ens_ways
    per_device, slot_count = obs_value.shape
    state_width = nfield * columns
    first_tile = (lax.axis_index("bal") * ens_ways + lax.axis_index("ens")) * per_device
    ensemble = lax.all_to_all(members, "ens", split_axis=1, concat_axis=0, tiled=True)
    observed = lax.all_to_all(obs_ens, "ens", split_axis=1, concat_axis=0, tiled=True)
    mean_tiles = jnp.mean(ensemble, axis=0)
    pert_tiles = (ensemble - mean_tiles[None]).astype(jnp.bfloat16)
    pert_tiles = pert_tiles.reshape(ens_size, per_device, state_width)
    mean_tiles = mean_tiles.reshape(per_device, state_width)
    obs_mean = jnp.sum(observed, axis=0, dtype=jnp.float32) / ens_size
    counts = lax.dynamic_slice_in_dim(obs_count, first_tile, per_device, 0)
    positions = lax.broadcasted_iota(jnp.int32, (per_device, slot_count), 1)
    live_mask = positions < counts[:, None]
    innovation = jnp.where(live_mask, obs_value - obs_mean, 0.0)
    root_weight = jnp.sqrt(obs_weight)
    masked_weight = jnp.where(live_mask, root_weight, 0.0)
    scaled_innov = (root_weight * innovation).astype(jnp.bfloat16)
    grams = []
    vectors = []
    for tile_index in range(per_device):
        gram_one, vector_one = tile_gram(
            observed[:, tile_index],
            obs_mean[tile_index],
            masked_weight[tile_index],
            scaled_innov[tile_index],
            counts[tile_index],
            ens_size,
        )
        grams.append(gram_one)
        vectors.append(vector_one)
    gram_tiles = jnp.stack(grams)
    vector_tiles = jnp.stack(vectors)
    weights = lax.map(tile_weights, (gram_tiles, vector_tiles))
    result = mean_tiles[None] + jnp.einsum(
        "tjk,jtf->ktf", weights, pert_tiles, preferred_element_type=jnp.float32
    )
    result = result.reshape(ens_size, per_device, nfield, columns)
    return lax.all_to_all(result, "ens", split_axis=0, concat_axis=1, tiled=True)


def write_plan(counts, table, fits):
    lane = lax.broadcasted_iota(jnp.int32, (8, LANES), 1)
    device = lane % WAYS
    tiles = counts[...]
    key = tiles * GROUP + lane
    rank = jnp.zeros_like(key)
    for step in range(1, GROUP):
        rank += (pltpu.roll(key, step, 1) > key).astype(jnp.int32)
    first, second, third = jnp.zeros_like(key), jnp.zeros_like(key), jnp.zeros_like(key)
    third_rank = jnp.where(device % 2 == 0, 79 - device // 2, -1)
    for step in range(GROUP):
        there = pltpu.roll(rank, step, 1) if step else rank
        value = pltpu.roll(key, step, 1) if step else key
        first = jnp.where(there == device, value, first)
        second = jnp.where(there == 2 * WAYS - 1 - device, value, second)
        third = jnp.where(there == third_rank, value, third)

    def blocks_of(array):
        return ((array >> 7) + LANES - 1) >> 7

    pair = (blocks_of(first) + blocks_of(second)) * WAYS + device
    pair_rank = jnp.zeros_like(pair)
    for step in range(1, WAYS):
        pair_rank += (pltpu.roll(pair, step, 1) > pair).astype(jnp.int32)
    wanted = device // 2 + jnp.where(device % 2 == 0, WAYS // 2, 0)
    one, two = jnp.zeros_like(key), jnp.zeros_like(key)
    for step in range(WAYS):
        hit = (pltpu.roll(pair_rank, step, 1) if step else pair_rank) == wanted
        one = jnp.where(hit, pltpu.roll(first, step, 1) if step else first, one)
        two = jnp.where(hit, pltpu.roll(second, step, 1) if step else second, two)
    load = blocks_of(one) + blocks_of(two) + blocks_of(third)
    over = (load > CAPACITY) | (blocks_of(third) > THIRD) | ((rank >= 80) & (tiles > 0))
    over = jnp.max(jnp.max(over.astype(jnp.int32), axis=1, keepdims=True), axis=0, keepdims=True)

    row = lax.broadcasted_iota(jnp.int32, (8, LANES), 0)
    wide_lane = lax.broadcasted_iota(jnp.int32, (WAYS, LANES), 1)
    wide_row = lax.broadcasted_iota(jnp.int32, (WAYS, LANES), 0)

    def column(array):
        mine = jnp.sum(jnp.where(row == lax.axis_index("bal"), array, 0), axis=0, keepdims=True)
        mine = jnp.broadcast_to(mine, (WAYS, LANES))
        return jnp.sum(jnp.where(wide_lane == wide_row, mine, 0), axis=1, keepdims=True)

    keys = [column(array) for array in (one, two, third)]
    size = [blocks_of(array) for array in keys]
    start = [jnp.zeros_like(size[0]), CAPACITY - size[2] - size[1], CAPACITY - size[2]]

    def table_of(place):
        at_key, at_block = jnp.broadcast_to(keys[0], place.shape), jnp.full_like(place, -1)
        for slot in range(HELD):
            here = (place >= start[slot]) & (place < start[slot] + size[slot])
            at_key = jnp.where(here, keys[slot], at_key)
            at_block = jnp.where(here, place - start[slot], at_block)
        return at_key, at_block

    at_key, at_block = table_of(wide_lane)
    out = jnp.maximum(at_block, 0) * GROUP + (at_key & (GROUP - 1))
    at_key, at_block = table_of(wide_lane - AT_COUNT)
    left = jnp.where(at_block >= 0, (at_key >> 7) - at_block * LANES, 0)
    out = jnp.where(wide_lane >= AT_COUNT, left, out)
    at_key, at_block = table_of(wide_lane - AT_SIDE)
    tile = at_key & (GROUP - 1)
    near = jnp.where(lax.axis_index("ens") % 2 == 0, tile >> 5, (tile >> 3) & 3)
    side_row = near * SIDE_ROWS + jnp.maximum(at_block, 0) * 8 + (tile & 3)
    out = jnp.where(wide_lane >= AT_SIDE, side_row, out)
    for slot in range(HELD):
        out = jnp.where(wide_lane == AT_TILE + slot, keys[slot] & (GROUP - 1), out)
        out = jnp.where(wide_lane == AT_BLOCKS + slot, size[slot], out)
    table[0:WAYS, :] = out
    found = jnp.zeros_like(wide_lane)
    for slot in range(HELD):
        hit = (keys[slot] & (GROUP - 1) == wide_lane) & (size[slot] > 0)
        found += jnp.where(hit, slot * WAYS + wide_row + 1, 0)
    table[WAYS : WAYS + 8, :] = jnp.broadcast_to(jnp.sum(found, axis=0, keepdims=True), (8, LANES))
    fits[...] = 1 - over


def displacements():
    every = [(dx, dy, dc) for dx in range(4) for dy in range(4) for dc in range(2)][1:]
    return sorted(every, key=lambda d: -(min(d[0], 4 - d[0]) + min(d[1], 4 - d[1])))


def shifted(me, step, sign=1):
    x, y, core = me // 8, (me // 2) % 4, me % 2
    dx, dy = (step[0], step[1]) if sign > 0 else ((4 - step[0]) % 4, (4 - step[1]) % 4)
    return (((x + dx) % 4) * 4 + (y + dy) % 4) * 2 + (core + step[2]) % 2


def centred(c, matrix, eye):
    half = ENS // 2
    top, low = matrix[:half, :half], matrix[half:, half:]
    mean = jnp.sum((top + low) * eye) * (1.0 / ENS)
    upper = jnp.concatenate([top - mean * eye, matrix[:half, half:]], axis=1)
    lower = jnp.concatenate([matrix[half:, :half], low - mean * eye], axis=1)
    deviation = jnp.concatenate([upper, lower], axis=0)
    return c + mean, deviation, deviation.astype(jnp.bfloat16)


def times(left, right, eye):
    cross = left[0] * right[1] + right[0] * left[1]
    inner = jnp.dot(left[2], right[2], preferred_element_type=jnp.float32)
    return centred(left[0] * right[0], cross + inner, eye)


def middle_of(product):
    return 1.5 - 0.5 * product[0], -0.5 * product[1], product[2] * jnp.bfloat16(-0.5)


def row_times(row, z):
    high = row.astype(jnp.bfloat16)
    low = (row - high.astype(jnp.float32)).astype(jnp.bfloat16)
    rest = (z[1] - z[2].astype(jnp.float32)).astype(jnp.bfloat16)
    out = jnp.dot(high, z[2], preferred_element_type=jnp.float32)
    out = out + jnp.dot(low, z[2], preferred_element_type=jnp.float32)
    out = out + jnp.dot(high, rest, preferred_element_type=jnp.float32)
    return z[0] * row + out


def coded(array, scale):
    return jnp.round(array * scale).astype(jnp.int32).astype(jnp.int16)


def decoded(array, scale):
    return array.astype(jnp.int32).astype(jnp.float32) * (1.0 / scale)


def analyse_kernel(
    counts_hbm, obs_hbm, mem_hbm, values_hbm, weights_hbm,
    out_recv, plan_hbm, fits_hbm,
    counts, values, weights, plan, fits, table, obs_in, wide, mem_in, obs_send_a, obs_send_b, obs_send_c, mem_send, side_send,
    row_send, obs_recv_a, obs_recv_b, obs_recv_c, mem_recv,
    side_recv, row_recv, side, rows, out_send, root, root_t, pert,
    in_sem, phase_sem, obs_sem,
):
    me = lax.axis_index("ens")
    core = me % 2
    obs_send = (obs_send_a, obs_send_b, obs_send_c)
    obs_recv = (obs_recv_a, obs_recv_b, obs_recv_c)
    steps = displacements()
    targets = [shifted(me, step) for step in steps]

    def remote(src, dst, ssem, rsem, target):
        return pltpu.make_async_remote_copy(
            src_ref=src, dst_ref=dst, send_sem=ssem, recv_sem=rsem,
            device_id={"ens": target}, device_id_type=MESH,
        )

    barrier = pltpu.get_barrier_semaphore()
    for target in targets:
        pl.semaphore_signal(barrier, inc=1, device_id={"ens": target}, device_id_type=MESH)
    def drain(ref, sem):
        pltpu.make_async_copy(ref, ref, sem).wait()

    mem_load = pltpu.make_async_copy(mem_hbm, mem_in, in_sem.at[ROWS])
    obs_loads = [
        pltpu.make_async_copy(obs_hbm.at[m], obs_in.at[m], in_sem.at[m]) for m in range(ROWS)
    ]
    small_loads = [
        pltpu.make_async_copy(values_hbm, values, in_sem.at[ROWS + 2]),
        pltpu.make_async_copy(weights_hbm, weights, in_sem.at[ROWS + 3]),
        pltpu.make_async_copy(counts_hbm, counts, in_sem.at[ROWS + 4]),
    ]
    for copy in small_loads + obs_loads:
        copy.start()
    mem_load.start()
    for copy in small_loads:
        copy.wait()

    parts = []
    for part in range(SLOT_BLOCKS):
        lanes = slice(part * LANES, (part + 1) * LANES)
        parts += [values[:, lanes] * CODE, jnp.sqrt(weights[:, lanes]) * ROOT_CODE]
    side_send[...] = coded(jnp.concatenate(parts, axis=0), 1.0)
    write_plan(counts, plan, fits)
    table_copy = pltpu.make_async_copy(plan, table, in_sem.at[ROWS + 1])
    table_copy.start()
    plan_copy = pltpu.make_async_copy(plan, plan_hbm, in_sem.at[ROWS + 5])
    plan_copy.start()
    fits_copy = pltpu.make_async_copy(fits, fits_hbm, in_sem.at[ROWS + 6])
    fits_copy.start()
    for m in range(ROWS):
        obs_loads[m].wait()

        def widen(block, carry):
            first = pl.multiple_of((m * SLOT_BLOCKS + block) * GROUP, GROUP)
            lanes = pl.ds(pl.multiple_of(block * LANES, LANES), LANES)
            wide[pl.ds(first, GROUP), :] = obs_in[m, :, lanes].astype(jnp.float32)
            return carry

        lax.fori_loop(0, SLOT_BLOCKS, widen, 0)

    pl.semaphore_wait(barrier, WAYS - 1)

    x, y = me // 8, (me // 2) % 4
    near = x + core * (y - x)
    for step in range(1, 4):
        target = ((x + step * (1 - core)) % 4) * 8 + ((y + step * core) % 4) * 2 + core
        remote(
            side_send, side_recv.at[near], phase_sem.at[14], phase_sem.at[15], target
        ).start()
    pltpu.make_async_copy(side_send, side_recv.at[near], phase_sem.at[15]).start()

    table_copy.wait()
    plan_copy.wait()
    fits_copy.wait()

    def pack_obs(dest, part):
        for pair in range((PARTS[part + 1] - PARTS[part]) // 2):
            at = PARTS[part] + 2 * pair
            rows = [
                wide[pl.ds(table[dest, at + j], ROWS, stride=SLOT_BLOCKS * GROUP), :]
                for j in range(2)
            ]
            obs_send[part][dest, pair] = jnp.concatenate(rows, axis=0).astype(jnp.bfloat16)

    def send_obs(part):
        for target in targets:
            pack_obs(target, part)
            remote(
                obs_send[part].at[target], obs_recv[part].at[me],
                obs_sem.at[part], obs_sem.at[3 + part], target,
            ).start()
        pack_obs(me, part)
        pltpu.make_async_copy(
            obs_send[part].at[me], obs_recv[part].at[me], obs_sem.at[3 + part]
        ).start()

    def pack_members(dest, slot):
        row = table[dest, AT_TILE + slot] * 4
        parts = [mem_in[pl.ds(row + f, ROWS, stride=4 * GROUP), :] for f in range(4)]
        mem_send[slot, dest] = coded(jnp.concatenate(parts, axis=0), CODE)

    send_obs(0)

    drain(side_recv, phase_sem.at[15])
    side[...] = side_recv[...].reshape(4 * SIDE_ROWS, LANES).astype(jnp.int32).astype(jnp.float32)
    own_slot = y + core * (4 + x - y)
    for step in range(4):
        for other in range(2):
            dest = ((x + step * core) % 4) * 8 + ((y + step * (1 - core)) % 4) * 2
            dest = dest + (core + other) % 2
            picked = [
                side[pl.ds(table[dest, AT_SIDE + block], 2, stride=4), :] for block in range(CAPACITY)
            ]
            at = step * 2 + other
            row_send[at] = coded(jnp.concatenate(picked, axis=0), 1.0)
            if at:
                remote(
                    row_send.at[at], row_recv.at[own_slot], phase_sem.at[18], phase_sem.at[19], dest
                ).start()
            else:
                pltpu.make_async_copy(
                    row_send.at[at], row_recv.at[own_slot], phase_sem.at[19]
                ).start()

    send_obs(1)
    send_obs(2)

    mem_load.wait()
    for slot in range(HELD):

        def send_members(target, slot=slot):
            remote(
                mem_send.at[slot, target], mem_recv.at[slot, me],
                phase_sem.at[2 + slot], phase_sem.at[5 + slot], target,
            ).start()

        def keep_members(slot=slot):
            pltpu.make_async_copy(
                mem_send.at[slot, me], mem_recv.at[slot, me], phase_sem.at[5 + slot]
            ).start()

        for target in targets:
            pack_members(target, slot)
            if slot < 2:
                send_members(target)
            else:
                pl.when(target % 2 == 0)(functools.partial(send_members, target))
        pack_members(me, slot)
        if slot < 2:
            keep_members()
        else:
            pl.when(core == 0)(keep_members)

    drain(row_recv, phase_sem.at[19])
    rows[...] = row_recv[...].reshape(8 * 2 * CAPACITY, LANES).astype(jnp.int32).astype(jnp.float32)

    lane = lax.broadcasted_iota(jnp.int32, (1, LANES), 1)

    def form_roots(block):
        part = sum(block >= begin for begin in PARTS[1:-1])
        place = block - PARTS[part]
        half = (place % 2) * ROWS
        columns = pl.ds(block * LANES, LANES)
        seen = obs_recv[part][:, place // 2].astype(jnp.float32)[:, half : half + ROWS, :]
        seen = seen.reshape(ENS, LANES)
        mean = jnp.sum(seen, axis=0, keepdims=True) * (1.0 / ENS)
        owner = (table[me, block] & (GROUP - 1)) >> 2
        owner_core = owner & 1
        slot = (1 - owner_core) * ((owner >> 1) & 3) + owner_core * (4 + (owner >> 3))
        pair = rows[pl.ds(slot * 2 * CAPACITY + 2 * block, 2), :]
        live = lane < table[me, AT_COUNT + block]
        scale = jnp.where(live, pair[1:2] * (1.0 / ROOT_CODE), 0.0)
        innov = scale * (pair[0:1] * (1.0 / CODE) - mean)
        scaled = scale * (seen - mean)
        root[0:ENS, columns] = scaled.astype(jnp.bfloat16)
        root[ENS : ENS + 16, columns] = jnp.broadcast_to(innov, (16, LANES)).astype(jnp.bfloat16)
        root_t[block * LANES : (block + 1) * LANES, :] = scaled.T.astype(jnp.bfloat16)

    reach = [
        (0, SLOT_BLOCKS),
        ((CAPACITY - THIRD - CAPACITY // 2) // 2 * 2, CAPACITY),
        (CAPACITY - THIRD, CAPACITY),
    ]
    size = [table[me, AT_BLOCKS + slot] for slot in range(HELD)]
    start = [jnp.int32(0), CAPACITY - size[2] - size[1], CAPACITY - size[2]]
    half = ENS // 2
    eye = (
        lax.broadcasted_iota(jnp.int32, (half, half), 0)
        == lax.broadcasted_iota(jnp.int32, (half, half), 1)
    ).astype(jnp.float32)
    held = range(HELD)

    def sums_of(slot, part):
        low, high = max(reach[slot][0], PARTS[part]), min(reach[slot][1], PARTS[part + 1])
        if low >= high:
            return None
        place = low + lax.broadcasted_iota(jnp.int32, (1, (high - low) * LANES), 1) // LANES
        mine = (place >= start[slot]) & (place < start[slot] + size[slot])
        masked = root[:, low * LANES : high * LANES] * mine.astype(jnp.float32).astype(jnp.bfloat16)
        return jnp.dot(
            masked, root_t[low * LANES : high * LANES, :], preferred_element_type=jnp.float32
        )

    sums = [None] * HELD
    for part in range(len(PARTS) - 1):
        drain(obs_recv[part], obs_sem.at[3 + part])
        for block in range(PARTS[part], PARTS[part + 1]):
            form_roots(block)
        for slot in held:
            more = sums_of(slot, part)
            sums[slot] = more if sums[slot] is None else sums[slot] if more is None else sums[slot] + more

    def centre_members(slot):
        if slot < 2:
            drain(mem_recv.at[slot], phase_sem.at[5 + slot])
        else:
            pl.when(core == 0)(lambda: drain(mem_recv.at[2], phase_sem.at[7]))
        raw = decoded(mem_recv[slot], CODE)
        fields = [raw[:, f * ROWS : (f + 1) * ROWS, :].reshape(ENS, LANES) for f in range(4)]
        state = jnp.concatenate(fields, axis=1)
        mean = jnp.sum(state, axis=0, keepdims=True) * (1.0 / ENS)
        pert[slot] = (state - mean).astype(jnp.bfloat16)
        return mean

    def weights_of(slots):
        vecs, bounds, ys, means = [], [], [], []
        for slot in slots:
            gram = sums[slot][0:ENS]
            vecs.append(sums[slot][ENS : ENS + 8])
            trace = jnp.sum((gram[:half, :half] + gram[half:, half:]) * eye)
            bound = (ENS - 1.0) + trace
            bounds.append(bound)
            ys.append(centred((ENS - 1.0) / bound, gram * (1.0 / bound), eye))
        zs = middles = [middle_of(y) for y in ys]
        ys = [times(y, middle, eye) for y, middle in zip(ys, middles)]
        for iteration in range(1, NEWTON):
            if NEWTON - iteration <= len(slots):
                means.append(centre_members(slots[len(means)]))
            middles = [middle_of(times(z, y, eye)) for z, y in zip(zs, ys)]
            if iteration < NEWTON - 1:
                ys = [times(y, middle, eye) for y, middle in zip(ys, middles)]
            zs = [times(middle, z, eye) for middle, z in zip(middles, zs)]
        out = []
        for z, bound, vec in zip(zs, bounds, vecs):
            shift = row_times(row_times(vec, z), z)[0:1] * (1.0 / bound)
            factor = jnp.sqrt(jnp.float32(ENS - 1.0)) / jnp.sqrt(bound)
            diagonal = (factor * z[0]) * eye
            full = factor * z[1] + shift
            upper = jnp.concatenate([full[:half, :half] + diagonal, full[:half, half:]], axis=1)
            lower = jnp.concatenate([full[half:, :half], full[half:, half:] + diagonal], axis=1)
            out.append(jnp.concatenate([upper, lower], axis=0).astype(jnp.bfloat16))
        return out, means

    half_ways = WAYS // 2
    for slots in ((0, 1), (2,)):
        for slot, weight_t, mean in zip(slots, *weights_of(slots)):
            result = mean + jnp.dot(weight_t, pert[slot], preferred_element_type=jnp.float32)
            parts = [
                result[:, f * LANES : (f + 1) * LANES].reshape(WAYS, ROWS, LANES) for f in range(4)
            ]
            out_send[slot] = jnp.concatenate(parts, axis=1).astype(jnp.bfloat16)

            def send_result(slot=slot):
                for target in targets:
                    remote(
                        out_send.at[slot, target], out_recv.at[slot, me],
                        phase_sem.at[8 + slot], phase_sem.at[11 + slot], target,
                    ).start()
                pltpu.make_async_copy(
                    out_send.at[slot, me], out_recv.at[slot, me], phase_sem.at[11 + slot]
                ).start()

            if slot < 2:
                send_result()
            else:
                pl.when(core == 0)(send_result)

    sent = pl.ds(0, WAYS - 1)
    for part in range(len(PARTS) - 1):
        drain(obs_send[part].at[sent], obs_sem.at[part])
    drain(side_recv.at[pl.ds(0, 3)], phase_sem.at[14])
    drain(row_send.at[pl.ds(0, 7)], phase_sem.at[18])
    for slot in range(2):
        drain(mem_send.at[slot, sent], phase_sem.at[2 + slot])
        drain(out_send.at[slot, sent], phase_sem.at[8 + slot])
        drain(out_recv.at[slot], phase_sem.at[11 + slot])
    drain(mem_send.at[2, pl.ds(0, half_ways - 1)], phase_sem.at[4])
    pl.when(core == 1)(lambda: drain(mem_send.at[2, 0], phase_sem.at[4]))
    pl.when(core == 0)(lambda: drain(out_send.at[2, sent], phase_sem.at[10]))
    drain(out_recv.at[2, pl.ds(0, half_ways)], phase_sem.at[13])


def exchange_and_analyse(counts, obs_ens, members, values, weights):
    anywhere = pl.BlockSpec(memory_space=pl.ANY)
    dma = pltpu.SemaphoreType.DMA
    obs_parts = [
        pltpu.VMEM((WAYS, (end - begin) // 2, 16, LANES), jnp.bfloat16)
        for begin, end in zip(PARTS, PARTS[1:])
    ]
    return pl.pallas_call(
        analyse_kernel,
        out_shape=(
            jax.ShapeDtypeStruct((HELD, WAYS, 32, LANES), jnp.bfloat16),
            jax.ShapeDtypeStruct((WAYS + 8, LANES), jnp.int32),
            jax.ShapeDtypeStruct((1, 1), jnp.int32),
        ),
        in_specs=[anywhere] * 5,
        out_specs=(anywhere, anywhere, anywhere),
        scratch_shapes=[
            pltpu.VMEM((8, GROUP), jnp.int32),
            pltpu.VMEM(values.shape, jnp.float32),
            pltpu.VMEM(weights.shape, jnp.float32),
            pltpu.VMEM((WAYS + 8, LANES), jnp.int32),
            pltpu.VMEM((1, 1), jnp.int32),
            pltpu.SMEM((WAYS + 8, LANES), jnp.int32),
            pltpu.VMEM((ROWS, GROUP, SLOT_BLOCKS * LANES), jnp.bfloat16),
            pltpu.VMEM((ROWS * SLOT_BLOCKS * GROUP, LANES), jnp.float32),
            pltpu.VMEM((ROWS * GROUP * 4, LANES), jnp.float32),
            *obs_parts,
            pltpu.VMEM((HELD, WAYS, 32, LANES), jnp.int16),
            pltpu.VMEM((SIDE_ROWS, LANES), jnp.int16),
            pltpu.VMEM((8, 2 * CAPACITY, LANES), jnp.int16),
            *obs_parts,
            pltpu.VMEM((HELD, WAYS, 32, LANES), jnp.int16),
            pltpu.VMEM((4, SIDE_ROWS, LANES), jnp.int16),
            pltpu.VMEM((8, 2 * CAPACITY, LANES), jnp.int16),
            pltpu.VMEM((4 * SIDE_ROWS, LANES), jnp.float32),
            pltpu.VMEM((16 * CAPACITY, LANES), jnp.float32),
            pltpu.VMEM((HELD, WAYS, 32, LANES), jnp.bfloat16),
            pltpu.VMEM((ENS + 16, CAPACITY * LANES), jnp.bfloat16),
            pltpu.VMEM((CAPACITY * LANES, ENS), jnp.bfloat16),
            pltpu.VMEM((HELD, ENS, 4 * LANES), jnp.bfloat16),
            dma((ROWS + 7,)),
            dma((20,)),
            dma((6,)),
        ],
        compiler_params=pltpu.CompilerParams(
            collective_id=0, has_side_effects=True, vmem_limit_bytes=56 << 20
        ),
        name="analyse",
    )(counts, obs_ens, members, values, weights)


def scatter_kernel(plan, members, recv_hbm, out_hbm, table, recv, out, sems):
    width = 4 * GROUP // CHUNKS
    recv_load = pltpu.make_async_copy(recv_hbm, recv, sems.at[0])
    table_load = pltpu.make_async_copy(plan, table, sems.at[1 + 2 * CHUNKS])
    table_load.start()
    recv_load.start()
    members = members.reshape(ROWS, 4 * GROUP, LANES)
    out_hbm = out_hbm.reshape(ROWS, 4 * GROUP, LANES)

    def rows(chunk):
        return pl.ds(chunk * width, width)

    loads = [
        pltpu.make_async_copy(
            members.at[:, rows(c)], out.at[c, :, pl.ds(0, width)], sems.at[1 + c]
        )
        for c in range(CHUNKS)
    ]
    stores = [
        pltpu.make_async_copy(
            out.at[c, :, pl.ds(0, width)], out_hbm.at[:, rows(c)], sems.at[1 + CHUNKS + c]
        )
        for c in range(CHUNKS)
    ]
    for copy in loads:
        copy.start()
    table_load.wait()
    recv_load.wait()
    for c in range(CHUNKS):
        loads[c].wait()
        flat = out.at[c].reshape(ROWS * (width + 8), LANES)

        def place(index, carry):
            at = table[WAYS, c * (GROUP // CHUNKS) + index]
            tall = recv[jnp.maximum(at - 1, 0)].astype(jnp.float32)
            row = jnp.where(at > 0, index * 4, width)
            for f in range(4):
                flat[pl.ds(row + f, ROWS, stride=width + 8), :] = tall[f * ROWS : (f + 1) * ROWS]
            return carry

        lax.fori_loop(0, GROUP // CHUNKS, place, 0, unroll=8)
        stores[c].start()
    for copy in stores:
        copy.wait()


def scatter(plan, members, recv):
    anywhere = pl.BlockSpec(memory_space=pl.ANY)
    return pl.pallas_call(
        scatter_kernel,
        out_shape=jax.ShapeDtypeStruct(members.shape, jnp.float32),
        in_specs=[anywhere] * 3,
        out_specs=anywhere,
        scratch_shapes=[
            pltpu.SMEM((WAYS + 8, LANES), jnp.int32),
            pltpu.VMEM(recv.shape, recv.dtype),
            pltpu.VMEM((CHUNKS, ROWS, 4 * GROUP // CHUNKS + 8, LANES), jnp.float32),
            pltpu.SemaphoreType.DMA((2 + 2 * CHUNKS,)),
        ],
        compiler_params=pltpu.CompilerParams(vmem_limit_bytes=60 << 20),
        name="scatter",
    )(plan, members, recv)


def body(members, obs_ens, obs_count, obs_value, obs_weight):
    flat = members.reshape(-1, LANES)
    recv, plan, fits = exchange_and_analyse(
        obs_count.reshape(-1, GROUP), obs_ens, flat, obs_value, obs_weight
    )
    recv = recv.reshape(HELD * WAYS, 32, LANES)
    result = scatter(plan, flat, recv).reshape(members.shape)
    return lax.cond(
        fits[0, 0] > 0,
        lambda result, *_: result,
        lambda _, *inputs: static_body(*inputs),
        result, members, obs_ens, obs_count, obs_value, obs_weight,
    )


def solution(mesh):
    in_specs = (
        P("ens", "bal", None, None),
        P("ens", "bal", None),
        P(),
        P(("bal", "ens"), None),
        P(("bal", "ens"), None),
    )
    out_specs = P("ens", "bal", None, None)
    return jax.shard_map(body, mesh=mesh, in_specs=in_specs, out_specs=out_specs, check_vma=False)
```
